32 devices in a mesh: dp: 8 (over z, x), row: 2 (over y), col: 2 (over core).
Axes of the slice: x: 2, y: 2, z: 4, core: 2. Of those that a mesh axis runs over, the one named last changes fastest.
Arguments:
- layer_input: bfloat16 [16384, 768], P(('dp', 'col'), 'row'), may hold values from -6 to 6
- teacher: bfloat16 [16384, 768], P(('dp', 'col'), 'row'), may hold values from -6 to 6
- valid_mask: int32 [16384], P(('dp', 'col')), may hold values from 0 to 1, as said below
- routes: int32 [16384, 2], P('dp'), may hold values from 0 to 3, all different within a row; in each aligned block of 1024 rows (0 to 1023, 1024 to 2047, ...) at most 640 rows name the same one
- segments: int32 [16, 1024], P('dp'), may hold values from 0 to 3, never falling along the last dimension, each value on 1 to 512 neighbouring positions
- gain_attn: float32 [768], P('row'), may hold values from 0.5 to 1.5
- gain_ffn: float32 [768], P('row'), may hold values from 0.5 to 1.5
- w_qkv: bfloat16 [768, 3, 768], P('row', None, 'col'), may hold values from -0.21875 to 0.21875
- w_out: bfloat16 [768, 768], P('col', 'row'), may hold values from -0.625 to 0.625
- w_router: bfloat16 [768, 4], P('row'), may hold values from -0.15625 to 0.15625
- w_shared_up: bfloat16 [768, 2, 2048], P('row', None, 'col'), may hold values from -0.21875 to 0.21875
- w_shared_down: bfloat16 [2048, 768], P('col', 'row'), may hold values from -0.125 to 0.125
- w_expert_up: bfloat16 [4, 768, 2, 2048], P(None, 'row', None, 'col'), may hold values from -0.21875 to 0.21875
- w_expert_down: bfloat16 [4, 2048, 768], P(None, 'col', 'row'), may hold values from -0.125 to 0.125
Outputs:
- output: float32 [16384, 768], P(('dp', 'col'), 'row')
- loss: float32 [], replicated
- input_grad: float32 [16384, 768], P(('dp', 'col'), 'row')
- gain_attn_grad: float32 [768], P('row')
- gain_ffn_grad: float32 [768], P('row')
- w_qkv_grad: float32 [768, 3, 768], P('row', None, 'col')
- w_out_grad: float32 [768, 768], P('col', 'row')
- w_router_grad: float32 [768, 4], P('row')
- w_shared_up_grad: float32 [768, 2, 2048], P('row', None, 'col')
- w_shared_down_grad: float32 [2048, 768], P('col', 'row')
- w_expert_up_grad: float32 [4, 768, 2, 2048], P(None, 'row', None, 'col')
- w_expert_down_grad: float32 [4, 2048, 768], P(None, 'col', 'row')
The draws below stay inside these ranges and needn't reach their ends.
Inputs may be any that keep to these rules, and one draw needn't show every extreme that they name: The first token of every sequence has valid_mask 1. `routes`: each token names two different experts; among the 1024 tokens of one residual-stream device (aligned blocks of rows) no expert is named more than 640 times, a bound that some block reaches. `segments`: document numbers never fall along a sequence; every document has 1 to 512 tokens and one has exactly 512.
All inputs are finite; a program needn't handle non-finite values.
Results may differ from the reference program's by a relative error of at most 0.02.
Values may be sent and summed in bfloat16 or wider, within the bound.
A program may use at most 320 MiB of HBM per device.

```python
import math
import jax
import jax.numpy as jnp
import numpy as np
from jax import lax

D = 768
HEADS = 12
HEAD_DIM = 64
FF = 2048
HE = 2048
E = 4
LEN = 1024
ABLOCK = 256
SEQ_DEV = 1
CAP = 640
SEQS = 16
TOKENS = 16384


def draw_valid_mask(key, part):
    key = jax.random.fold_in(key, 11)
    positions = jnp.arange(TOKENS, dtype=jnp.int32)
    ticket = jax.random.randint(key, (TOKENS,), 0, 4 * TOKENS, dtype=jnp.int32)
    counted = (ticket < TOKENS + 2 * positions) | (positions % LEN == 0)
    return counted.astype(jnp.int32)


def block_scale(rng, shape, cuts, smallest, top_value):
    gain = 1.0
    for axis_at, parts in cuts:
        steps = jax.random.uniform(jax.random.fold_in(jax.random.fold_in(rng, 6), axis_at), (parts,), jnp.float32, smallest / len(cuts), top_value / len(cuts))
        gain = gain * jnp.repeat(jnp.exp(steps), shape[axis_at] // parts).reshape((-1,) + (1,) * (len(shape) - 1 - axis_at))
    return gain


def length_profile(amount, total, reach, slope):
    weights = [(1 << 20) // math.isqrt(grade ** slope) + 1 for grade in range(2, amount + 1)]
    surplus, given = total - reach - (amount - 1), [1] * (amount - 1)
    while surplus > 0:
        candidates = [i for i in range(amount - 1) if given[i] < reach]
        mass, remaining = sum([weights[i] for i in candidates]), surplus
        for i in candidates:
            more = min(reach - given[i], max(1, remaining * weights[i] // mass), surplus)
            given[i] = given[i] + more
            surplus = surplus - more
    return np.array([reach] + given)


def ragged_sizes(key, number_of, total, limit, skew):
    if number_of == 2:
        one = jax.random.randint(key, (), max(1, total - limit), min(limit, total - 1) + 1)
        return jnp.stack([one, total - one])
    lengths = jnp.asarray(length_profile(number_of, total, limit, skew), jnp.int32)
    couples = (number_of - 1) // 2
    donor, receiver = lengths[1:1 + 2 * couples:2], lengths[2:2 + 2 * couples:2]
    room = jnp.minimum(donor - 1, limit - receiver)
    moved = jax.random.randint(jax.random.fold_in(key, 1), (couples,), 0, 1 << 20) % (room + 1)
    lengths = lengths.at[1:1 + 2 * couples:2].set(donor - moved).at[2:2 + 2 * couples:2].set(receiver + moved)
    return lengths[jax.random.permutation(jax.random.fold_in(key, 2), number_of)]


def assign_block(key, own, number, rows, count, top, limit, lean):
    order = jax.random.permutation(key, count)
    heavy_load, common = portions_of(count, rows * top, limit, lean, True), portions_of(count, rows * top, limit, lean, False)
    places = jnp.arange(count)

    def named(sizes, rotation):
        used = int((sizes > 0).sum())
        fixed = max(1, used // 4)
        shifted = fixed + (places - fixed + rotation * (used - fixed)) % max(1, count - fixed)
        return jnp.zeros((count,), jnp.int32).at[order[jnp.where(places < fixed, places, shifted)]].set(jnp.asarray(sizes, jnp.int32))

    sizes = jnp.where(number % 4 == 0, named(heavy_load, number // 4), named(common, number - number // 4 - 1))
    mixed = jax.random.permutation(jax.random.fold_in(own, 3), count)
    source_of, taker = mixed[0:count // 2 * 2:2], mixed[1:count // 2 * 2:2]
    room = jnp.minimum(sizes[source_of] - 1, limit - sizes[taker]) // 2
    room = jnp.where((source_of == order[0]) | (taker == order[0]) | (sizes[taker] == 0), 0, jnp.maximum(room, 0))
    shifted = jax.random.randint(jax.random.fold_in(own, 4), (count // 2,), 0, 1 << 20) % (room + 1)
    sizes = sizes.at[source_of].add(-shifted).at[taker].add(shifted)
    members = jnp.searchsorted(jnp.cumsum(sizes), jnp.arange(rows * top), side="right").astype(jnp.int32)
    table = members.reshape(top, rows).T
    table = table[jax.random.permutation(jax.random.fold_in(own, 1), rows)]
    rotation = jax.random.randint(jax.random.fold_in(own, 2), (rows, 1), 0, top)
    return jnp.take_along_axis(table, (jnp.arange(top)[None, :] + rotation) % top, axis=1)


def portions_of(number_of, total, most, skew, full):
    loads = [(1 << 20) // math.isqrt(standing ** skew) + 1 for standing in range(1, number_of + 1)]
    largest = most if full else min(most, max(-(-total // number_of), total * loads[0] // sum(loads)))
    least = 1 if total - largest >= number_of - 1 else 0
    counts, spare = [largest] + [least] * (number_of - 1), total - largest - least * (number_of - 1)
    while spare > 0:
        free = [i for i in range(1, number_of) if counts[i] < largest] or [i for i in range(1, number_of) if counts[i] < most]
        pool, left = sum([loads[i] for i in free]), spare
        for i in free:
            more = min(most - counts[i], max(1, left * loads[i] // pool), spare)
            counts[i] = counts[i] + more
            spare = spare - more
    return np.array(counts)


def scatter_about(own_key, extent, deviation, bound, split=(), kind=jnp.bfloat16):
    drawn = deviation * jax.random.normal(own_key, extent, jnp.float32)
    if split:
        drawn = drawn * block_scale(own_key, extent, split, -0.22, 0.18)
    return jnp.clip(drawn, -bound, bound).astype(kind)


def setup_inputs(seed: int = 0) -> dict:
    key_of = jax.random.split(jax.random.key(seed), 15)
    layer_input = scatter_about(key_of[0], (TOKENS, D), 1.0, 6.0, ((0, 16), (1, 2)))
    teacher = scatter_about(key_of[1], (TOKENS, D), 1.0, 6.0, ((0, 16), (1, 2)))
    valid_mask = draw_valid_mask(jax.random.fold_in(key_of[14], 71), 0)
    routes_keys = jax.random.split(jax.random.fold_in(key_of[3], 1), TOKENS // (SEQ_DEV * LEN))
    routes_turns = jax.random.permutation(jax.random.fold_in(key_of[3], 3), TOKENS // (SEQ_DEV * LEN))
    routes = jax.vmap(lambda own, number: assign_block(jax.random.fold_in(key_of[3], 2), own, number, SEQ_DEV * LEN, E, 2, CAP, 0))(routes_keys, routes_turns).reshape((TOKENS, 2))
    segments = jax.vmap(lambda own: jnp.searchsorted(jnp.cumsum(ragged_sizes(own, 4, LEN, LEN // 2, 0)), jnp.arange(LEN), side="right"))(jax.random.split(key_of[4], SEQS)).reshape((SEQS, LEN)).astype(jnp.int32)
    gain_attn = jnp.clip(1.0 + 0.1 * jax.random.normal(key_of[5], (D,), jnp.float32), 0.5, 1.5)
    gain_ffn = jnp.clip(1.0 + 0.1 * jax.random.normal(key_of[6], (D,), jnp.float32), 0.5, 1.5)
    w_qkv = scatter_about(key_of[7], (D, 3, D), D ** -0.5, 0.21875, ((0, 2), (2, 2)))
    w_out = scatter_about(key_of[8], (D, D), (D // 8) ** -0.5, 0.625, ((0, 2), (1, 2)))
    w_router = scatter_about(key_of[9], (D, E), (2 * D) ** -0.5, 0.15625, ((0, 2),))
    w_shared_up = scatter_about(key_of[10], (D, 2, FF), D ** -0.5, 0.21875, ((0, 2), (2, 2)))
    w_shared_down = scatter_about(key_of[11], (FF, D), FF ** -0.5, 0.125, ((0, 2), (1, 2)))
    w_expert_up = scatter_about(key_of[12], (E, D, 2, HE), D ** -0.5, 0.21875, ((1, 2), (3, 2)))
    w_expert_down = scatter_about(key_of[13], (E, HE, D), HE ** -0.5, 0.125, ((1, 2), (2, 2)))
    return dict(layer_input=layer_input, teacher=teacher, valid_mask=valid_mask, routes=routes, segments=segments, gain_attn=gain_attn, gain_ffn=gain_ffn, w_qkv=w_qkv, w_out=w_out, w_router=w_router, w_shared_up=w_shared_up, w_shared_down=w_shared_down, w_expert_up=w_expert_up, w_expert_down=w_expert_down)


@jax.custom_vjp
def low(v):
    return lax.optimization_barrier(v.astype(jnp.bfloat16)).astype(jnp.float32)

@jax.custom_vjp
def low_back(v):
    return v

def low_keep(v):
    return (low(v), None)

def low_pass(kept, grad):
    return (grad,)

def back_keep(v):
    return (v, None)

def back_low(kept, grad):
    return (low(grad),)
low.defvjp(low_keep, low_pass)
low_back.defvjp(back_keep, back_low)

def norm_rows(values, gain_vec):
    return values * lax.rsqrt(lax.optimization_barrier(jnp.mean(values * values, axis=-1, keepdims=True)) + 1e-06) * gain_vec

def rope_tables(length):
    half_dim = HEAD_DIM // 2
    freqs = 10000.0 ** (-jnp.arange(half_dim, dtype=jnp.float32) * 2.0 / HEAD_DIM)
    angles = jnp.arange(length, dtype=jnp.float32)[:, None] * freqs[None, :]
    angles = jnp.concatenate([angles, angles], axis=1)
    return (jnp.cos(angles), jnp.sin(angles))

def rotate(values, cosine, sine):
    half_dim = values.shape[-1] // 2
    turned = jnp.concatenate([-values[..., half_dim:], values[..., :half_dim]], axis=-1)
    return values * cosine[:, None, :] + turned * sine[:, None, :]

def attend(queries, keys_in, values_in, segment_ids):
    highest_precision = lax.Precision.HIGHEST
    scores = jnp.einsum('qhd,khd->hqk', queries, keys_in, precision=highest_precision) * HEAD_DIM ** (-0.5)
    scores = low_back(scores)
    positions = jnp.arange(LEN)
    allowed = (segment_ids[:, None] == segment_ids[None, :]) & (positions[None, :] // ABLOCK <= positions[:, None] // ABLOCK)
    scores = jnp.where(allowed[None], scores, -1e+30)
    highest = lax.optimization_barrier(jnp.max(scores, axis=-1, keepdims=True))
    weight = jnp.exp(scores - highest)
    shares = weight / lax.optimization_barrier(jnp.sum(weight, axis=-1, keepdims=True))
    return jnp.einsum('hqk,khd->qhd', low(shares), values_in, precision=highest_precision)

def group_loss(residual, teacher, valid_mask, routes, segments, gain_attn, gain_ffn, w_qkv, w_out, w_router, w_shared_up, w_shared_down, w_expert_up, w_expert_down):
    highest_precision = lax.Precision.HIGHEST
    group_rows = residual.shape[0]
    normed_attn = low(norm_rows(residual, gain_attn))
    qkv_pre = low_back(jnp.einsum('td,dke->tke', normed_attn, w_qkv, precision=highest_precision))
    qkv_pre = qkv_pre.reshape(group_rows // LEN, LEN, 3, HEADS, HEAD_DIM)
    cosine, sine = rope_tables(LEN)

    def one_sequence(pieces):
        sequence, segment_ids = pieces
        queries = low(rotate(sequence[:, 0], cosine, sine))
        keys_in = low(rotate(sequence[:, 1], cosine, sine))
        values_in = low(sequence[:, 2])
        return attend(queries, keys_in, values_in, segment_ids)
    context = lax.map(jax.checkpoint(one_sequence), (qkv_pre, segments))
    context = low_back(low(context.reshape(group_rows, D)))
    attention = low_back(jnp.dot(context, w_out, precision=highest_precision))
    hidden = residual + attention
    normed_ffn = low(norm_rows(hidden, gain_ffn))
    logits = low_back(jnp.dot(normed_ffn, w_router, precision=highest_precision))
    picks = (routes[:, :, None] == jnp.arange(E, dtype=jnp.int32)[None, None, :]).astype(jnp.float32)
    chosen = lax.optimization_barrier(jnp.sum(picks * logits[:, None, :], axis=2))
    chosen = chosen - lax.optimization_barrier(jnp.max(chosen, axis=1, keepdims=True))
    gates = jnp.exp(chosen)
    gates = gates / lax.optimization_barrier(jnp.sum(gates, axis=1, keepdims=True))
    mixing = lax.optimization_barrier(jnp.sum(picks * gates[:, :, None], axis=1))
    shared_pre = low_back(jnp.einsum('td,dkf->tkf', normed_ffn, w_shared_up, precision=highest_precision))
    shared_act = low(jax.nn.silu(shared_pre[:, 0]) * shared_pre[:, 1])
    branch = jnp.dot(shared_act, w_shared_down, precision=highest_precision)
    for expert in range(E):
        expert_pre = low_back(jnp.einsum('td,dkh->tkh', normed_ffn, w_expert_up[expert], precision=highest_precision))
        expert_act = low(jax.nn.silu(expert_pre[:, 0]) * expert_pre[:, 1] * mixing[:, expert:expert + 1])
        branch = branch + jnp.dot(expert_act, w_expert_down[expert], precision=highest_precision)
    branch = low_back(branch)
    output = hidden + branch
    error = output - teacher
    loss_part = jnp.sum(valid_mask.astype(jnp.float32) * lax.optimization_barrier(jnp.sum(error * error, axis=-1)))
    return (loss_part, output)

def reference(layer_input, teacher, valid_mask, routes, segments, gain_attn, gain_ffn, w_qkv, w_out, w_router, w_shared_up, w_shared_down, w_expert_up, w_expert_down):
    group_rows = LEN * math.gcd(TOKENS // LEN, max(1, 4096 // LEN))
    count = jnp.sum(valid_mask.astype(jnp.float32))
    teacher_groups = teacher.astype(jnp.float32).reshape(-1, group_rows, D)
    valid_groups = valid_mask.reshape(-1, group_rows)
    route_groups = routes.reshape(-1, group_rows, 2)
    segment_groups = segments.reshape(-1, group_rows // LEN, LEN)
    params = (layer_input.astype(jnp.float32), gain_attn.astype(jnp.float32), gain_ffn.astype(jnp.float32), w_qkv.astype(jnp.float32), w_out.astype(jnp.float32), w_router.astype(jnp.float32), w_shared_up.astype(jnp.float32), w_shared_down.astype(jnp.float32), w_expert_up.astype(jnp.float32), w_expert_down.astype(jnp.float32))

    def total_loss(residual, g_attn, g_ffn, wq, wo, wr, wsu, wsd, weu, wed):
        residual_groups = residual.reshape(-1, group_rows, D)
        checked = jax.checkpoint(group_loss)

        def advance(carry, pieces):
            part_loss, output = checked(pieces[0], pieces[1], pieces[2], pieces[3], pieces[4], g_attn, g_ffn, wq, wo, wr, wsu, wsd, weu, wed)
            return (carry + part_loss, output)
        summed, outputs = lax.scan(advance, jnp.zeros((), jnp.float32), (residual_groups, teacher_groups, valid_groups, route_groups, segment_groups))
        return (summed / (2.0 * count), outputs.reshape(TOKENS, D))
    loss, backward, output = jax.vjp(total_loss, *params, has_aux=True)
    grads = backward(jnp.asarray(float(TOKENS), dtype=jnp.float32))
    return (output, loss, grads[0], grads[1], grads[2], grads[3], grads[4], grads[5], grads[6], grads[7], grads[8], grads[9])
```

```python
import jax
import jax.numpy as jnp
from jax import lax
from jax.sharding import PartitionSpec as P

D = 768
HEAD_DIM = 64
E = 4
LEN = 1024
ABLOCK = 256
BF = jnp.bfloat16
F32 = jnp.float32


def norm_forward(values, gain_vec):
    rstd_rows = lax.rsqrt(jnp.mean(values * values, axis=1) + 1e-06)
    return (rstd_rows, values * rstd_rows[:, None] * gain_vec)


def norm_backward(values, rstd_rows, gain_vec, incoming):
    scaled = incoming * gain_vec
    inner_sum = jnp.sum(scaled * values, axis=1)
    gain_grad = jnp.sum(incoming * values * rstd_rows[:, None], axis=0)
    result = rstd_rows[:, None] * scaled - values * (rstd_rows**3 * inner_sum / D)[:, None]
    return (result, gain_grad)


def rope_tables(length):
    half_dim = HEAD_DIM // 2
    freqs = 10000.0 ** (-jnp.arange(half_dim, dtype=jnp.float32) * 2.0 / HEAD_DIM)
    angles = jnp.arange(length, dtype=jnp.float32)[:, None] * freqs[None, :]
    angles = jnp.concatenate([angles, angles], axis=1)
    return (jnp.cos(angles), jnp.sin(angles))


def rotate(values, cosine, sine):
    half_dim = values.shape[-1] // 2
    turned = jnp.concatenate([-values[..., half_dim:], values[..., :half_dim]], axis=-1)
    return values * cosine[:, None, :] + turned * sine[:, None, :]


def unrotate(incoming, cosine, sine):
    half_dim = incoming.shape[-1] // 2
    moved = incoming * sine[:, None, :]
    return incoming * cosine[:, None, :] + jnp.concatenate(
        [moved[..., half_dim:], -moved[..., :half_dim]], axis=-1
    )


def allowed_pairs(segment_ids, first_row, query_rows):
    query_pos = first_row + jnp.arange(query_rows)
    key_pos = jnp.arange(segment_ids.shape[0])
    query_seg = lax.dynamic_slice_in_dim(segment_ids, first_row, query_rows, 0)
    return (query_seg[:, None] == segment_ids[None, :]) & (
        key_pos[None, :] // ABLOCK <= query_pos[:, None] // ABLOCK
    )


def attend_forward(query_all, key_all, value_all, segment_ids, query_rows):
    length = key_all.shape[0]
    rescale = HEAD_DIM ** (-0.5)

    def one_block(block_index):
        first_row = block_index * query_rows
        query_part = lax.dynamic_slice_in_dim(query_all, first_row, query_rows, 0)
        scores = (
            jnp.einsum("qhd,khd->hqk", query_part, key_all, preferred_element_type=jnp.float32)
            * rescale
        )
        scores = jnp.where(allowed_pairs(segment_ids, first_row, query_rows)[None], scores, -1e30)
        highest = jnp.max(scores, axis=2, keepdims=True)
        weight = jnp.exp(scores - highest)
        totals = jnp.sum(weight, axis=2, keepdims=True)
        shares_low = (weight / totals).astype(jnp.bfloat16)
        context = jnp.einsum(
            "hqk,khd->qhd", shares_low, value_all, preferred_element_type=jnp.float32
        )
        return (context, jnp.transpose((highest + jnp.log(totals))[:, :, 0]))

    context, log_totals = lax.map(one_block, jnp.arange(length // query_rows))
    return (context.reshape(key_all.shape), log_totals.reshape(length, -1))


def attend_backward(
    query_all, key_all, value_all, context_grad, log_totals, segment_ids, query_rows
):
    length = key_all.shape[0]
    rescale = HEAD_DIM ** (-0.5)

    def one_block(carry, block_index):
        key_grad, value_grad = carry
        first_row = block_index * query_rows
        query_part = lax.dynamic_slice_in_dim(query_all, first_row, query_rows, 0)
        grad_part = lax.dynamic_slice_in_dim(context_grad, first_row, query_rows, 0)
        total_part = jnp.transpose(lax.dynamic_slice_in_dim(log_totals, first_row, query_rows, 0))
        scores = (
            jnp.einsum("qhd,khd->hqk", query_part, key_all, preferred_element_type=jnp.float32)
            * rescale
        )
        scores = jnp.where(allowed_pairs(segment_ids, first_row, query_rows)[None], scores, -1e30)
        shares = jnp.exp(scores - total_part[:, :, None])
        value_grad = value_grad + jnp.einsum(
            "hqk,qhd->khd",
            shares.astype(jnp.bfloat16),
            grad_part,
            preferred_element_type=jnp.float32,
        )
        share_grad = jnp.einsum(
            "qhd,khd->hqk", grad_part, value_all, preferred_element_type=jnp.float32
        )
        centre = jnp.sum(shares * share_grad, axis=2, keepdims=True)
        score_grad = (shares * (share_grad - centre)).astype(jnp.bfloat16)
        query_grad = (
            jnp.einsum("hqk,khd->qhd", score_grad, key_all, preferred_element_type=jnp.float32)
            * rescale
        )
        key_grad = (
            key_grad
            + jnp.einsum("hqk,qhd->khd", score_grad, query_part, preferred_element_type=jnp.float32)
            * rescale
        )
        return ((key_grad, value_grad), query_grad)

    zero_grads = jnp.zeros(key_all.shape, jnp.float32)
    (key_grad, value_grad), query_grad = lax.scan(
        one_block, (zero_grads, zero_grads), jnp.arange(length // query_rows)
    )
    return (query_grad.reshape(key_all.shape), key_grad, value_grad)


def swap(values, axis):
    return lax.ppermute(values, axis, [(0, 1), (1, 0)])


def flip(values):
    half = values.shape[-1] // 2
    return jnp.concatenate([values[..., half:], values[..., :half]], axis=-1)


def dp_pairs(bit):
    n = lax.axis_size("dp")
    return [(i, i ^ (1 << bit)) for i in range(n)]


def dp_bits():
    count = lax.axis_size("dp").bit_length() - 1
    return [0] + list(range(count - 1, 0, -1)) if count else []


def my_bit(bit):
    return (lax.axis_index("dp") >> bit) & 1


def dp_reduce(values, axis):
    n = lax.axis_size("dp")
    count = n.bit_length() - 1
    shape = values.shape
    values = values.reshape(shape[:axis] + (2,) * count + shape[axis + 1 :])
    left = list(range(count - 1, -1, -1))
    for bit in dp_bits():
        at = axis + left.index(bit)
        mine = my_bit(bit)
        keep = lax.dynamic_index_in_dim(values, mine, at, keepdims=False)
        send = lax.dynamic_index_in_dim(values, 1 - mine, at, keepdims=False)
        recv = lax.ppermute(send, "dp", dp_pairs(bit))
        values = (keep.astype(F32) + recv.astype(F32)).astype(BF)
        left.remove(bit)
    return values


def order_pair(first_is_own, own, other, axis, stack=False):
    if stack:
        return jnp.where(first_is_own, jnp.stack([own, other], axis), jnp.stack([other, own], axis))
    return jnp.where(
        first_is_own, jnp.concatenate([own, other], axis), jnp.concatenate([other, own], axis)
    )


def dp_gather(values, axis):
    n = lax.axis_size("dp")
    have = []
    for bit in reversed(dp_bits()):
        have = sorted(have + [bit], reverse=True)
        at = axis + have.index(bit)
        recv = lax.ppermute(values, "dp", dp_pairs(bit))
        values = order_pair(my_bit(bit) == 0, values, recv, at, stack=True)
    shape = values.shape
    count = len(have)
    return values.reshape(shape[:axis] + (n,) + shape[axis + count :])


def silu_parts(values):
    sigma = jax.nn.sigmoid(values)
    return (values * sigma, sigma * (1.0 + values * (1.0 - sigma)))


def spread_tokens(own):
    near = swap(own, "col")
    far = swap(flip(own), "row")
    far_near = swap(far, "col")
    return jnp.stack([own, near, far, far_near])


def collect_tokens(parts):
    recv = swap(jnp.stack([parts[1], parts[3]]).astype(BF), "col").astype(F32)
    own = parts[0] + recv[0]
    far = parts[2] + recv[1]
    return own + swap(flip(far.astype(BF)), "row").astype(F32)


def to_sequence(values, r, c):
    other = lax.ppermute(values, ("row", "col"), [(1, 3), (2, 0)])
    pair = jnp.stack([values, other])
    copied = lax.ppermute(pair, ("row", "col"), [(0, 1), (3, 2)])
    return jnp.where(r == c, pair, copied)


def from_sequence(values, r, c):
    half = values.shape[1] // 2
    own, peer = values[:, :half], values[:, half:]
    diag = r == c
    send = jnp.where(diag, peer, own)
    kept = jnp.where(diag, own, peer)
    recv = swap(send, "col")
    whole = order_pair(c == 0, kept, recv, 0)
    moved = lax.ppermute(whole, ("row", "col"), [(1, 2), (2, 1)])
    return jnp.where(diag, whole, moved)


def local(
    layer_input,
    teacher,
    valid_mask,
    routes,
    segments,
    gain_attn,
    gain_ffn,
    w_qkv,
    w_out,
    w_router,
    w_shared_up,
    w_shared_down,
    w_expert_up,
    w_expert_down,
):
    r = lax.axis_index("row")
    c = lax.axis_index("col")
    n_dp = lax.axis_size("dp")
    rows = layer_input.shape[0]
    part = rows // 2
    half = layer_input.shape[1]
    heads = w_qkv.shape[2] // HEAD_DIM
    ff = w_shared_up.shape[2]
    quarter = ff // 2
    slots = E + 1

    x_pair = to_sequence(layer_input, r, c)
    x_seq = jnp.concatenate([x_pair[0], x_pair[1]], axis=1).astype(F32)
    w_qkv_full = jnp.concatenate([w_qkv, swap(w_qkv, "row")], axis=0)
    w_out_full = jnp.concatenate([w_out, swap(w_out, "row")], axis=1)
    gain_a = jnp.concatenate([gain_attn, swap(gain_attn, "row")])
    gain_f = jnp.concatenate([gain_ffn, swap(gain_ffn, "row")])
    w_r = jnp.concatenate([w_router, swap(w_router, "row")])
    t_pair = to_sequence(teacher, r, c)
    t_seq = jnp.concatenate([t_pair[0], t_pair[1]], axis=1)
    teacher_own = lax.dynamic_slice_in_dim(t_seq, c * part, part, 0).astype(F32)
    valid_other = swap(valid_mask, "col")
    valid_seq = jnp.where(r == c, valid_mask, valid_other).astype(F32)
    valid_own = lax.dynamic_slice_in_dim(valid_seq, c * part, part, 0)
    count = lax.psum(jnp.sum(valid_own), ("dp", "row", "col"))
    seg = lax.dynamic_slice_in_dim(segments, r, 1, 0)[0]
    route_blocks = routes.reshape(2, 2, part, 2)
    route_blocks = jnp.where(r == 0, route_blocks, route_blocks[::-1])
    route_blocks = jnp.where(c == 0, route_blocks, route_blocks[:, ::-1]).reshape(4 * part, 2)
    picks = (route_blocks[:, :, None] == jnp.arange(E, dtype=jnp.int32)[None, None, :]).astype(F32)

    up_all = jnp.concatenate([w_shared_up[None], w_expert_up], axis=0)
    down_all = jnp.concatenate([w_shared_down[None], w_expert_down], axis=0)
    up_keep = lax.dynamic_slice_in_dim(up_all, r * quarter, quarter, 3)
    up_send = lax.dynamic_slice_in_dim(up_all, (1 - r) * quarter, quarter, 3)
    down_keep = lax.dynamic_slice_in_dim(down_all, r * quarter, quarter, 1)
    down_send = lax.dynamic_slice_in_dim(down_all, (1 - r) * quarter, quarter, 1)
    w_up = jnp.concatenate([up_keep, swap(up_send, "row")], axis=1)
    w_down = jnp.concatenate([down_keep, swap(down_send, "row")], axis=2)

    rstd_seq, normed = norm_forward(x_seq, gain_a)
    normed_attn = normed.astype(BF)
    qkv_pre = jnp.einsum("td,dke->tke", normed_attn, w_qkv_full, preferred_element_type=F32)
    qkv_pre = qkv_pre.reshape(rows, 3, heads, HEAD_DIM)
    cosine, sine = rope_tables(rows)
    queries = rotate(qkv_pre[:, 0], cosine, sine).astype(BF)
    keys_rot = rotate(qkv_pre[:, 1], cosine, sine).astype(BF)
    values_low = qkv_pre[:, 2].astype(BF)
    query_rows = min(512, rows)
    context, log_totals = attend_forward(queries, keys_rot, values_low, seg, query_rows)
    context_low = context.reshape(rows, -1).astype(BF)
    attention = jnp.dot(context_low, w_out_full, preferred_element_type=F32)
    att_halves = attention.reshape(2, part, D)
    att_keep = lax.dynamic_index_in_dim(att_halves, c, 0, keepdims=False)
    att_send = lax.dynamic_index_in_dim(att_halves, 1 - c, 0, keepdims=False)
    x_own = lax.dynamic_slice_in_dim(x_seq, c * part, part, 0)
    rstd_attn = lax.dynamic_slice_in_dim(rstd_seq, c * part, part, 0)
    hidden = x_own + att_keep + swap(att_send.astype(BF), "col").astype(F32)

    rstd_ffn, normed = norm_forward(hidden, gain_f)
    normed_low = normed.astype(BF)
    tokens = spread_tokens(normed_low).reshape(4 * part, D)
    logits = jnp.dot(tokens, w_r, preferred_element_type=F32)
    chosen = jnp.sum(picks * logits[:, None, :], axis=2)
    chosen = chosen - jnp.max(chosen, axis=1, keepdims=True)
    gates = jnp.exp(chosen)
    gates = gates / jnp.sum(gates, axis=1, keepdims=True)
    mixing = jnp.sum(picks * gates[:, :, None], axis=1)
    mix_all = jnp.concatenate([jnp.ones((4 * part, 1), F32), mixing], axis=1).T
    pre = [
        jnp.dot(tokens, w_up[e].reshape(D, 2 * quarter), preferred_element_type=F32).astype(BF)
        for e in range(slots)
    ]
    acts = []
    for e in range(slots):
        gate_pre, up_pre = pre[e][:, :quarter].astype(F32), pre[e][:, quarter:].astype(F32)
        act = gate_pre * jax.nn.sigmoid(gate_pre) * up_pre
        acts.append((act * mix_all[e][:, None]).astype(BF))
    act_all = jnp.concatenate(acts, axis=1)
    branch = jnp.dot(act_all, w_down.reshape(slots * quarter, D), preferred_element_type=F32)
    output = hidden + collect_tokens(branch.reshape(4, part, D))

    error = output - teacher_own
    loss_part = jnp.sum(valid_own * jnp.sum(error * error, axis=1))
    total_tokens = part * 4 * n_dp
    grad_out = total_tokens / count * valid_own[:, None] * error

    grads = spread_tokens(grad_out.astype(BF)).reshape(4 * part, D)
    down_grad = jnp.dot(act_all.T, grads, preferred_element_type=F32).astype(BF)
    act_back = jnp.dot(
        grads, w_down.reshape(slots * quarter, D).T, preferred_element_type=F32
    ).astype(BF)
    pre_grads = []
    gate_sums = []
    for e in range(slots):
        gate_pre, up_pre = pre[e][:, :quarter].astype(F32), pre[e][:, quarter:].astype(F32)
        back = act_back[:, e * quarter : (e + 1) * quarter].astype(F32)
        act_silu, slope = silu_parts(gate_pre)
        if e:
            gate_sums.append(jnp.sum(back * act_silu * up_pre, axis=1))
        back = back * mix_all[e][:, None]
        pre_grads.append(
            jnp.concatenate([back * up_pre * slope, back * act_silu], axis=1).astype(BF)
        )
    up_grads = [
        jnp.dot(tokens.T, pre_grads[e], preferred_element_type=F32).astype(BF)
        for e in range(slots)
    ]
    input_part = jnp.zeros((4 * part, D), F32)
    for e in range(slots):
        input_part = input_part + jnp.dot(
            pre_grads[e], w_up[e].reshape(D, 2 * quarter).T, preferred_element_type=F32
        )
    normed_ffn_grad = collect_tokens(input_part.reshape(4, part, D))
    gate_parts = jnp.stack(gate_sums, axis=0).reshape(E, 4, part)
    recv = swap(jnp.stack([gate_parts[:, 1], gate_parts[:, 3]]), "col")
    gate_grad = gate_parts[:, 0] + recv[0] + swap(gate_parts[:, 2] + recv[1], "row")
    mix_own = mixing[:part].T
    centre = jnp.sum(mix_own * gate_grad, axis=0, keepdims=True)
    logit_grad = (mix_own * (gate_grad - centre)).T.astype(BF)
    normed_ffn_grad = normed_ffn_grad + jnp.dot(logit_grad, w_r.T, preferred_element_type=F32)
    router_grad = jnp.dot(normed_low.T, logit_grad, preferred_element_type=F32)
    hidden_back, gain_ffn_grad = norm_backward(hidden, rstd_ffn, gain_f, normed_ffn_grad)
    hidden_grad = grad_out + hidden_back

    owner_f = quarter // n_dp
    owner_d = half // n_dp
    down_split = dp_reduce(down_grad.reshape(slots, n_dp, owner_f, 2, half), 1)
    down_own = down_split[:, :, 0]
    down_peer = swap(down_split[:, :, 1], "row")
    up_split = dp_reduce(jnp.stack(up_grads).reshape(slots, 2, n_dp, owner_d, 2 * quarter), 2)
    up_own = up_split[:, 0]
    up_peer = swap(up_split[:, 1], "row")
    down_out = dp_gather(jnp.stack([down_own, down_peer], 1), 2).reshape(slots, 2, quarter, half)
    down_out = jnp.where(r == 0, down_out, down_out[:, ::-1]).astype(F32)
    down_out = down_out.reshape(slots, ff, half)
    up_out = dp_gather(jnp.stack([up_own, up_peer], 1), 2)
    up_out = up_out.reshape(slots, 2, half, 2, quarter)
    up_out = order_pair(r == 0, up_out[:, 0], up_out[:, 1], 3).astype(F32)

    low_own = hidden_grad.astype(BF)
    low_seq = order_pair(c == 0, low_own, swap(low_own, "col"), 0)
    w_out_grad = jnp.dot(context_low.T, low_seq, preferred_element_type=F32).astype(BF)
    context_grad = jnp.dot(low_seq, w_out_full.T, preferred_element_type=F32)
    context_grad = context_grad.astype(BF).reshape(rows, heads, HEAD_DIM)
    query_grad, key_grad, value_grad = attend_backward(
        queries, keys_rot, values_low, context_grad, log_totals, seg, query_rows
    )
    query_grad = unrotate(query_grad, cosine, sine)
    key_grad = unrotate(key_grad, cosine, sine)
    qkv_grad = jnp.stack((query_grad, key_grad, value_grad), axis=1).reshape(rows, -1).astype(BF)
    w_qkv_grad = jnp.dot(normed_attn.T, qkv_grad, preferred_element_type=F32).astype(BF)
    back_part = jnp.dot(qkv_grad, w_qkv_full.reshape(D, -1).T, preferred_element_type=F32)
    back_halves = back_part.reshape(2, part, D)
    back_keep = lax.dynamic_index_in_dim(back_halves, c, 0, keepdims=False)
    back_send = lax.dynamic_index_in_dim(back_halves, 1 - c, 0, keepdims=False)
    normed_attn_grad = back_keep + swap(back_send.astype(BF), "col").astype(F32)
    input_back, gain_attn_grad = norm_backward(x_own, rstd_attn, gain_a, normed_attn_grad)
    input_grad = hidden_grad + input_back

    out_split = dp_reduce(w_out_grad.reshape(n_dp, owner_d, 2, half), 0)
    out_sum = out_split[:, 0].astype(F32) + swap(out_split[:, 1], "row").astype(F32)
    out_sum = dp_gather(out_sum.astype(BF), 0).reshape(half, half).astype(F32)
    qkv_split = dp_reduce(w_qkv_grad.reshape(2, n_dp, owner_d, 3 * half), 1)
    qkv_sum = qkv_split[0].astype(F32) + swap(qkv_split[1], "row").astype(F32)
    qkv_sum = dp_gather(qkv_sum.astype(BF), 0).reshape(half, 3, half).astype(F32)

    small = jnp.concatenate([gain_attn_grad[None], gain_ffn_grad[None], router_grad.T], axis=0)
    small = jnp.where(r == 0, small, flip(small))
    small = jnp.concatenate([small.reshape(-1), loss_part[None]])
    small = lax.psum(small, ("dp", "row", "col"))
    loss = small[-1] / (2.0 * count)
    small = small[:-1].reshape(E + 2, D)
    small = lax.dynamic_slice_in_dim(small, r * half, half, 1)
    return (
        from_sequence(output, r, c),
        loss,
        from_sequence(input_grad, r, c),
        small[0],
        small[1],
        qkv_sum,
        out_sum,
        small[2:].T,
        up_out[0],
        down_out[0],
        up_out[1:],
        down_out[1:],
    )


def solution(mesh):
    return jax.shard_map(
        local,
        mesh=mesh,
        in_specs=(
            P(("dp", "col"), "row"),
            P(("dp", "col"), "row"),
            P(("dp", "col")),
            P("dp", None),
            P("dp", None),
            P("row"),
            P("row"),
            P("row", None, "col"),
            P("col", "row"),
            P("row", None),
            P("row", None, "col"),
            P("col", "row"),
            P(None, "row", None, "col"),
            P(None, "col", "row"),
        ),
        out_specs=(
            P(("dp", "col"), "row"),
            P(),
            P(("dp", "col"), "row"),
            P("row"),
            P("row"),
            P("row", None, "col"),
            P("col", "row"),
            P("row", None),
            P("row", None, "col"),
            P("col", "row"),
            P(None, "row", None, "col"),
            P(None, "col", "row"),
        ),
        check_vma=False,
    )
```

```python
import functools

import jax
import jax.numpy as jnp
from jax import lax
from jax.experimental import pallas as pl
from jax.experimental.pallas import tpu as pltpu
from jax.sharding import PartitionSpec as P

D = 768
HEAD_DIM = 64
E = 4
LEN = 1024
ABLOCK = 256
BF = jnp.bfloat16
F32 = jnp.float32


def norm_forward(values, gain_vec):
    rstd_rows = lax.rsqrt(jnp.mean(values * values, axis=1) + 1e-06)
    return (rstd_rows, values * rstd_rows[:, None] * gain_vec)


def norm_backward(values, rstd_rows, gain_vec, incoming):
    scaled = incoming * gain_vec
    inner_sum = jnp.sum(scaled * values, axis=1)
    gain_grad = jnp.sum(incoming * values * rstd_rows[:, None], axis=0)
    result = rstd_rows[:, None] * scaled - values * (rstd_rows**3 * inner_sum / D)[:, None]
    return (result, gain_grad)


def rope_tables(length):
    half_dim = HEAD_DIM // 2
    freqs = 10000.0 ** (-jnp.arange(half_dim, dtype=F32) * 2.0 / HEAD_DIM)
    angles = jnp.arange(length, dtype=F32)[:, None] * freqs[None, :]
    sine = jnp.sin(angles)
    return (jnp.tile(jnp.cos(angles), (1, 4)), jnp.tile(jnp.concatenate([-sine, sine], axis=1), (1, 2)))


def lanes_of(shape):
    return lax.broadcasted_iota(jnp.int32, shape, len(shape) - 1)


def turn(values, first):
    half_dim = HEAD_DIM // 2
    return jnp.where(
        first,
        pltpu.roll(values, PAIR - half_dim, values.ndim - 1),
        pltpu.roll(values, half_dim, values.ndim - 1),
    )


PAIR = 2 * HEAD_DIM
NT = (((1,), (1,)), ((), ()))


def shares_of(key_pair, query_head, seg_col, seg_row):
    scores = lax.dot_general(key_pair, query_head, NT, preferred_element_type=F32)
    scores = jnp.where(seg_col == seg_row, scores, -1e30)
    weight = jnp.exp(scores - jnp.max(scores, axis=0, keepdims=True))
    return weight * (1.0 / jnp.sum(weight, axis=0, keepdims=True))


def attend_kernel(pre, cosine, sine, seg_row, seg_col, queries, keys, values, context):
    rows = pre.shape[1]
    first = lanes_of((rows, PAIR)) % HEAD_DIM < HEAD_DIM // 2
    cos, sin = cosine[...], sine[...]
    query = pre[0]
    queries[...] = ((query * cos + turn(query, first) * sin) * HEAD_DIM**-0.5).astype(BF)
    key = pre[1]
    keys[...] = (key * cos + turn(key, first) * sin).astype(BF)
    value = pre[2]
    values[...] = value.astype(BF)
    value_t = value.T.astype(BF)
    lower = lanes_of((ABLOCK, PAIR)) < HEAD_DIM
    for block in range(rows // ABLOCK):
        start, stop = block * ABLOCK, (block + 1) * ABLOCK
        query = queries[start:stop]
        parts = []
        for head in range(2):
            query_head = jnp.where(lower == (head == 0), query, jnp.zeros_like(query))
            shares = shares_of(
                keys[:stop], query_head, seg_col[:stop], seg_row[:, start:stop]
            ).astype(BF)
            parts.append(jnp.dot(value_t[:, :stop], shares, preferred_element_type=F32))
        both = jnp.concatenate([parts[0][:HEAD_DIM], parts[1][HEAD_DIM:]], axis=0)
        context[start:stop] = both.T.astype(BF)


def attend_forward(pre, tables, seg_row, seg_col):
    _, rows, width = pre.shape
    block = pl.BlockSpec((rows, PAIR), lambda i: (0, i))
    whole = pl.BlockSpec((rows, PAIR), lambda i: (0, 0))
    return pl.pallas_call(
        attend_kernel,
        grid=(width // PAIR,),
        out_shape=[jax.ShapeDtypeStruct((rows, width), BF)] * 4,
        in_specs=[
            pl.BlockSpec((3, rows, PAIR), lambda i: (0, 0, i)),
            whole,
            whole,
            pl.BlockSpec((1, rows), lambda i: (0, 0)),
            pl.BlockSpec((rows, 1), lambda i: (0, 0)),
        ],
        out_specs=[block] * 4,
        compiler_params=pltpu.CompilerParams(vmem_limit_bytes=40 << 20),
        cost_estimate=pl.CostEstimate(
            flops=20_000_000_000, bytes_accessed=8 << 20, transcendentals=4 << 20
        ),
    )(pre, tables[0], tables[1], seg_row, seg_col)


def attend_back_kernel(
    queries, keys, values, context_grad, cosine, sine, seg_row, seg_col, out, key_sum, value_sum
):
    rows = queries.shape[0]
    key_t = keys[...].astype(F32).T.astype(BF)
    lower = lanes_of((ABLOCK, PAIR)) < HEAD_DIM
    first = lanes_of((ABLOCK, PAIR)) % HEAD_DIM < HEAD_DIM // 2
    for block in reversed(range(rows // ABLOCK)):
        start, stop = block * ABLOCK, (block + 1) * ABLOCK
        query, incoming = queries[start:stop], context_grad[start:stop]
        parts, key_part, value_part = [], None, None
        for head in range(2):
            mine = lower == (head == 0)
            query_head = jnp.where(mine, query, jnp.zeros_like(query))
            incoming_head = jnp.where(mine, incoming, jnp.zeros_like(incoming))
            shares = shares_of(keys[:stop], query_head, seg_col[:stop], seg_row[:, start:stop])
            share_grad = lax.dot_general(
                values[:stop], incoming_head, NT, preferred_element_type=F32
            )
            centre = jnp.sum(shares * share_grad, axis=0, keepdims=True)
            score_grad = (shares * (share_grad - centre)).astype(BF)
            parts.append(jnp.dot(key_t[:, :stop], score_grad, preferred_element_type=F32))
            more = jnp.dot(shares.astype(BF), incoming_head, preferred_element_type=F32)
            value_part = more if head == 0 else value_part + more
            more = jnp.dot(score_grad, query_head, preferred_element_type=F32)
            key_part = more if head == 0 else key_part + more
        both = jnp.concatenate([parts[0][:HEAD_DIM], parts[1][HEAD_DIM:]], axis=0)
        grad = both.T * HEAD_DIM**-0.5
        cos, sin = cosine[start:stop], sine[start:stop]
        out[0, start:stop] = (grad * cos + turn(grad * sin, first)).astype(BF)
        if stop == rows:
            key_sum[...] = key_part
            value_sum[...] = value_part
        else:
            key_sum[:stop] += key_part
            value_sum[:stop] += value_part
    for block in range(rows // ABLOCK):
        start, stop = block * ABLOCK, (block + 1) * ABLOCK
        grad = key_sum[start:stop]
        cos, sin = cosine[start:stop], sine[start:stop]
        out[1, start:stop] = (grad * cos + turn(grad * sin, first)).astype(BF)
        out[2, start:stop] = value_sum[start:stop].astype(BF)


def attend_backward(queries, keys, values, context_grad, tables, seg_row, seg_col, first_pair, pairs):
    rows = queries.shape[0]
    block = pl.BlockSpec((rows, PAIR), lambda i: (0, i + first_pair))
    whole = pl.BlockSpec((rows, PAIR), lambda i: (0, 0))
    return pl.pallas_call(
        attend_back_kernel,
        grid=(pairs,),
        out_shape=jax.ShapeDtypeStruct((3, rows, pairs * PAIR), BF),
        in_specs=[block] * 4
        + [
            whole,
            whole,
            pl.BlockSpec((1, rows), lambda i: (0, 0)),
            pl.BlockSpec((rows, 1), lambda i: (0, 0)),
        ],
        out_specs=pl.BlockSpec((3, rows, PAIR), lambda i: (0, 0, i)),
        scratch_shapes=[pltpu.VMEM((rows, PAIR), F32), pltpu.VMEM((rows, PAIR), F32)],
        compiler_params=pltpu.CompilerParams(vmem_limit_bytes=40 << 20),
        cost_estimate=pl.CostEstimate(
            flops=pairs * 14_000_000_000, bytes_accessed=4 << 20, transcendentals=2 << 20
        ),
    )(queries, keys, values, context_grad, tables[0], tables[1], seg_row, seg_col)


def swap(values, axis):
    return lax.ppermute(values, axis, [(0, 1), (1, 0)])


def flip(values):
    half = values.shape[-1] // 2
    return jnp.concatenate([values[..., half:], values[..., :half]], axis=-1)


def dp_pairs(bit):
    n = lax.axis_size("dp")
    return [(i, i ^ (1 << bit)) for i in range(n)]


def dp_sum(values):
    for bit in range(lax.axis_size("dp").bit_length() - 1):
        values = values + lax.ppermute(values, "dp", dp_pairs(bit))
    values = values + swap(values, "row")
    return values + swap(values, "col")


def remote(src, dst, send, recv, device):
    return pltpu.make_async_remote_copy(
        src_ref=src,
        dst_ref=dst,
        send_sem=send,
        recv_sem=recv,
        device_id=device,
        device_id_type=pl.DeviceIdType.MESH,
    )


def greet(devices):
    barrier = pltpu.get_barrier_semaphore()
    for device in devices:
        pl.semaphore_signal(
            barrier, inc=1, device_id=device, device_id_type=pl.DeviceIdType.MESH
        )
    pl.semaphore_wait(barrier, len(devices))


AHEAD = 3
BEHIND = 3


def reduce_kernel(n, slots, *refs):
    ups, (down, attn) = refs[:slots], refs[slots : slots + 2]
    up_out, down_out, attn_out = refs[slots + 2 : slots + 5]
    (
        up_keep, down_keep, attn_keep, up_x, down_x, attn_x, up_z, down_z, attn_z,
        up_done, down_done, attn_done, attn_y,
        keep_sem, x_send, x_recv, z_send, z_recv, out_sem, y_send, y_recv,
    ) = refs[slots + 5 :]
    me = lax.axis_index("dp")
    row = lax.axis_index("row")
    deep = n // 2
    z, x = me // 2, me % 2
    partner = {"dp": 2 * z + (1 - x)}
    peer = {"row": 1 - row}
    ahead = [lax.rem(z + k, deep) for k in range(deep)]
    greet([partner, peer] + [{"dp": 2 * ahead[k] + x} for k in range(1, deep)])

    items = [("down", e) for e in range(slots)]
    items += [("up", 2 * e + h) for e in range(slots) for h in (1, 0)]
    items += [("attn", 0)]
    count = len(items)
    last = count - 1

    def buffers(item):
        kind, at = items[item]
        if kind == "down":
            return down.at[at], down_keep.at[at], down_x.at[at], down_z.at[at], down_done.at[at]
        if kind == "up":
            return ups[at // 2].at[at % 2], up_keep.at[at], up_x.at[at], up_z.at[at], up_done.at[at]
        return None, attn_keep.at[:, x], attn_x, attn_z, attn_done

    y_first = remote(attn.at[1], attn_y, y_send.at[last], y_recv.at[last], peer)
    y_first.start()
    attn_load = pltpu.make_async_copy(attn.at[0], attn_keep, keep_sem.at[last])
    attn_load.start()
    loads, x_copies, z_copies, outs, y_copies = {}, {}, {}, [], [y_first]
    for item in range(last):
        source, keep, _, _, _ = buffers(item)
        loads[item] = pltpu.make_async_copy(source.at[:, x], keep, keep_sem.at[item])
        loads[item].start()

    def send_x(item):
        source, keep, landing, _, _ = buffers(item)
        if item == last:
            attn_load.wait()
            y_first.wait_recv()
            attn_keep[...] = (attn_keep[...].astype(F32) + attn_y[...].astype(F32)).astype(BF)
            given = attn_keep.at[:, 1 - x]
        else:
            given = source.at[:, 1 - x]
        x_copies[item] = remote(given, landing, x_send.at[item], x_recv.at[item], partner)
        x_copies[item].start()

    def send_z(item):
        _, keep, landing, arrivals, _ = buffers(item)
        if item in loads:
            loads[item].wait()
        x_copies[item].wait_recv()
        keep[...] = (keep[...].astype(F32) + landing[...].astype(F32)).astype(BF)
        for k in range(1, deep):
            copy = remote(
                keep.at[ahead[k]],
                arrivals.at[k - 1],
                z_send.at[item, k],
                z_recv.at[item, k],
                {"dp": 2 * ahead[k] + x},
            )
            copy.start()
            z_copies[item, k] = copy

    def finish(item):
        kind, at = items[item]
        _, keep, _, arrivals, done = buffers(item)
        total = keep[z].astype(F32)
        for k in range(1, deep):
            z_copies[item, k].wait_recv()
            total = total + arrivals[k - 1].astype(F32)
        done[...] = total.astype(BF)
        half = down.shape[4] // 2

        def keep_own(source, target):
            copy = pltpu.make_async_copy(source, target, out_sem.at[item])
            copy.start()
            outs.append(copy)

        def give_peer(source, target):
            copy = remote(source, target, y_send.at[item], y_recv.at[item], peer)
            copy.start()
            y_copies.append(copy)

        if kind == "down":
            keep_own(done.at[:, :half], down_out.at[0, at])
            give_peer(done.at[:, half:], down_out.at[1, at])
        elif kind == "attn":
            keep_own(done, attn_out)
        elif at % 2 == 0:
            keep_own(done, up_out.at[0, at // 2])
        else:
            give_peer(done, up_out.at[1, at // 2])

    for step in range(count + AHEAD + BEHIND):
        if step < count:
            send_x(step)
        if 0 <= step - AHEAD < count:
            send_z(step - AHEAD)
        if 0 <= step - AHEAD - BEHIND < count:
            finish(step - AHEAD - BEHIND)
    for copy in outs:
        copy.wait()
    y_first.wait_send()
    for copy in y_copies[1:]:
        copy.wait()
    for copy in list(x_copies.values()) + list(z_copies.values()):
        copy.wait_send()


def dp_reduce(up_grads, down_grad, attn_grad):
    n = lax.axis_size("dp")
    deep = n // 2
    slots = len(up_grads)
    up_tail, down_tail, attn_tail = up_grads[0].shape[3:], down_grad.shape[3:], attn_grad.shape[3:]
    sems = pltpu.SemaphoreType.DMA
    count = 3 * slots + 1
    vmem = lambda *shape: pltpu.VMEM(shape, BF)
    half = down_tail[1] // 2
    any_spec = pl.BlockSpec(memory_space=pl.ANY)
    return pl.pallas_call(
        functools.partial(reduce_kernel, n, slots),
        out_shape=[
            jax.ShapeDtypeStruct((2, slots) + up_tail, BF),
            jax.ShapeDtypeStruct((2, slots, down_tail[0], half), BF),
            jax.ShapeDtypeStruct(attn_tail, BF),
        ],
        in_specs=[any_spec] * (slots + 2),
        out_specs=[any_spec] * 3,
        scratch_shapes=[
            vmem(2 * slots, deep, *up_tail),
            vmem(slots, deep, *down_tail),
            vmem(deep, 2, *attn_tail),
            vmem(2 * slots, deep, *up_tail),
            vmem(slots, deep, *down_tail),
            vmem(deep, *attn_tail),
            vmem(2 * slots, deep - 1, *up_tail),
            vmem(slots, deep - 1, *down_tail),
            vmem(deep - 1, *attn_tail),
            vmem(2 * slots, *up_tail),
            vmem(slots, *down_tail),
            vmem(*attn_tail),
            vmem(deep, 2, *attn_tail),
            sems((count,)),
            sems((count,)),
            sems((count,)),
            sems((count, deep)),
            sems((count, deep)),
            sems((count,)),
            sems((count,)),
            sems((count,)),
        ],
        compiler_params=pltpu.CompilerParams(
            collective_id=1, has_side_effects=True, vmem_limit_bytes=48 << 20
        ),
    )(*up_grads, down_grad, attn_grad)


def order_pair(first_is_own, own, other, axis):
    return jnp.where(
        first_is_own, jnp.concatenate([own, other], axis), jnp.concatenate([other, own], axis)
    )


WINDOW = 2


def gather_kernel(n, plan, *refs):
    count = max(item[0] for item in plan) + 1
    pieces, fulls = refs[:count], refs[count : 2 * count]
    own_sem, z_send, z_recv, x_send, x_recv = refs[2 * count :]
    me = lax.axis_index("dp")
    deep = n // 2
    z, x = me // 2, me % 2
    partner = 2 * z + (1 - x)
    peers = [2 * lax.rem(z + k, deep) + x for k in range(1, deep)]
    sources = [2 * lax.rem(z + deep - k, deep) + x for k in range(deep)]

    greet([{"dp": device} for device in peers + [partner]])

    def region(item, owner):
        at, lead, rows = plan[item]
        full = fulls[at]
        for index in lead:
            full = full.at[index]
        if rows == 0:
            return full.at[owner]
        start = owner * rows
        if rows % 16 == 0:
            start = pl.multiple_of(start, 16)
        return full.at[pl.ds(start, rows)]

    def piece(item):
        at, lead, rows = plan[item]
        ref = pieces[at]
        for index in lead:
            ref = ref.at[index]
        return ref

    total = len(plan)
    local_copies = []
    z_copies = [[] for _ in range(total)]
    x_copies = [[] for _ in range(total)]
    for step in range(total + WINDOW):
        if step < total:
            here = region(step, me)
            for k in range(1, deep):
                copy = remote(
                    piece(step), here, z_send.at[step, k], z_recv.at[step, k], {"dp": peers[k - 1]}
                )
                copy.start()
                z_copies[step].append(copy)
            copy = remote(piece(step), here, x_send.at[step, 0], x_recv.at[step, 0], {"dp": partner})
            copy.start()
            x_copies[step].append(copy)
            copy = pltpu.make_async_copy(piece(step), here, own_sem.at[step])
            copy.start()
            local_copies.append(copy)
        if step >= WINDOW:
            item = step - WINDOW
            for k in range(1, deep):
                z_copies[item][k - 1].wait_recv()
                arrived = region(item, sources[k])
                copy = remote(
                    arrived, arrived, x_send.at[item, k], x_recv.at[item, k], {"dp": partner}
                )
                copy.start()
                x_copies[item].append(copy)
    for item in range(total):
        local_copies[item].wait()
        for copy in z_copies[item]:
            copy.wait_send()
        for copy in x_copies[item]:
            copy.wait()


def dp_gather(pieces, fulls, plan):
    n = lax.axis_size("dp")
    total = len(plan)
    sems = pltpu.SemaphoreType.DMA
    return pl.pallas_call(
        functools.partial(gather_kernel, n, plan),
        out_shape=[jax.ShapeDtypeStruct(shape, BF) for shape in fulls],
        in_specs=[pl.BlockSpec(memory_space=pl.ANY)] * len(pieces),
        out_specs=[pl.BlockSpec(memory_space=pl.ANY)] * len(fulls),
        scratch_shapes=[
            sems((total,)),
            sems((total, n // 2)),
            sems((total, n // 2)),
            sems((total, n // 2)),
            sems((total, n // 2)),
        ],
        compiler_params=pltpu.CompilerParams(collective_id=0, has_side_effects=True),
    )(*pieces)


def half_by_x(values, axis):
    size = values.shape[axis] // 2
    return lax.dynamic_slice_in_dim(values, (lax.axis_index("dp") % 2) * size, size, axis)


def fetch_row(values, axis):
    first = swap(half_by_x(values, axis), "row")
    second = lax.ppermute(first, "dp", dp_pairs(0))
    return order_pair(lax.axis_index("dp") % 2 == 0, first, second, axis)


def silu_parts(values):
    sigma = jax.nn.sigmoid(values)
    return (values * sigma, sigma * (1.0 + values * (1.0 - sigma)))


def spread_tokens(own):
    near = swap(own, "col")
    far = swap(flip(own), "row")
    far_near = swap(far, "col")
    return jnp.stack([own, near, far, far_near])


def collect_tokens(parts):
    recv = swap(jnp.stack([parts[1], parts[3]]).astype(BF), "col").astype(F32)
    own = parts[0] + recv[0]
    far = parts[2] + recv[1]
    return own + swap(flip(far.astype(BF)), "row").astype(F32)


def to_sequence(values, r, c):
    other = lax.ppermute(values, ("row", "col"), [(1, 3), (2, 0)])
    pair = jnp.stack([values, other])
    copied = lax.ppermute(pair, ("row", "col"), [(0, 1), (3, 2)])
    return jnp.where(r == c, pair, copied)


def from_sequence(values, r, c):
    half = values.shape[1] // 2
    own, peer = values[:, :half], values[:, half:]
    diag = r == c
    send = jnp.where(diag, peer, own)
    kept = jnp.where(diag, own, peer)
    recv = swap(send, "col")
    whole = order_pair(c == 0, kept, recv, 0)
    moved = lax.ppermute(whole, ("row", "col"), [(1, 2), (2, 1)])
    return jnp.where(diag, whole, moved)


def local(
    layer_input,
    teacher,
    valid_mask,
    routes,
    segments,
    gain_attn,
    gain_ffn,
    w_qkv,
    w_out,
    w_router,
    w_shared_up,
    w_shared_down,
    w_expert_up,
    w_expert_down,
):
    r = lax.axis_index("row")
    c = lax.axis_index("col")
    n_dp = lax.axis_size("dp")
    rows = layer_input.shape[0]
    part = rows // 2
    half = layer_input.shape[1]
    heads = w_qkv.shape[2] // HEAD_DIM
    ff = w_shared_up.shape[2]
    quarter = ff // 2
    slots = E + 1

    x_pair = to_sequence(layer_input, r, c)
    x_seq = jnp.concatenate([x_pair[0], x_pair[1]], axis=1).astype(F32)
    w_qkv_full = jnp.concatenate([w_qkv, swap(w_qkv, "row")], axis=0)
    w_out_full = jnp.concatenate([w_out, swap(w_out, "row")], axis=1)
    gain_a = jnp.concatenate([gain_attn, swap(gain_attn, "row")])
    gain_f = jnp.concatenate([gain_ffn, swap(gain_ffn, "row")])
    w_r = jnp.concatenate([w_router, swap(w_router, "row")])
    t_pair = to_sequence(teacher, r, c)
    t_seq = jnp.concatenate([t_pair[0], t_pair[1]], axis=1)
    teacher_own = lax.dynamic_slice_in_dim(t_seq, c * part, part, 0).astype(F32)
    valid_other = swap(valid_mask, "col")
    valid_seq = jnp.where(r == c, valid_mask, valid_other).astype(F32)
    valid_own = lax.dynamic_slice_in_dim(valid_seq, c * part, part, 0)
    count = dp_sum(jnp.full((128,), jnp.sum(valid_own), F32))[0]
    seg = lax.dynamic_slice_in_dim(segments, r, 1, 0)[0]
    route_blocks = routes.reshape(2, 2, part, 2)
    route_blocks = jnp.where(r == 0, route_blocks, route_blocks[::-1])
    route_blocks = jnp.where(c == 0, route_blocks, route_blocks[:, ::-1]).reshape(4 * part, 2)
    picks = (route_blocks[:, :, None] == jnp.arange(E, dtype=jnp.int32)[None, None, :]).astype(F32)

    up_parts = [w_shared_up] + [w_expert_up[e] for e in range(E)]
    down_parts = [w_shared_down] + [w_expert_down[e] for e in range(E)]
    w_up, w_down = [], []
    for e in range(slots):
        keep = lax.dynamic_slice_in_dim(up_parts[e], r * quarter, quarter, 2)
        send = lax.dynamic_slice_in_dim(up_parts[e], (1 - r) * quarter, quarter, 2)
        w_up.append(
            jnp.concatenate([keep, fetch_row(send, 0)], axis=0).reshape(D, 2 * quarter)
        )
        keep = lax.dynamic_slice_in_dim(down_parts[e], r * quarter, quarter, 0)
        send = lax.dynamic_slice_in_dim(down_parts[e], (1 - r) * quarter, quarter, 0)
        w_down.append(jnp.concatenate([keep, fetch_row(send, 0)], axis=1))
    w_down = jnp.concatenate(w_down, axis=0)

    rstd_seq, normed = norm_forward(x_seq, gain_a)
    normed_attn = normed.astype(BF)
    qkv_pre = jnp.einsum("td,dke->kte", normed_attn, w_qkv_full, preferred_element_type=F32)
    tables = rope_tables(rows)
    seg_row, seg_col = seg[None, :], seg[:, None]
    queries, keys_rot, values_low, context_low = attend_forward(qkv_pre, tables, seg_row, seg_col)
    attention = jnp.dot(context_low, w_out_full, preferred_element_type=F32)
    att_halves = attention.reshape(2, part, D)
    att_keep = lax.dynamic_index_in_dim(att_halves, c, 0, keepdims=False)
    att_send = lax.dynamic_index_in_dim(att_halves, 1 - c, 0, keepdims=False)
    x_own = lax.dynamic_slice_in_dim(x_seq, c * part, part, 0)
    rstd_attn = lax.dynamic_slice_in_dim(rstd_seq, c * part, part, 0)
    hidden = x_own + att_keep + swap(att_send.astype(BF), "col").astype(F32)

    rstd_ffn, normed = norm_forward(hidden, gain_f)
    normed_low = normed.astype(BF)
    tokens = spread_tokens(normed_low).reshape(4 * part, D)
    logits = jnp.dot(tokens, w_r, preferred_element_type=F32)
    chosen = jnp.sum(picks * logits[:, None, :], axis=2)
    chosen = chosen - jnp.max(chosen, axis=1, keepdims=True)
    gates = jnp.exp(chosen)
    gates = gates / jnp.sum(gates, axis=1, keepdims=True)
    mixing = jnp.sum(picks * gates[:, :, None], axis=1)
    mix_all = jnp.concatenate([jnp.ones((4 * part, 1), F32), mixing], axis=1).T
    pre = [
        jnp.dot(tokens, w_up[e], preferred_element_type=F32).astype(BF)
        for e in range(slots)
    ]
    acts = []
    for e in range(slots):
        gate_pre, up_pre = pre[e][:, :quarter].astype(F32), pre[e][:, quarter:].astype(F32)
        act = gate_pre * jax.nn.sigmoid(gate_pre) * up_pre
        acts.append((act * mix_all[e][:, None]).astype(BF))
    act_all = jnp.concatenate(acts, axis=1)
    branch = jnp.dot(act_all, w_down, preferred_element_type=F32)
    output = hidden + collect_tokens(branch.reshape(4, part, D))

    error = output - teacher_own
    loss_part = jnp.sum(valid_own * jnp.sum(error * error, axis=1))
    total_tokens = part * 4 * n_dp
    grad_out = total_tokens / count * valid_own[:, None] * error

    grads = spread_tokens(grad_out.astype(BF)).reshape(4 * part, D)
    down_grad = jnp.dot(act_all.T, grads, preferred_element_type=F32).astype(BF)
    act_back = jnp.dot(
        grads, w_down.T, preferred_element_type=F32
    ).astype(BF)
    pre_grads = []
    gate_sums = []
    for e in range(slots):
        gate_pre, up_pre = pre[e][:, :quarter].astype(F32), pre[e][:, quarter:].astype(F32)
        back = act_back[:, e * quarter : (e + 1) * quarter].astype(F32)
        act_silu, slope = silu_parts(gate_pre)
        if e:
            gate_sums.append(jnp.sum(back * act_silu * up_pre, axis=1))
        back = back * mix_all[e][:, None]
        pre_grads.append(
            jnp.concatenate([back * up_pre * slope, back * act_silu], axis=1).astype(BF)
        )
    up_grads = [
        jnp.dot(tokens.T, pre_grads[e], preferred_element_type=F32).astype(BF)
        for e in range(slots)
    ]
    input_part = jnp.zeros((4 * part, D), F32)
    for e in range(slots):
        input_part = input_part + jnp.dot(
            pre_grads[e], w_up[e].T, preferred_element_type=F32
        )
    normed_ffn_grad = collect_tokens(input_part.reshape(4, part, D))
    gate_parts = jnp.stack(gate_sums, axis=0).reshape(E, 4, part)
    recv = swap(jnp.stack([gate_parts[:, 1], gate_parts[:, 3]]), "col")
    gate_grad = gate_parts[:, 0] + recv[0] + swap(gate_parts[:, 2] + recv[1], "row")
    mix_own = mixing[:part].T
    centre = jnp.sum(mix_own * gate_grad, axis=0, keepdims=True)
    logit_grad = (mix_own * (gate_grad - centre)).T.astype(BF)
    normed_ffn_grad = normed_ffn_grad + jnp.dot(logit_grad, w_r.T, preferred_element_type=F32)
    router_grad = jnp.dot(normed_low.T, logit_grad, preferred_element_type=F32)
    hidden_back, gain_ffn_grad = norm_backward(hidden, rstd_ffn, gain_f, normed_ffn_grad)
    hidden_grad = grad_out + hidden_back

    low_own = hidden_grad.astype(BF)
    low_seq = order_pair(c == 0, low_own, swap(low_own, "col"), 0)
    w_out_grad = jnp.dot(context_low.T, low_seq, preferred_element_type=F32).astype(BF)
    context_grad = jnp.dot(low_seq, w_out_full.T, preferred_element_type=F32)
    context_grad = context_grad.astype(BF)
    qkv_grad = jnp.concatenate(
        [
            attend_backward(
                queries, keys_rot, values_low, context_grad, tables, seg_row, seg_col, pair, 1
            )
            for pair in range(heads // 2)
        ],
        axis=2,
    )
    w_qkv_grad = jnp.einsum(
        "td,kte->dke", normed_attn, qkv_grad, preferred_element_type=F32
    ).astype(BF)
    back_part = jnp.einsum("kte,dke->td", qkv_grad, w_qkv_full, preferred_element_type=F32)
    back_halves = back_part.reshape(2, part, D)
    back_keep = lax.dynamic_index_in_dim(back_halves, c, 0, keepdims=False)
    back_send = lax.dynamic_index_in_dim(back_halves, 1 - c, 0, keepdims=False)
    normed_attn_grad = back_keep + swap(back_send.astype(BF), "col").astype(F32)
    input_back, gain_attn_grad = norm_backward(x_own, rstd_attn, gain_a, normed_attn_grad)
    input_grad = hidden_grad + input_back

    owner_f = quarter // n_dp
    owner_d = half // n_dp
    deep = n_dp // 2
    grad_pair = jnp.concatenate(
        [
            w_qkv_grad.reshape(2, n_dp, owner_d, 3, half),
            w_out_grad.reshape(n_dp, owner_d, 2, half).transpose(2, 0, 1, 3)[:, :, :, None],
        ],
        axis=3,
    ).transpose(0, 1, 3, 2, 4)
    up_pair, down_pair, attn_piece = dp_reduce(
        [grad.reshape(2, deep, 2, owner_d, 2 * quarter) for grad in up_grads],
        down_grad.reshape(slots, deep, 2, owner_f, D),
        grad_pair.reshape(2, deep, 2, 4 * owner_d, half),
    )
    attn_piece = attn_piece.reshape(4, owner_d, half)
    down_piece = jnp.where(r == 0, down_pair, down_pair[::-1]).swapaxes(0, 1)
    up_pair = up_pair.reshape(2, slots, owner_d, 2, quarter)
    up_piece = order_pair(r == 0, up_pair[0], up_pair[1], 3)

    plan = [(1, (), owner_d), (3, (0,), owner_f), (3, (1,), owner_f)]
    for e in range(E):
        plan += [(0, (e,), owner_d), (2, (e, 0), owner_f), (2, (e, 1), owner_f)]
    plan += [(4, (), 0)]
    up_full, shared_up_full, down_full, shared_down_full, attn_full = dp_gather(
        (up_piece[1:], up_piece[0], down_piece[1:], down_piece[0], attn_piece),
        (
            (E, half, 2, ff),
            (half, 2, ff),
            (E, 2, quarter, half),
            (2, quarter, half),
            (n_dp, 4, owner_d, half),
        ),
        tuple(plan),
    )
    attn_full = attn_full.swapaxes(0, 1).reshape(4, half, half).astype(F32)

    small = jnp.concatenate([gain_attn_grad[None], gain_ffn_grad[None], router_grad.T], axis=0)
    small = jnp.where(r == 0, small, flip(small))
    small = jnp.concatenate([small.reshape(-1), loss_part[None]])
    small = dp_sum(small)
    loss = small[-1] / (2.0 * count)
    small = small[:-1].reshape(E + 2, D)
    small = lax.dynamic_slice_in_dim(small, r * half, half, 1)
    return (
        from_sequence(output, r, c),
        loss,
        from_sequence(input_grad, r, c),
        small[0],
        small[1],
        attn_full[:3].swapaxes(0, 1),
        attn_full[3],
        small[2:].T,
        shared_up_full.astype(F32),
        shared_down_full.reshape(ff, half).astype(F32),
        up_full.astype(F32),
        down_full.reshape(E, ff, half).astype(F32),
    )


def solution(mesh):
    return jax.shard_map(
        local,
        mesh=mesh,
        in_specs=(
            P(("dp", "col"), "row"),
            P(("dp", "col"), "row"),
            P(("dp", "col")),
            P("dp", None),
            P("dp", None),
            P("row"),
            P("row"),
            P("row", None, "col"),
            P("col", "row"),
            P("row", None),
            P("row", None, "col"),
            P("col", "row"),
            P(None, "row", None, "col"),
            P(None, "col", "row"),
        ),
        out_specs=(
            P(("dp", "col"), "row"),
            P(),
            P(("dp", "col"), "row"),
            P("row"),
            P("row"),
            P("row", None, "col"),
            P("col", "row"),
            P("row", None),
            P("row", None, "col"),
            P("col", "row"),
            P(None, "row", None, "col"),
            P(None, "col", "row"),
        ),
        check_vma=False,
    )
```

```python
import functools

import jax
import jax.numpy as jnp
from jax import lax
from jax.experimental import pallas as pl
from jax.experimental.pallas import tpu as pltpu
from jax.sharding import PartitionSpec as P

D = 768
HEAD_DIM = 64
E = 4
LEN = 1024
ABLOCK = 256
BF = jnp.bfloat16
F32 = jnp.float32


def norm_backward(values, rstd_rows, gain_vec, incoming):
    scaled = incoming * gain_vec
    inner_sum = jnp.sum(scaled * values, axis=1)
    gain_grad = jnp.sum(incoming * values * rstd_rows[:, None], axis=0)
    result = rstd_rows[:, None] * scaled - values * (rstd_rows**3 * inner_sum / D)[:, None]
    return (result, gain_grad)


def rope_tables(length):
    half_dim = HEAD_DIM // 2
    freqs = 10000.0 ** (-jnp.arange(half_dim, dtype=F32) * 2.0 / HEAD_DIM)
    angles = jnp.arange(length, dtype=F32)[:, None] * freqs[None, :]
    sine = jnp.sin(angles)
    return (jnp.tile(jnp.cos(angles), (1, 4)), jnp.tile(jnp.concatenate([-sine, sine], axis=1), (1, 2)))


def lanes_of(shape):
    return lax.broadcasted_iota(jnp.int32, shape, len(shape) - 1)


def turn(values, first):
    half_dim = HEAD_DIM // 2
    return jnp.where(
        first,
        pltpu.roll(values, PAIR - half_dim, values.ndim - 1),
        pltpu.roll(values, half_dim, values.ndim - 1),
    )


PAIR = 2 * HEAD_DIM
NT = (((1,), (1,)), ((), ()))


def shares_of(key_pair, query_head, seg_col, seg_row):
    scores = lax.dot_general(key_pair, query_head, NT, preferred_element_type=F32)
    scores = jnp.where(seg_col == seg_row, scores, -1e30)
    weight = jnp.exp(scores - jnp.max(scores, axis=0, keepdims=True))
    return weight * (1.0 / jnp.sum(weight, axis=0, keepdims=True))


def front_kernel(
    n, x_in, w_qkv, w_out, vectors, shared_up, expert_up, shared_down, expert_down,
    cosine, sine, seg_row, seg_col,
    queries, keys, values, context, normed, x_own, hidden, w_qkv_peer, w_out_peer, vec_peer, up_own,
    tokens, up_peer, down_peer,
    x_pair, qkv_own, out_own, up_raw, part_raw, up_part, pre, att_send, att_recv, low, low_flip,
    own_sem, x_send, x_recv, w_send, w_recv, t_send, t_recv,
):
    me = lax.axis_index("dp")
    row, col = lax.axis_index("row"), lax.axis_index("col")
    z, x = me // 2, me % 2
    low_z = lax.rem(z, 2)
    x_peer = {"dp": 2 * z + (1 - x)}
    z_peer = {"dp": 2 * (z + 1 - 2 * low_z) + x}
    row_peer, core = {"row": 1 - row}, {"col": 1 - col}
    mine = 2 * low_z + x
    of_x, of_z = 2 * low_z + (1 - x), 2 * (1 - low_z) + x
    rows, half = x_in.shape
    part = rows // 2
    quarter = shared_up.shape[2] // 2
    slots = expert_up.shape[0] + 1
    greet([row_peer, core, x_peer, z_peer])

    def split(index, size):
        return pl.ds(pl.multiple_of(index * size, 16), size)

    def source(item, index):
        if item == 0:
            return w_qkv.at[:, split(index, half // 4)]
        if item == 1:
            return w_out.at[split(index, w_out.shape[0] // 4)]
        slot, kind = (item - 2) // 2, (item - 2) % 2
        if kind == 0:
            return up_part.at[slot]
        ref = shared_down if slot == 0 else expert_down.at[slot - 1]
        first = (1 - row) * quarter + index * (quarter // 4)
        return ref.at[pl.ds(pl.multiple_of(first, 16), quarter // 4)]

    def landing(item, index):
        if item == 0:
            return w_qkv_peer.at[:, split(index, half // 4)]
        if item == 1:
            return w_out_peer.at[split(index, w_out.shape[0] // 4)]
        slot, kind = (item - 2) // 2, (item - 2) % 2
        if kind == 0:
            return up_peer.at[slot, split(index, half // 4)]
        return down_peer.at[slot, split(index, quarter // 4)]

    count = 2 + 2 * slots
    copies = {}

    def start(item, leg, src, device, index):
        copy = remote(
            src, landing(item, index), w_send.at[item, leg], w_recv.at[item, leg], device
        )
        copy.start()
        copies[item, leg] = copy

    def fetch(item):
        start(item, 0, source(item, mine), row_peer, mine)

    def pass_on(item):
        copies[item, 0].wait_recv()
        start(item, 1, landing(item, mine), x_peer, mine)
        start(item, 2, landing(item, mine), z_peer, mine)

    def by_x(item):
        return (item - item // 4) % 2 == 0

    def pass_far(item):
        if by_x(item):
            copies[item, 1].wait_recv()
            start(item, 3, landing(item, of_x), z_peer, of_x)
        else:
            copies[item, 2].wait_recv()
            start(item, 3, landing(item, of_z), x_peer, of_z)

    def arrive(item):
        copies[item, 2 if by_x(item) else 1].wait_recv()
        copies[item, 3].wait_recv()

    progress = [0]

    def pump():
        at = progress[0]
        progress[0] += 1
        if 2 <= at - 1 < count:
            pass_far(at - 1)
        if 2 <= at < count:
            pass_on(at)

    diagonal = row == col
    over_row = remote(x_in, x_pair.at[1], x_send.at[0], x_recv.at[0], row_peer)
    across_own = remote(x_in, x_pair.at[0], x_send.at[1], x_recv.at[1], core)
    across_peer = remote(x_pair.at[1], x_pair.at[1], x_send.at[2], x_recv.at[2], core)
    own_x = pltpu.make_async_copy(x_in, x_pair.at[0], own_sem.at[0])

    @pl.when(diagonal)
    def _():
        own_x.start()
        across_own.start()

    @pl.when(jnp.logical_not(diagonal))
    def _():
        over_row.start()

    def up_slot(slot):
        return shared_up if slot == 0 else expert_up.at[slot - 1]

    keep_lanes = pl.ds(pl.multiple_of(row * quarter, 128), quarter)
    send_lanes = pl.ds(pl.multiple_of((1 - row) * quarter, 128), quarter)
    part_loads, up_loads = [], []
    for slot in range(slots):
        piece = up_slot(slot).at[pl.ds(mine * (half // 4), half // 4), :, send_lanes]
        part_loads.append(pltpu.make_async_copy(piece, part_raw.at[slot], own_sem.at[4 + slot]))
        part_loads[slot].start()

    def split_own(slot):
        up_loads[slot].wait()
        for k in range(2):
            up_own[slot, :, k * quarter : (k + 1) * quarter] = up_raw[slot, :, k]

    give_vectors = remote(vectors, vec_peer, x_send.at[3], x_recv.at[3], row_peer)
    give_vectors.start()
    fetch(0)
    fetch(1)
    own_qkv = pltpu.make_async_copy(w_qkv, qkv_own, own_sem.at[1])
    own_qkv.start()
    own_out = pltpu.make_async_copy(w_out, out_own, own_sem.at[2])
    own_out.start()

    for slot in range(slots):
        piece = up_slot(slot).at[:, :, keep_lanes]
        up_loads.append(
            pltpu.make_async_copy(piece, up_raw.at[slot], own_sem.at[4 + slots + slot])
        )
        up_loads[slot].start()
    for slot in range(slots):
        part_loads[slot].wait()
        for k in range(2):
            up_part[slot, :, k * quarter : (k + 1) * quarter] = part_raw[slot, :, k]

    @pl.when(diagonal)
    def _():
        over_row.wait_recv()
        across_peer.start()
        own_x.wait()

    @pl.when(jnp.logical_not(diagonal))
    def _():
        over_row.wait_send()

    for item in range(2, count):
        fetch(item)
    pass_on(0)
    pass_on(1)
    split_own(0)

    @pl.when(jnp.logical_not(diagonal))
    def _():
        across_own.wait_recv()
        across_peer.wait_recv()

    give_vectors.wait_recv()
    progress[0] = 2
    x_first, x_second = x_pair[0].astype(F32), x_pair[1].astype(F32)
    squares = jnp.sum(x_first * x_first, axis=1, keepdims=True)
    squares = squares + jnp.sum(x_second * x_second, axis=1, keepdims=True)
    rstd = lax.rsqrt(squares / (2 * half) + 1e-06)
    normed[0] = (x_first * rstd * vectors[0:1]).astype(BF)
    normed[1] = (x_second * rstd * vec_peer[0:1]).astype(BF)
    pass_far(0)
    pass_far(1)
    for slot in range(1, slots):
        split_own(slot)
    arrive(0)
    own_qkv.wait()
    for j in range(3):
        pre[j] = jnp.dot(normed[0], qkv_own[j], preferred_element_type=F32) + jnp.dot(
            normed[1], w_qkv_peer[j], preferred_element_type=F32
        )
        pump()

    first = lanes_of((rows, PAIR)) % HEAD_DIM < HEAD_DIM // 2
    lower = lanes_of((ABLOCK, PAIR)) < HEAD_DIM
    cos, sin = cosine[...], sine[...]
    for pair in range(half // PAIR):
        lanes = slice(pair * PAIR, (pair + 1) * PAIR)
        query = pre[0, :, lanes]
        queries[:, lanes] = ((query * cos + turn(query, first) * sin) * HEAD_DIM**-0.5).astype(BF)
        key = pre[1, :, lanes]
        keys[:, lanes] = (key * cos + turn(key, first) * sin).astype(BF)
        value = pre[2, :, lanes]
        values[:, lanes] = value.astype(BF)
        value_t = value.T.astype(BF)
        for block in range(rows // ABLOCK):
            begin, stop = block * ABLOCK, (block + 1) * ABLOCK
            query = queries[begin:stop, lanes]
            parts = []
            for head in range(2):
                query_head = jnp.where(lower == (head == 0), query, jnp.zeros_like(query))
                shares = shares_of(
                    keys[:stop, lanes], query_head, seg_col[:stop], seg_row[:, begin:stop]
                ).astype(BF)
                parts.append(jnp.dot(value_t[:, :stop], shares, preferred_element_type=F32))
            both = jnp.concatenate([parts[0][:HEAD_DIM], parts[1][HEAD_DIM:]], axis=0)
            context[begin:stop, lanes] = both.T.astype(BF)
            if block % 2 == 1:
                pump()

    arrive(1)
    own_out.wait()
    there, here = split(1 - col, part), split(col, part)
    for at, weight in enumerate((out_own, w_out_peer)):
        att_send[:, at * half : (at + 1) * half] = jnp.dot(
            context[there], weight[...], preferred_element_type=F32
        ).astype(BF)
    swap_att = remote(att_send, att_recv, t_send.at[0], t_recv.at[0], core)
    swap_att.start()
    pump()
    for at, weight in enumerate((out_own, w_out_peer)):
        lanes = slice(at * half, (at + 1) * half)
        x_own[at] = x_pair[at, here]
        hidden[:, lanes] = x_own[at].astype(F32) + jnp.dot(
            context[here], weight[...], preferred_element_type=F32
        )
    swap_att.wait_recv()
    total = hidden[...] + att_recv[...].astype(F32)
    hidden[...] = total
    rstd = lax.rsqrt(jnp.mean(total * total, axis=1, keepdims=True) + 1e-06)
    gains = jnp.concatenate([vectors[1:2], vec_peer[1:2]], axis=1)
    total = (total * rstd * gains).astype(BF)
    low[...] = total
    low_flip[:, :half] = total[:, half:]
    low_flip[:, half:] = total[:, :half]
    own_tokens = pltpu.make_async_copy(low, tokens.at[0], own_sem.at[3])
    own_tokens.start()
    far = remote(low_flip, tokens.at[2], t_send.at[1], t_recv.at[1], row_peer)
    far.start()
    near = remote(low, tokens.at[1], t_send.at[2], t_recv.at[2], core)
    near.start()
    while progress[0] <= count:
        pump()
    far.wait_recv()
    far_near = remote(tokens.at[2], tokens.at[3], t_send.at[3], t_recv.at[3], core)
    far_near.start()
    for item in range(2, count):
        arrive(item)
    near.wait_recv()
    far_near.wait_recv()
    own_tokens.wait()
    for copy in (give_vectors, swap_att, far, near, far_near, *copies.values()):
        copy.wait_send()

    @pl.when(diagonal)
    def _():
        across_own.wait_send()
        across_peer.wait_send()


def front(x_in, w_qkv, w_out, vectors, shared_up, expert_up, shared_down, expert_down, tables, seg):
    n = lax.axis_size("dp")
    rows, half = x_in.shape
    quarter = shared_up.shape[2] // 2
    slots = expert_up.shape[0] + 1
    count = 2 + 2 * slots
    sems = pltpu.SemaphoreType.DMA
    any_spec = pl.BlockSpec(memory_space=pl.ANY)
    vmem_spec = pl.BlockSpec(memory_space=pltpu.VMEM)
    shape = jax.ShapeDtypeStruct
    wide = w_out.shape[0]
    return pl.pallas_call(
        functools.partial(front_kernel, n),
        out_shape=[shape((rows, wide), BF)] * 4
        + [
            shape((2, rows, half), BF),
            shape((2, rows // 2, half), BF),
            shape((rows // 2, 2 * half), F32),
            shape(w_qkv.shape, BF),
            shape(w_out.shape, BF),
            shape(vectors.shape, F32),
            shape((slots, half, 2 * quarter), BF),
            shape((4, rows // 2, 2 * half), BF),
            shape((slots, half, 2 * quarter), BF),
            shape((slots, quarter, half), BF),
        ],
        in_specs=[any_spec] * 3 + [vmem_spec] + [any_spec] * 4 + [vmem_spec] * 4,
        out_specs=[vmem_spec] * 11 + [any_spec] * 3,
        scratch_shapes=[
            pltpu.VMEM((2, rows, half), BF),
            pltpu.VMEM(w_qkv.shape, BF),
            pltpu.VMEM(w_out.shape, BF),
            pltpu.VMEM((slots, half, 2, quarter), BF),
            pltpu.VMEM((slots, half // 4, 2, quarter), BF),
            pltpu.VMEM((slots, half // 4, 2 * quarter), BF),
            pltpu.VMEM((3, rows, wide), F32),
            pltpu.VMEM((rows // 2, 2 * half), BF),
            pltpu.VMEM((rows // 2, 2 * half), BF),
            pltpu.VMEM((rows // 2, 2 * half), BF),
            pltpu.VMEM((rows // 2, 2 * half), BF),
            sems((4 + 2 * slots,)),
            sems((4,)),
            sems((4,)),
            sems((count, 4)),
            sems((count, 4)),
            sems((4,)),
            sems((4,)),
        ],
        compiler_params=pltpu.CompilerParams(
            collective_id=2, has_side_effects=True, vmem_limit_bytes=48 << 20
        ),
    )(
        x_in, w_qkv, w_out, vectors, shared_up, expert_up, shared_down, expert_down,
        tables[0], tables[1], seg[None, :], seg[:, None],
    )


def attend_back_kernel(
    queries, keys, values, context_grad, cosine, sine, seg_row, seg_col, out, key_sum, value_sum
):
    rows = queries.shape[0]
    key_t = keys[...].astype(F32).T.astype(BF)
    lower = lanes_of((ABLOCK, PAIR)) < HEAD_DIM
    first = lanes_of((ABLOCK, PAIR)) % HEAD_DIM < HEAD_DIM // 2
    for block in reversed(range(rows // ABLOCK)):
        start, stop = block * ABLOCK, (block + 1) * ABLOCK
        query, incoming = queries[start:stop], context_grad[start:stop]
        parts, key_part, value_part = [], None, None
        for head in range(2):
            mine = lower == (head == 0)
            query_head = jnp.where(mine, query, jnp.zeros_like(query))
            incoming_head = jnp.where(mine, incoming, jnp.zeros_like(incoming))
            shares = shares_of(keys[:stop], query_head, seg_col[:stop], seg_row[:, start:stop])
            share_grad = lax.dot_general(
                values[:stop], incoming_head, NT, preferred_element_type=F32
            )
            centre = jnp.sum(shares * share_grad, axis=0, keepdims=True)
            score_grad = (shares * (share_grad - centre)).astype(BF)
            parts.append(jnp.dot(key_t[:, :stop], score_grad, preferred_element_type=F32))
            more = jnp.dot(shares.astype(BF), incoming_head, preferred_element_type=F32)
            value_part = more if head == 0 else value_part + more
            more = jnp.dot(score_grad, query_head, preferred_element_type=F32)
            key_part = more if head == 0 else key_part + more
        both = jnp.concatenate([parts[0][:HEAD_DIM], parts[1][HEAD_DIM:]], axis=0)
        grad = both.T * HEAD_DIM**-0.5
        cos, sin = cosine[start:stop], sine[start:stop]
        out[0, start:stop] = (grad * cos + turn(grad * sin, first)).astype(BF)
        if stop == rows:
            key_sum[...] = key_part
            value_sum[...] = value_part
        else:
            key_sum[:stop] += key_part
            value_sum[:stop] += value_part
    for block in range(rows // ABLOCK):
        start, stop = block * ABLOCK, (block + 1) * ABLOCK
        grad = key_sum[start:stop]
        cos, sin = cosine[start:stop], sine[start:stop]
        out[1, start:stop] = (grad * cos + turn(grad * sin, first)).astype(BF)
        out[2, start:stop] = value_sum[start:stop].astype(BF)


def attend_backward(queries, keys, values, context_grad, tables, seg_row, seg_col, first_pair, pairs):
    rows = queries.shape[0]
    block = pl.BlockSpec((rows, PAIR), lambda i: (0, i + first_pair))
    whole = pl.BlockSpec((rows, PAIR), lambda i: (0, 0))
    return pl.pallas_call(
        attend_back_kernel,
        grid=(pairs,),
        out_shape=jax.ShapeDtypeStruct((3, rows, pairs * PAIR), BF),
        in_specs=[block] * 4
        + [
            whole,
            whole,
            pl.BlockSpec((1, rows), lambda i: (0, 0)),
            pl.BlockSpec((rows, 1), lambda i: (0, 0)),
        ],
        out_specs=pl.BlockSpec((3, rows, PAIR), lambda i: (0, 0, i)),
        scratch_shapes=[pltpu.VMEM((rows, PAIR), F32), pltpu.VMEM((rows, PAIR), F32)],
        compiler_params=pltpu.CompilerParams(vmem_limit_bytes=40 << 20),
        cost_estimate=pl.CostEstimate(
            flops=pairs * 14_000_000_000, bytes_accessed=4 << 20, transcendentals=2 << 20
        ),
    )(queries, keys, values, context_grad, tables[0], tables[1], seg_row, seg_col)


def swap(values, axis):
    return lax.ppermute(values, axis, [(0, 1), (1, 0)])


def flip(values):
    half = values.shape[-1] // 2
    return jnp.concatenate([values[..., half:], values[..., :half]], axis=-1)


def dp_pairs(bit):
    n = lax.axis_size("dp")
    return [(i, i ^ (1 << bit)) for i in range(n)]


def dp_sum(values):
    for bit in range(lax.axis_size("dp").bit_length() - 1):
        values = values + lax.ppermute(values, "dp", dp_pairs(bit))
    values = values + swap(values, "row")
    return values + swap(values, "col")


def remote(src, dst, send, recv, device):
    return pltpu.make_async_remote_copy(
        src_ref=src,
        dst_ref=dst,
        send_sem=send,
        recv_sem=recv,
        device_id=device,
        device_id_type=pl.DeviceIdType.MESH,
    )


def greet(devices):
    barrier = pltpu.get_barrier_semaphore()
    for device in devices:
        pl.semaphore_signal(
            barrier, inc=1, device_id=device, device_id_type=pl.DeviceIdType.MESH
        )
    pl.semaphore_wait(barrier, len(devices))


AHEAD = 3
BEHIND = 3


def reduce_kernel(n, slots, *refs):
    ups, down, attn, up_out, down_out, attn_out = refs[:6]
    (
        up_keep, down_keep, attn_keep, up_x, down_x, attn_x, up_z, down_z, attn_z,
        up_done, down_done, attn_done, attn_y,
        keep_sem, x_send, x_recv, z_send, z_recv, out_sem, y_send, y_recv,
    ) = refs[6:]
    me = lax.axis_index("dp")
    row = lax.axis_index("row")
    deep = n // 2
    z, x = me // 2, me % 2
    partner = {"dp": 2 * z + (1 - x)}
    peer = {"row": 1 - row}
    ahead = [lax.rem(z + k, deep) for k in range(deep)]
    greet([partner, peer] + [{"dp": 2 * ahead[k] + x} for k in range(1, deep)])

    items = [("down", e) for e in range(slots)]
    items += [("up", 2 * e + h) for e in range(slots) for h in (1, 0)]
    items += [("attn", 0)]
    count = len(items)
    last = count - 1

    def buffers(item):
        kind, at = items[item]
        if kind == "down":
            return down.at[at], down_keep.at[at], down_x.at[at], down_z.at[at], down_done.at[at]
        if kind == "up":
            return ups.at[at // 2, at % 2], up_keep.at[at], up_x.at[at], up_z.at[at], up_done.at[at]
        return None, attn_keep.at[:, x], attn_x, attn_z, attn_done

    y_first = remote(attn.at[1], attn_y, y_send.at[last], y_recv.at[last], peer)
    y_first.start()
    attn_load = pltpu.make_async_copy(attn.at[0], attn_keep, keep_sem.at[last])
    attn_load.start()
    loads, x_copies, z_copies, outs, y_copies = {}, {}, {}, [], [y_first]
    for item in range(last):
        source, keep, _, _, _ = buffers(item)
        loads[item] = pltpu.make_async_copy(source.at[:, x], keep, keep_sem.at[item])
        loads[item].start()

    def send_x(item):
        source, keep, landing, _, _ = buffers(item)
        if item == last:
            attn_load.wait()
            y_first.wait_recv()
            attn_keep[...] = (attn_keep[...].astype(F32) + attn_y[...].astype(F32)).astype(BF)
            given = attn_keep.at[:, 1 - x]
        else:
            given = source.at[:, 1 - x]
        x_copies[item] = remote(given, landing, x_send.at[item], x_recv.at[item], partner)
        x_copies[item].start()

    def send_z(item):
        _, keep, landing, arrivals, _ = buffers(item)
        if item in loads:
            loads[item].wait()
        x_copies[item].wait_recv()
        keep[...] = (keep[...].astype(F32) + landing[...].astype(F32)).astype(BF)
        for k in range(1, deep):
            copy = remote(
                keep.at[ahead[k]],
                arrivals.at[k - 1],
                z_send.at[item, k],
                z_recv.at[item, k],
                {"dp": 2 * ahead[k] + x},
            )
            copy.start()
            z_copies[item, k] = copy

    def finish(item):
        kind, at = items[item]
        _, keep, _, arrivals, done = buffers(item)
        total = keep[z].astype(F32)
        for k in range(1, deep):
            z_copies[item, k].wait_recv()
            total = total + arrivals[k - 1].astype(F32)
        done[...] = total.astype(BF)
        half = down.shape[4] // 2

        def keep_own(source, target):
            copy = pltpu.make_async_copy(source, target, out_sem.at[item])
            copy.start()
            outs.append(copy)

        def give_peer(source, target):
            copy = remote(source, target, y_send.at[item], y_recv.at[item], peer)
            copy.start()
            y_copies.append(copy)

        if kind == "down":
            keep_own(done.at[:, :half], down_out.at[0, at])
            give_peer(done.at[:, half:], down_out.at[1, at])
        elif kind == "attn":
            keep_own(done, attn_out)
        elif at % 2 == 0:
            keep_own(done, up_out.at[0, at // 2])
        else:
            give_peer(done, up_out.at[1, at // 2])

    for step in range(count + AHEAD + BEHIND):
        if step < count:
            send_x(step)
        if 0 <= step - AHEAD < count:
            send_z(step - AHEAD)
        if 0 <= step - AHEAD - BEHIND < count:
            finish(step - AHEAD - BEHIND)
    for copy in outs:
        copy.wait()
    y_first.wait_send()
    for copy in y_copies[1:]:
        copy.wait()
    for copy in list(x_copies.values()) + list(z_copies.values()):
        copy.wait_send()


def dp_reduce(up_grads, down_grad, attn_grad):
    n = lax.axis_size("dp")
    deep = n // 2
    slots = up_grads.shape[0]
    up_tail, down_tail, attn_tail = up_grads.shape[4:], down_grad.shape[3:], attn_grad.shape[3:]
    sems = pltpu.SemaphoreType.DMA
    count = 3 * slots + 1
    vmem = lambda *shape: pltpu.VMEM(shape, BF)
    half = down_tail[1] // 2
    any_spec = pl.BlockSpec(memory_space=pl.ANY)
    return pl.pallas_call(
        functools.partial(reduce_kernel, n, slots),
        out_shape=[
            jax.ShapeDtypeStruct((2, slots) + up_tail, BF),
            jax.ShapeDtypeStruct((2, slots, down_tail[0], half), BF),
            jax.ShapeDtypeStruct(attn_tail, BF),
        ],
        in_specs=[any_spec] * 3,
        out_specs=[any_spec] * 3,
        scratch_shapes=[
            vmem(2 * slots, deep, *up_tail),
            vmem(slots, deep, *down_tail),
            vmem(deep, 2, *attn_tail),
            vmem(2 * slots, deep, *up_tail),
            vmem(slots, deep, *down_tail),
            vmem(deep, *attn_tail),
            vmem(2 * slots, deep - 1, *up_tail),
            vmem(slots, deep - 1, *down_tail),
            vmem(deep - 1, *attn_tail),
            vmem(2 * slots, *up_tail),
            vmem(slots, *down_tail),
            vmem(*attn_tail),
            vmem(deep, 2, *attn_tail),
            sems((count,)),
            sems((count,)),
            sems((count,)),
            sems((count, deep)),
            sems((count, deep)),
            sems((count,)),
            sems((count,)),
            sems((count,)),
        ],
        compiler_params=pltpu.CompilerParams(
            collective_id=1, has_side_effects=True, vmem_limit_bytes=48 << 20
        ),
    )(up_grads, down_grad, attn_grad)


def order_pair(first_is_own, own, other, axis):
    return jnp.where(
        first_is_own, jnp.concatenate([own, other], axis), jnp.concatenate([other, own], axis)
    )


WINDOW = 2


def gather_kernel(n, plan, *refs):
    count = max(item[0] for item in plan) + 1
    pieces, fulls = refs[:count], refs[count : 2 * count]
    own_sem, z_send, z_recv, x_send, x_recv = refs[2 * count :]
    me = lax.axis_index("dp")
    deep = n // 2
    z, x = me // 2, me % 2
    partner = 2 * z + (1 - x)
    peers = [2 * lax.rem(z + k, deep) + x for k in range(1, deep)]
    sources = [2 * lax.rem(z + deep - k, deep) + x for k in range(deep)]

    greet([{"dp": device} for device in peers + [partner]])

    def region(item, owner):
        at, lead, rows = plan[item]
        full = fulls[at]
        for index in lead:
            full = full.at[index]
        if rows == 0:
            return full.at[owner]
        start = owner * rows
        if rows % 16 == 0:
            start = pl.multiple_of(start, 16)
        return full.at[pl.ds(start, rows)]

    def piece(item):
        at, lead, rows = plan[item]
        ref = pieces[at]
        for index in lead:
            ref = ref.at[index]
        return ref

    total = len(plan)
    local_copies = []
    z_copies = [[] for _ in range(total)]
    x_copies = [[] for _ in range(total)]
    for step in range(total + WINDOW):
        if step < total:
            here = region(step, me)
            for k in range(1, deep):
                copy = remote(
                    piece(step), here, z_send.at[step, k], z_recv.at[step, k], {"dp": peers[k - 1]}
                )
                copy.start()
                z_copies[step].append(copy)
            copy = remote(piece(step), here, x_send.at[step, 0], x_recv.at[step, 0], {"dp": partner})
            copy.start()
            x_copies[step].append(copy)
            copy = pltpu.make_async_copy(piece(step), here, own_sem.at[step])
            copy.start()
            local_copies.append(copy)
        if step >= WINDOW:
            item = step - WINDOW
            for k in range(1, deep):
                z_copies[item][k - 1].wait_recv()
                arrived = region(item, sources[k])
                copy = remote(
                    arrived, arrived, x_send.at[item, k], x_recv.at[item, k], {"dp": partner}
                )
                copy.start()
                x_copies[item].append(copy)
    for item in range(total):
        local_copies[item].wait()
        for copy in z_copies[item]:
            copy.wait_send()
        for copy in x_copies[item]:
            copy.wait()


def dp_gather(pieces, fulls, plan):
    n = lax.axis_size("dp")
    total = len(plan)
    sems = pltpu.SemaphoreType.DMA
    return pl.pallas_call(
        functools.partial(gather_kernel, n, plan),
        out_shape=[jax.ShapeDtypeStruct(shape, BF) for shape in fulls],
        in_specs=[pl.BlockSpec(memory_space=pl.ANY)] * len(pieces),
        out_specs=[pl.BlockSpec(memory_space=pl.ANY)] * len(fulls),
        scratch_shapes=[
            sems((total,)),
            sems((total, n // 2)),
            sems((total, n // 2)),
            sems((total, n // 2)),
            sems((total, n // 2)),
        ],
        compiler_params=pltpu.CompilerParams(collective_id=0, has_side_effects=True),
    )(*pieces)


TN = (((0,), (0,)), ((), ()))
TILE = 512


def column(values, index):
    return jnp.sum(jnp.where(lanes_of(values.shape) == index, values, 0.0), axis=1, keepdims=True)


def ffn_kernel(tokens, up_own, up_peer, down_own, down_peer, mix, pre, act, out):
    slot = pl.program_id(0)
    quarter = down_own.shape[1]
    w_up = jnp.concatenate([up_own[0], up_peer[0]], axis=0)
    w_down = jnp.concatenate([down_own[0], down_peer[0]], axis=1)
    for tile in range(tokens.shape[0] // TILE):
        rows = pl.ds(tile * TILE, TILE)
        both = jnp.dot(tokens[rows], w_up, preferred_element_type=F32)
        pre[0, rows] = both.astype(BF)
        gate, up = both[:, :quarter], both[:, quarter:]
        hidden = gate / (1.0 + jnp.exp(-gate)) * up * column(mix[rows], slot)
        act[0, rows] = hidden.astype(BF)
        part = jnp.dot(hidden.astype(BF), w_down, preferred_element_type=F32)

        @pl.when(slot == 0)
        def _():
            out[rows] = part

        @pl.when(slot > 0)
        def _():
            out[rows] += part


def ffn_forward(tokens, up_own, up_peer, down_own, down_peer, mix):
    slots, half, width = up_own.shape
    rows, depth = tokens.shape
    per_slot = lambda *shape: pl.BlockSpec((1,) + shape, lambda e: (e, 0, 0))
    whole = lambda *shape: pl.BlockSpec(shape, lambda e: (0, 0))
    return pl.pallas_call(
        ffn_kernel,
        grid=(slots,),
        out_shape=[
            jax.ShapeDtypeStruct((slots, rows, width), BF),
            jax.ShapeDtypeStruct((slots, rows, width // 2), BF),
            jax.ShapeDtypeStruct((rows, depth), F32),
        ],
        in_specs=[
            whole(rows, depth),
            per_slot(half, width),
            per_slot(half, width),
            per_slot(width // 2, half),
            per_slot(width // 2, half),
            whole(rows, 8),
        ],
        out_specs=[per_slot(rows, width), per_slot(rows, width // 2), whole(rows, depth)],
        compiler_params=pltpu.CompilerParams(vmem_limit_bytes=56 << 20),
        cost_estimate=pl.CostEstimate(
            flops=3 * slots * rows * depth * width,
            bytes_accessed=40 << 20,
            transcendentals=slots * rows * width // 2,
        ),
    )(tokens, up_own, up_peer, down_own, down_peer, mix)


def ffn_back_kernel(
    grads, tokens, pre, act, down_own, down_peer, mix, down_grad, up_grad, pre_grad, gate_sum
):
    slot = pl.program_id(0)
    quarter = down_own.shape[1]
    w_down = jnp.concatenate([down_own[0], down_peer[0]], axis=1)
    depth = tokens.shape[1]
    for tile in range(tokens.shape[0] // TILE):
        rows = pl.ds(tile * TILE, TILE)
        back = lax.dot_general(grads[rows], w_down, NT, preferred_element_type=F32)
        gate = pre[0, rows, :quarter].astype(F32)
        up = pre[0, rows, quarter:].astype(F32)
        sigma = 1.0 / (1.0 + jnp.exp(-gate))
        act_silu = gate * sigma
        sums = jnp.sum(back * act_silu * up, axis=1, keepdims=True)
        mine = lanes_of((TILE, 8)) == slot

        @pl.when(slot == 0)
        def _():
            gate_sum[rows] = jnp.zeros((TILE, 8), F32)

        gate_sum[rows] += jnp.where(mine, sums, 0.0)
        back = back * column(mix[rows], slot)
        pre_grad[0, rows, :quarter] = (back * up * (sigma * (1.0 + gate * (1.0 - sigma)))).astype(BF)
        pre_grad[0, rows, quarter:] = (back * act_silu).astype(BF)
    down_grad[0] = lax.dot_general(act[0], grads[...], TN, preferred_element_type=F32).astype(BF)
    for tile in range(depth // 256):
        columns = slice(tile * 256, (tile + 1) * 256)
        up_grad[0, columns] = lax.dot_general(
            tokens[:, columns], pre_grad[0], TN, preferred_element_type=F32
        ).astype(BF)


def ffn_backward(grads, tokens, pre, act, down_own, down_peer, mix):
    slots, rows, width = pre.shape
    depth = tokens.shape[1]
    per_slot = lambda *shape: pl.BlockSpec((1,) + shape, lambda e: (e, 0, 0))
    whole = lambda *shape: pl.BlockSpec(shape, lambda e: (0, 0), pipeline_mode=pl.Buffered(1))
    return pl.pallas_call(
        ffn_back_kernel,
        grid=(slots,),
        out_shape=[
            jax.ShapeDtypeStruct((slots, width // 2, depth), BF),
            jax.ShapeDtypeStruct((slots, depth, width), BF),
            jax.ShapeDtypeStruct((slots, rows, width), BF),
            jax.ShapeDtypeStruct((rows, 8), F32),
        ],
        in_specs=[
            whole(rows, depth),
            whole(rows, depth),
            per_slot(rows, width),
            per_slot(rows, width // 2),
            per_slot(width // 2, depth // 2),
            per_slot(width // 2, depth // 2),
            whole(rows, 8),
        ],
        out_specs=[
            per_slot(width // 2, depth),
            per_slot(depth, width),
            per_slot(rows, width),
            pl.BlockSpec((rows, 8), lambda e: (0, 0)),
        ],
        compiler_params=pltpu.CompilerParams(vmem_limit_bytes=58 << 20),
        cost_estimate=pl.CostEstimate(
            flops=4 * slots * rows * depth * width,
            bytes_accessed=70 << 20,
            transcendentals=slots * rows * width // 2,
        ),
    )(grads, tokens, pre, act, down_own, down_peer, mix)


def ffn_input_kernel(pre_grad, up_own, up_peer, out):
    slot = pl.program_id(0)
    w_up = jnp.concatenate([up_own[0], up_peer[0]], axis=0)
    for tile in range(out.shape[0] // TILE):
        rows = pl.ds(tile * TILE, TILE)
        part = lax.dot_general(pre_grad[0, rows], w_up, NT, preferred_element_type=F32)

        @pl.when(slot == 0)
        def _():
            out[rows] = part

        @pl.when(slot > 0)
        def _():
            out[rows] += part


def ffn_input(pre_grad, up_own, up_peer, part, parts):
    slots, rows, width = pre_grad.shape
    half = up_own.shape[1]
    depth = 2 * half
    rows = rows // parts
    return pl.pallas_call(
        ffn_input_kernel,
        grid=(slots,),
        out_shape=jax.ShapeDtypeStruct((rows, depth), F32),
        in_specs=[
            pl.BlockSpec((1, rows, width), lambda e: (e, part, 0)),
            pl.BlockSpec((1, half, width), lambda e: (e, 0, 0)),
            pl.BlockSpec((1, half, width), lambda e: (e, 0, 0)),
        ],
        out_specs=pl.BlockSpec((rows, depth), lambda e: (0, 0)),
        compiler_params=pltpu.CompilerParams(vmem_limit_bytes=40 << 20),
        cost_estimate=pl.CostEstimate(
            flops=2 * slots * rows * depth * width, bytes_accessed=20 << 20, transcendentals=0
        ),
    )(pre_grad, up_own, up_peer)


def spread_tokens(own):
    near = swap(own, "col")
    far = swap(flip(own), "row")
    far_near = swap(far, "col")
    return jnp.stack([own, near, far, far_near])


def collect_tokens(parts):
    far = parts[2] + swap(parts[3].astype(BF), "col").astype(F32)
    far = swap(flip(far.astype(BF)), "row").astype(F32)
    own = parts[0] + swap(parts[1].astype(BF), "col").astype(F32)
    return own + far


def to_sequence(values, r, c):
    other = lax.ppermute(values, ("row", "col"), [(1, 3), (2, 0)])
    pair = jnp.stack([values, other])
    copied = lax.ppermute(pair, ("row", "col"), [(0, 1), (3, 2)])
    return jnp.where(r == c, pair, copied)


def from_sequence(values, r, c):
    half = values.shape[1] // 2
    own, peer = values[:, :half], values[:, half:]
    diag = r == c
    send = jnp.where(diag, peer, own)
    kept = jnp.where(diag, own, peer)
    recv = swap(send, "col")
    whole = order_pair(c == 0, kept, recv, 0)
    moved = lax.ppermute(whole, ("row", "col"), [(1, 2), (2, 1)])
    return jnp.where(diag, whole, moved)


def local(
    layer_input,
    teacher,
    valid_mask,
    routes,
    segments,
    gain_attn,
    gain_ffn,
    w_qkv,
    w_out,
    w_router,
    w_shared_up,
    w_shared_down,
    w_expert_up,
    w_expert_down,
):
    r = lax.axis_index("row")
    c = lax.axis_index("col")
    n_dp = lax.axis_size("dp")
    rows = layer_input.shape[0]
    part = rows // 2
    half = layer_input.shape[1]
    heads = w_qkv.shape[2] // HEAD_DIM
    ff = w_shared_up.shape[2]
    quarter = ff // 2
    slots = E + 1

    seg = lax.dynamic_slice_in_dim(segments, r, 1, 0)[0]
    seg_row, seg_col = seg[None, :], seg[:, None]
    tables = rope_tables(rows)
    w_qkv = w_qkv.swapaxes(0, 1)
    vectors = jnp.concatenate(
        [gain_attn[None], gain_ffn[None], w_router.T.astype(F32), jnp.zeros((6 - E, half), F32)]
    )
    (
        queries, keys_rot, values_low, context_low, normed_attn, x_own, hidden,
        w_qkv_peer, w_out_peer, vec_peer, up_own, tokens, up_peer, down_peer,
    ) = front(
        layer_input, w_qkv, w_out, vectors, w_shared_up, w_expert_up, w_shared_down, w_expert_down,
        tables, seg,
    )

    vectors = jnp.concatenate([vectors, vec_peer], axis=1)
    gain_a, gain_f, w_r = vectors[0], vectors[1], vectors[2 : 2 + E].astype(BF).T
    t_pair = to_sequence(teacher, r, c)
    t_seq = jnp.concatenate([t_pair[0], t_pair[1]], axis=1)
    teacher_own = lax.dynamic_slice_in_dim(t_seq, c * part, part, 0).astype(F32)
    valid_other = swap(valid_mask, "col")
    valid_seq = jnp.where(r == c, valid_mask, valid_other).astype(F32)
    valid_own = lax.dynamic_slice_in_dim(valid_seq, c * part, part, 0)
    count = dp_sum(jnp.full((128,), jnp.sum(valid_own), F32))[0]
    route_blocks = routes.reshape(2, 2, part, 2)
    route_blocks = jnp.where(r == 0, route_blocks, route_blocks[::-1])
    route_blocks = jnp.where(c == 0, route_blocks, route_blocks[:, ::-1]).reshape(4 * part, 2)
    picks = (route_blocks[:, :, None] == jnp.arange(E, dtype=jnp.int32)[None, None, :]).astype(F32)

    down_own = jnp.concatenate([w_shared_down[None], w_expert_down])
    down_own = lax.dynamic_slice_in_dim(down_own, r * quarter, quarter, 1)

    x_own = jnp.concatenate([x_own[0], x_own[1]], axis=1).astype(F32)
    rstd_attn = lax.rsqrt(jnp.mean(x_own * x_own, axis=1) + 1e-06)

    rstd_ffn = lax.rsqrt(jnp.mean(hidden * hidden, axis=1) + 1e-06)
    normed_low = tokens[0]
    tokens = tokens.reshape(4 * part, D)
    logits = jnp.dot(tokens, w_r, preferred_element_type=F32)
    chosen = jnp.sum(picks * logits[:, None, :], axis=2)
    chosen = chosen - jnp.max(chosen, axis=1, keepdims=True)
    gates = jnp.exp(chosen)
    gates = gates / jnp.sum(gates, axis=1, keepdims=True)
    mixing = jnp.sum(picks * gates[:, :, None], axis=1)
    mix = jnp.concatenate(
        [jnp.ones((4 * part, 1), F32), mixing, jnp.zeros((4 * part, 7 - E), F32)], axis=1
    )
    pre, act, branch = ffn_forward(tokens, up_own, up_peer, down_own, down_peer, mix)
    output = hidden + collect_tokens(branch.reshape(4, part, D))

    error = output - teacher_own
    loss_part = jnp.sum(valid_own * jnp.sum(error * error, axis=1))
    total_tokens = part * 4 * n_dp
    grad_out = total_tokens / count * valid_own[:, None] * error

    grads = spread_tokens(grad_out.astype(BF)).reshape(4 * part, D)
    down_grad, up_grad, pre_grad, gate_sums = ffn_backward(
        grads, tokens, pre, act, down_own, down_peer, mix
    )
    far_part = ffn_input(pre_grad, up_own, up_peer, 1, 2).reshape(2, part, D)
    near_part = ffn_input(pre_grad, up_own, up_peer, 0, 2).reshape(2, part, D)
    normed_ffn_grad = collect_tokens([near_part[0], near_part[1], far_part[0], far_part[1]])
    gate_parts = gate_sums[:, 1 : E + 1].T.reshape(E, 4, part)
    recv = swap(jnp.stack([gate_parts[:, 1], gate_parts[:, 3]]), "col")
    gate_grad = gate_parts[:, 0] + recv[0] + swap(gate_parts[:, 2] + recv[1], "row")
    mix_own = mixing[:part].T
    centre = jnp.sum(mix_own * gate_grad, axis=0, keepdims=True)
    logit_grad = (mix_own * (gate_grad - centre)).T.astype(BF)
    normed_ffn_grad = normed_ffn_grad + jnp.dot(logit_grad, w_r.T, preferred_element_type=F32)
    router_grad = jnp.dot(normed_low.T, logit_grad, preferred_element_type=F32)
    hidden_back, gain_ffn_grad = norm_backward(hidden, rstd_ffn, gain_f, normed_ffn_grad)
    hidden_grad = grad_out + hidden_back

    low_own = hidden_grad.astype(BF)
    low_seq = order_pair(c == 0, low_own, swap(low_own, "col"), 0)
    w_out_grad = jnp.dot(context_low.T, low_seq, preferred_element_type=F32).astype(BF)
    w_out_full = jnp.concatenate([w_out, w_out_peer], axis=1)
    w_qkv_full = jnp.concatenate([w_qkv, w_qkv_peer], axis=1)
    normed_attn = jnp.concatenate([normed_attn[0], normed_attn[1]], axis=1)
    context_grad = jnp.dot(low_seq, w_out_full.T, preferred_element_type=F32)
    context_grad = context_grad.astype(BF)
    qkv_grad = jnp.concatenate(
        [
            attend_backward(
                queries, keys_rot, values_low, context_grad, tables, seg_row, seg_col, pair, 1
            )
            for pair in range(heads // 2)
        ],
        axis=2,
    )
    w_qkv_grad = jnp.einsum(
        "td,kte->dke", normed_attn, qkv_grad, preferred_element_type=F32
    ).astype(BF)
    back_part = jnp.einsum("kte,kde->td", qkv_grad, w_qkv_full, preferred_element_type=F32)
    back_halves = back_part.reshape(2, part, D)
    back_keep = lax.dynamic_index_in_dim(back_halves, c, 0, keepdims=False)
    back_send = lax.dynamic_index_in_dim(back_halves, 1 - c, 0, keepdims=False)
    normed_attn_grad = back_keep + swap(back_send.astype(BF), "col").astype(F32)
    input_back, gain_attn_grad = norm_backward(x_own, rstd_attn, gain_a, normed_attn_grad)
    input_grad = hidden_grad + input_back

    owner_f = quarter // n_dp
    owner_d = half // n_dp
    deep = n_dp // 2
    grad_pair = jnp.concatenate(
        [
            w_qkv_grad.reshape(2, n_dp, owner_d, 3, half),
            w_out_grad.reshape(n_dp, owner_d, 2, half).transpose(2, 0, 1, 3)[:, :, :, None],
        ],
        axis=3,
    ).transpose(0, 1, 3, 2, 4)
    up_pair, down_pair, attn_piece = dp_reduce(
        up_grad.reshape(slots, 2, deep, 2, owner_d, 2 * quarter),
        down_grad.reshape(slots, deep, 2, owner_f, D),
        grad_pair.reshape(2, deep, 2, 4 * owner_d, half),
    )
    attn_piece = attn_piece.reshape(4, owner_d, half)
    down_piece = jnp.where(r == 0, down_pair, down_pair[::-1]).swapaxes(0, 1)
    up_pair = up_pair.reshape(2, slots, owner_d, 2, quarter)
    up_piece = order_pair(r == 0, up_pair[0], up_pair[1], 3)

    plan = [(1, (), owner_d), (3, (0,), owner_f), (3, (1,), owner_f)]
    for e in range(E):
        plan += [(0, (e,), owner_d), (2, (e, 0), owner_f), (2, (e, 1), owner_f)]
    plan += [(4, (), 0)]
    up_full, shared_up_full, down_full, shared_down_full, attn_full = dp_gather(
        (up_piece[1:], up_piece[0], down_piece[1:], down_piece[0], attn_piece),
        (
            (E, half, 2, ff),
            (half, 2, ff),
            (E, 2, quarter, half),
            (2, quarter, half),
            (n_dp, 4, owner_d, half),
        ),
        tuple(plan),
    )
    attn_full = attn_full.swapaxes(0, 1).reshape(4, half, half).astype(F32)

    small = jnp.concatenate([gain_attn_grad[None], gain_ffn_grad[None], router_grad.T], axis=0)
    small = jnp.where(r == 0, small, flip(small))
    small = jnp.concatenate([small.reshape(-1), loss_part[None]])
    small = dp_sum(small)
    loss = small[-1] / (2.0 * count)
    small = small[:-1].reshape(E + 2, D)
    small = lax.dynamic_slice_in_dim(small, r * half, half, 1)
    return (
        from_sequence(output, r, c),
        loss,
        from_sequence(input_grad, r, c),
        small[0],
        small[1],
        attn_full[:3].swapaxes(0, 1),
        attn_full[3],
        small[2:].T,
        shared_up_full.astype(F32),
        shared_down_full.reshape(ff, half).astype(F32),
        up_full.astype(F32),
        down_full.reshape(E, ff, half).astype(F32),
    )


def solution(mesh):
    return jax.shard_map(
        local,
        mesh=mesh,
        in_specs=(
            P(("dp", "col"), "row"),
            P(("dp", "col"), "row"),
            P(("dp", "col")),
            P("dp", None),
            P("dp", None),
            P("row"),
            P("row"),
            P("row", None, "col"),
            P("col", "row"),
            P("row", None),
            P("row", None, "col"),
            P("col", "row"),
            P(None, "row", None, "col"),
            P(None, "col", "row"),
        ),
        out_specs=(
            P(("dp", "col"), "row"),
            P(),
            P(("dp", "col"), "row"),
            P("row"),
            P("row"),
            P("row", None, "col"),
            P("col", "row"),
            P("row", None),
            P("row", None, "col"),
            P("col", "row"),
            P(None, "row", None, "col"),
            P(None, "col", "row"),
        ),
        check_vma=False,
    )
```

```python
import functools

import jax
import jax.numpy as jnp
from jax import lax
from jax.experimental import pallas as pl
from jax.experimental.pallas import tpu as pltpu
from jax.sharding import PartitionSpec as P

D = 768
HEAD_DIM = 64
E = 4
LEN = 1024
ABLOCK = 256
BF = jnp.bfloat16
F32 = jnp.float32


def norm_backward(values, rstd_rows, gain_vec, incoming):
    scaled = incoming * gain_vec
    inner_sum = jnp.sum(scaled * values, axis=1)
    gain_grad = jnp.sum(incoming * values * rstd_rows[:, None], axis=0)
    result = rstd_rows[:, None] * scaled - values * (rstd_rows**3 * inner_sum / D)[:, None]
    return (result, gain_grad)


def rope_tables(length):
    half_dim = HEAD_DIM // 2
    freqs = 10000.0 ** (-jnp.arange(half_dim, dtype=F32) * 2.0 / HEAD_DIM)
    angles = jnp.arange(length, dtype=F32)[:, None] * freqs[None, :]
    sine = jnp.sin(angles)
    return (jnp.tile(jnp.cos(angles), (1, 4)), jnp.tile(jnp.concatenate([-sine, sine], axis=1), (1, 2)))


def lanes_of(shape):
    return lax.broadcasted_iota(jnp.int32, shape, len(shape) - 1)


def turn(values, first):
    half_dim = HEAD_DIM // 2
    return jnp.where(
        first,
        pltpu.roll(values, PAIR - half_dim, values.ndim - 1),
        pltpu.roll(values, half_dim, values.ndim - 1),
    )


PAIR = 2 * HEAD_DIM
NT = (((1,), (1,)), ((), ()))


def shares_of(key_pair, query_head, seg_col, seg_row):
    scores = lax.dot_general(key_pair, query_head, NT, preferred_element_type=F32)
    scores = jnp.where(seg_col == seg_row, scores, -1e30)
    weight = jnp.exp(scores - jnp.max(scores, axis=0, keepdims=True))
    return weight * (1.0 / jnp.sum(weight, axis=0, keepdims=True))


LAG = 3


def front_kernel(
    n, x_in, teacher, w_qkv, w_out, vectors, shared_up, expert_up, shared_down, expert_down,
    cosine, sine, seg_row, seg_col,
    queries, keys, values, context, normed, x_own, hidden, w_qkv_peer, w_out_peer, vec_peer, up_own,
    tokens, up_peer, down_peer, teacher_pair,
    x_pair, teacher_in, qkv_own, out_own, up_raw, part_raw, up_part, pre, att_send, att_recv, low, low_flip,
    own_sem, x_send, x_recv, w_send, w_recv, t_send, t_recv,
):
    me = lax.axis_index("dp")
    row, col = lax.axis_index("row"), lax.axis_index("col")
    z, x = me // 2, me % 2
    low_z = lax.rem(z, 2)
    x_peer = {"dp": 2 * z + (1 - x)}
    z_peer = {"dp": 2 * (z + 1 - 2 * low_z) + x}
    row_peer, core = {"row": 1 - row}, {"col": 1 - col}
    mine = 2 * low_z + x
    of_x, of_z = 2 * low_z + (1 - x), 2 * (1 - low_z) + x
    rows, half = x_in.shape
    part = rows // 2
    quarter = shared_up.shape[2] // 2
    slots = expert_up.shape[0] + 1
    greet([row_peer, core, x_peer, z_peer])

    def split(index, size):
        return pl.ds(pl.multiple_of(index * size, 16), size)

    def source(item, index):
        if item == 0:
            return w_qkv.at[:, split(index, half // 4)]
        if item == 1:
            return w_out.at[split(index, w_out.shape[0] // 4)]
        slot, kind = (item - 2) // 2, (item - 2) % 2
        if kind == 0:
            return up_part.at[slot]
        ref = shared_down if slot == 0 else expert_down.at[slot - 1]
        first = (1 - row) * quarter + index * (quarter // 4)
        return ref.at[pl.ds(pl.multiple_of(first, 16), quarter // 4)]

    def landing(item, index):
        if item == 0:
            return w_qkv_peer.at[:, split(index, half // 4)]
        if item == 1:
            return w_out_peer.at[split(index, w_out.shape[0] // 4)]
        slot, kind = (item - 2) // 2, (item - 2) % 2
        if kind == 0:
            return up_peer.at[slot, split(index, half // 4)]
        return down_peer.at[slot, split(index, quarter // 4)]

    count = 2 + 2 * slots
    copies = {}

    def start(item, leg, src, device, index):
        copy = remote(
            src, landing(item, index), w_send.at[item, leg], w_recv.at[item, leg], device
        )
        copy.start()
        copies[item, leg] = copy

    def fetch(item):
        start(item, 0, source(item, mine), row_peer, mine)

    def pass_on(item):
        copies[item, 0].wait_recv()
        start(item, 1, landing(item, mine), x_peer, mine)
        start(item, 2, landing(item, mine), z_peer, mine)

    def by_x(item):
        return (item - item // 4) % 2 == 0

    def pass_far(item):
        if by_x(item):
            copies[item, 1].wait_recv()
            start(item, 3, landing(item, of_x), z_peer, of_x)
        else:
            copies[item, 2].wait_recv()
            start(item, 3, landing(item, of_z), x_peer, of_z)

    def arrive(item):
        copies[item, 2 if by_x(item) else 1].wait_recv()
        copies[item, 3].wait_recv()

    progress = [0]

    def pump():
        at = progress[0]
        progress[0] += 1
        if 2 <= at < count:
            pass_on(at)
        if 2 <= at - LAG < count:
            pass_far(at - LAG)

    diagonal = row == col
    over_row = remote(x_in, x_pair.at[1], x_send.at[0], x_recv.at[0], row_peer)
    across_own = remote(x_in, x_pair.at[0], x_send.at[1], x_recv.at[1], core)
    across_peer = remote(x_pair.at[1], x_pair.at[1], x_send.at[2], x_recv.at[2], core)
    own_x = pltpu.make_async_copy(x_in, x_pair.at[0], own_sem.at[0])

    fetch(0)

    @pl.when(diagonal)
    def _():
        own_x.start()
        across_own.start()

    @pl.when(jnp.logical_not(diagonal))
    def _():
        over_row.start()

    def up_slot(slot):
        return shared_up if slot == 0 else expert_up.at[slot - 1]

    keep_lanes = pl.ds(pl.multiple_of(row * quarter, 128), quarter)
    send_lanes = pl.ds(pl.multiple_of((1 - row) * quarter, 128), quarter)
    part_loads, up_loads = [], []
    for slot in range(slots):
        piece = up_slot(slot).at[pl.ds(mine * (half // 4), half // 4), :, send_lanes]
        part_loads.append(pltpu.make_async_copy(piece, part_raw.at[slot], own_sem.at[4 + slot]))
        part_loads[slot].start()

    def split_own(slot):
        up_loads[slot].wait()
        for k in range(2):
            up_own[slot, :, k * quarter : (k + 1) * quarter] = up_raw[slot, :, k]

    give_vectors = remote(vectors, vec_peer, x_send.at[3], x_recv.at[3], row_peer)
    give_vectors.start()
    fetch(1)
    own_qkv = pltpu.make_async_copy(w_qkv, qkv_own, own_sem.at[1])
    own_qkv.start()
    own_out = pltpu.make_async_copy(w_out, out_own, own_sem.at[2])
    own_out.start()

    goal_row = remote(teacher, teacher_in, x_send.at[4], x_recv.at[4], row_peer)
    goal_own = remote(
        teacher.at[split(1 - col, part)], teacher_pair.at[0], x_send.at[5], x_recv.at[5], core
    )
    goal_peer = remote(
        teacher_in.at[split(1 - col, part)], teacher_pair.at[1], x_send.at[6], x_recv.at[6], core
    )
    keep_own = pltpu.make_async_copy(
        teacher.at[split(col, part)], teacher_pair.at[0], own_sem.at[4 + 2 * slots]
    )
    keep_peer = pltpu.make_async_copy(
        teacher_in.at[split(col, part)], teacher_pair.at[1], own_sem.at[5 + 2 * slots]
    )

    for slot in range(slots):
        piece = up_slot(slot).at[:, :, keep_lanes]
        up_loads.append(
            pltpu.make_async_copy(piece, up_raw.at[slot], own_sem.at[4 + slots + slot])
        )
        up_loads[slot].start()
    for slot in range(slots):
        part_loads[slot].wait()
        for k in range(2):
            up_part[slot, :, k * quarter : (k + 1) * quarter] = part_raw[slot, :, k]

    @pl.when(diagonal)
    def _():
        over_row.wait_recv()
        across_peer.start()
        own_x.wait()

    @pl.when(jnp.logical_not(diagonal))
    def _():
        over_row.wait_send()

    for item in range(2, count):
        fetch(item)

    @pl.when(diagonal)
    def _():
        goal_own.start()
        keep_own.start()

    @pl.when(jnp.logical_not(diagonal))
    def _():
        goal_row.start()

    pass_on(0)
    pass_on(1)
    split_own(0)

    @pl.when(jnp.logical_not(diagonal))
    def _():
        across_own.wait_recv()
        across_peer.wait_recv()

    give_vectors.wait_recv()
    progress[0] = 2
    x_first, x_second = x_pair[0].astype(F32), x_pair[1].astype(F32)
    squares = jnp.sum(x_first * x_first, axis=1, keepdims=True)
    squares = squares + jnp.sum(x_second * x_second, axis=1, keepdims=True)
    rstd = lax.rsqrt(squares / (2 * half) + 1e-06)
    normed[0] = (x_first * rstd * vectors[0:1]).astype(BF)
    normed[1] = (x_second * rstd * vec_peer[0:1]).astype(BF)
    pass_far(0)
    pass_far(1)
    for slot in range(1, slots):
        split_own(slot)
    arrive(0)
    own_qkv.wait()
    for j in range(3):
        pre[j] = jnp.dot(normed[0], qkv_own[j], preferred_element_type=F32) + jnp.dot(
            normed[1], w_qkv_peer[j], preferred_element_type=F32
        )
        pump()

    first = lanes_of((rows, PAIR)) % HEAD_DIM < HEAD_DIM // 2
    lower = lanes_of((ABLOCK, PAIR)) < HEAD_DIM
    cos, sin = cosine[...], sine[...]
    for pair in range(half // PAIR):
        lanes = slice(pair * PAIR, (pair + 1) * PAIR)
        query = pre[0, :, lanes]
        queries[:, lanes] = ((query * cos + turn(query, first) * sin) * HEAD_DIM**-0.5).astype(BF)
        key = pre[1, :, lanes]
        keys[:, lanes] = (key * cos + turn(key, first) * sin).astype(BF)
        value = pre[2, :, lanes]
        values[:, lanes] = value.astype(BF)
        value_t = value.T.astype(BF)
        for block in range(rows // ABLOCK):
            begin, stop = block * ABLOCK, (block + 1) * ABLOCK
            query = queries[begin:stop, lanes]
            parts = []
            for head in range(2):
                query_head = jnp.where(lower == (head == 0), query, jnp.zeros_like(query))
                shares = shares_of(
                    keys[:stop, lanes], query_head, seg_col[:stop], seg_row[:, begin:stop]
                ).astype(BF)
                parts.append(jnp.dot(value_t[:, :stop], shares, preferred_element_type=F32))
            both = jnp.concatenate([parts[0][:HEAD_DIM], parts[1][HEAD_DIM:]], axis=0)
            context[begin:stop, lanes] = both.T.astype(BF)
            if block % 2 == 1:
                pump()

    arrive(1)
    own_out.wait()
    there, here = split(1 - col, part), split(col, part)
    for at, weight in enumerate((out_own, w_out_peer)):
        att_send[:, at * half : (at + 1) * half] = jnp.dot(
            context[there], weight[...], preferred_element_type=F32
        ).astype(BF)
    swap_att = remote(att_send, att_recv, t_send.at[0], t_recv.at[0], core)
    swap_att.start()
    pump()
    for at, weight in enumerate((out_own, w_out_peer)):
        lanes = slice(at * half, (at + 1) * half)
        x_own[at] = x_pair[at, here]
        hidden[:, lanes] = x_own[at].astype(F32) + jnp.dot(
            context[here], weight[...], preferred_element_type=F32
        )
    swap_att.wait_recv()
    total = hidden[...] + att_recv[...].astype(F32)
    hidden[...] = total
    rstd = lax.rsqrt(jnp.mean(total * total, axis=1, keepdims=True) + 1e-06)
    gains = jnp.concatenate([vectors[1:2], vec_peer[1:2]], axis=1)
    total = (total * rstd * gains).astype(BF)
    low[...] = total
    low_flip[:, :half] = total[:, half:]
    low_flip[:, half:] = total[:, :half]
    own_tokens = pltpu.make_async_copy(low, tokens.at[0], own_sem.at[3])
    own_tokens.start()
    far = remote(low_flip, tokens.at[2], t_send.at[1], t_recv.at[1], row_peer)
    far.start()
    near = remote(low, tokens.at[1], t_send.at[2], t_recv.at[2], core)
    near.start()
    while progress[0] < count + LAG:
        pump()

    @pl.when(diagonal)
    def _():
        goal_row.wait_recv()
        goal_peer.start()
        keep_peer.start()

    far.wait_recv()
    far_near = remote(tokens.at[2], tokens.at[3], t_send.at[3], t_recv.at[3], core)
    far_near.start()
    for item in range(2, count):
        arrive(item)
    near.wait_recv()
    far_near.wait_recv()
    own_tokens.wait()
    for copy in (give_vectors, swap_att, far, near, far_near, *copies.values()):
        copy.wait_send()

    @pl.when(diagonal)
    def _():
        across_own.wait_send()
        across_peer.wait_send()
        goal_own.wait_send()
        goal_peer.wait_send()
        keep_own.wait()
        keep_peer.wait()

    @pl.when(jnp.logical_not(diagonal))
    def _():
        goal_row.wait_send()
        goal_own.wait_recv()
        goal_peer.wait_recv()


def front(x_in, teacher, w_qkv, w_out, vectors, shared_up, expert_up, shared_down, expert_down, tables, seg):
    n = lax.axis_size("dp")
    rows, half = x_in.shape
    quarter = shared_up.shape[2] // 2
    slots = expert_up.shape[0] + 1
    count = 2 + 2 * slots
    sems = pltpu.SemaphoreType.DMA
    any_spec = pl.BlockSpec(memory_space=pl.ANY)
    vmem_spec = pl.BlockSpec(memory_space=pltpu.VMEM)
    shape = jax.ShapeDtypeStruct
    wide = w_out.shape[0]
    return pl.pallas_call(
        functools.partial(front_kernel, n),
        out_shape=[shape((rows, wide), BF)] * 4
        + [
            shape((2, rows, half), BF),
            shape((2, rows // 2, half), BF),
            shape((rows // 2, 2 * half), F32),
            shape(w_qkv.shape, BF),
            shape(w_out.shape, BF),
            shape(vectors.shape, F32),
            shape((slots, half, 2 * quarter), BF),
            shape((4, rows // 2, 2 * half), BF),
            shape((slots, half, 2 * quarter), BF),
            shape((slots, quarter, half), BF),
            shape((2, rows // 2, half), BF),
        ],
        in_specs=[any_spec] * 4 + [vmem_spec] + [any_spec] * 4 + [vmem_spec] * 4,
        out_specs=[vmem_spec] * 11 + [any_spec] * 4,
        scratch_shapes=[
            pltpu.VMEM((2, rows, half), BF),
            pltpu.VMEM((rows, half), BF),
            pltpu.VMEM(w_qkv.shape, BF),
            pltpu.VMEM(w_out.shape, BF),
            pltpu.VMEM((slots, half, 2, quarter), BF),
            pltpu.VMEM((slots, half // 4, 2, quarter), BF),
            pltpu.VMEM((slots, half // 4, 2 * quarter), BF),
            pltpu.VMEM((3, rows, wide), F32),
            pltpu.VMEM((rows // 2, 2 * half), BF),
            pltpu.VMEM((rows // 2, 2 * half), BF),
            pltpu.VMEM((rows // 2, 2 * half), BF),
            pltpu.VMEM((rows // 2, 2 * half), BF),
            sems((6 + 2 * slots,)),
            sems((7,)),
            sems((7,)),
            sems((count, 4)),
            sems((count, 4)),
            sems((4,)),
            sems((4,)),
        ],
        compiler_params=pltpu.CompilerParams(
            collective_id=2, has_side_effects=True, vmem_limit_bytes=48 << 20
        ),
    )(
        x_in, teacher, w_qkv, w_out, vectors, shared_up, expert_up, shared_down, expert_down,
        tables[0], tables[1], seg[None, :], seg[:, None],
    )


def attend_back_kernel(
    queries, keys, values, context_grad, cosine, sine, seg_row, seg_col, out, key_sum, value_sum
):
    rows = queries.shape[0]
    key_t = keys[...].astype(F32).T.astype(BF)
    lower = lanes_of((ABLOCK, PAIR)) < HEAD_DIM
    first = lanes_of((ABLOCK, PAIR)) % HEAD_DIM < HEAD_DIM // 2
    for block in reversed(range(rows // ABLOCK)):
        start, stop = block * ABLOCK, (block + 1) * ABLOCK
        query, incoming = queries[start:stop], context_grad[start:stop]
        parts, key_part, value_part = [], None, None
        for head in range(2):
            mine = lower == (head == 0)
            query_head = jnp.where(mine, query, jnp.zeros_like(query))
            incoming_head = jnp.where(mine, incoming, jnp.zeros_like(incoming))
            shares = shares_of(keys[:stop], query_head, seg_col[:stop], seg_row[:, start:stop])
            share_grad = lax.dot_general(
                values[:stop], incoming_head, NT, preferred_element_type=F32
            )
            centre = jnp.sum(shares * share_grad, axis=0, keepdims=True)
            score_grad = (shares * (share_grad - centre)).astype(BF)
            parts.append(jnp.dot(key_t[:, :stop], score_grad, preferred_element_type=F32))
            more = jnp.dot(shares.astype(BF), incoming_head, preferred_element_type=F32)
            value_part = more if head == 0 else value_part + more
            more = jnp.dot(score_grad, query_head, preferred_element_type=F32)
            key_part = more if head == 0 else key_part + more
        both = jnp.concatenate([parts[0][:HEAD_DIM], parts[1][HEAD_DIM:]], axis=0)
        grad = both.T * HEAD_DIM**-0.5
        cos, sin = cosine[start:stop], sine[start:stop]
        out[0, start:stop] = (grad * cos + turn(grad * sin, first)).astype(BF)
        if stop == rows:
            key_sum[...] = key_part
            value_sum[...] = value_part
        else:
            key_sum[:stop] += key_part
            value_sum[:stop] += value_part
    for block in range(rows // ABLOCK):
        start, stop = block * ABLOCK, (block + 1) * ABLOCK
        grad = key_sum[start:stop]
        cos, sin = cosine[start:stop], sine[start:stop]
        out[1, start:stop] = (grad * cos + turn(grad * sin, first)).astype(BF)
        out[2, start:stop] = value_sum[start:stop].astype(BF)


def attend_backward(queries, keys, values, context_grad, tables, seg_row, seg_col, first_pair, pairs):
    rows = queries.shape[0]
    block = pl.BlockSpec((rows, PAIR), lambda i: (0, i + first_pair))
    whole = pl.BlockSpec((rows, PAIR), lambda i: (0, 0))
    return pl.pallas_call(
        attend_back_kernel,
        grid=(pairs,),
        out_shape=jax.ShapeDtypeStruct((3, rows, pairs * PAIR), BF),
        in_specs=[block] * 4
        + [
            whole,
            whole,
            pl.BlockSpec((1, rows), lambda i: (0, 0)),
            pl.BlockSpec((rows, 1), lambda i: (0, 0)),
        ],
        out_specs=pl.BlockSpec((3, rows, PAIR), lambda i: (0, 0, i)),
        scratch_shapes=[pltpu.VMEM((rows, PAIR), F32), pltpu.VMEM((rows, PAIR), F32)],
        compiler_params=pltpu.CompilerParams(vmem_limit_bytes=40 << 20),
        cost_estimate=pl.CostEstimate(
            flops=pairs * 14_000_000_000, bytes_accessed=4 << 20, transcendentals=2 << 20
        ),
    )(queries, keys, values, context_grad, tables[0], tables[1], seg_row, seg_col)


def swap(values, axis):
    return lax.ppermute(values, axis, [(0, 1), (1, 0)])


def flip(values):
    half = values.shape[-1] // 2
    return jnp.concatenate([values[..., half:], values[..., :half]], axis=-1)


def remote(src, dst, send, recv, device):
    return pltpu.make_async_remote_copy(
        src_ref=src,
        dst_ref=dst,
        send_sem=send,
        recv_sem=recv,
        device_id=device,
        device_id_type=pl.DeviceIdType.MESH,
    )


def greet(devices):
    barrier = pltpu.get_barrier_semaphore()
    for device in devices:
        pl.semaphore_signal(
            barrier, inc=1, device_id=device, device_id_type=pl.DeviceIdType.MESH
        )
    pl.semaphore_wait(barrier, len(devices))


AHEAD = 3
BEHIND = 3


def reduce_kernel(n, slots, *refs):
    ups, down, attn, up_out, down_out, attn_out = refs[:6]
    (
        up_keep, down_keep, attn_keep, up_x, down_x, attn_x, up_z, down_z, attn_z,
        up_done, down_done, attn_done, attn_y,
        keep_sem, x_send, x_recv, z_send, z_recv, out_sem, y_send, y_recv,
    ) = refs[6:]
    me = lax.axis_index("dp")
    row = lax.axis_index("row")
    deep = n // 2
    z, x = me // 2, me % 2
    partner = {"dp": 2 * z + (1 - x)}
    peer = {"row": 1 - row}
    ahead = [lax.rem(z + k, deep) for k in range(deep)]
    greet([partner, peer] + [{"dp": 2 * ahead[k] + x} for k in range(1, deep)])

    items = [("down", e) for e in range(slots)]
    items += [("up", 2 * e + h) for e in range(slots) for h in (1, 0)]
    items += [("attn", 0)]
    count = len(items)
    last = count - 1

    def buffers(item):
        kind, at = items[item]
        if kind == "down":
            return down.at[at], down_keep.at[at], down_x.at[at], down_z.at[at], down_done.at[at]
        if kind == "up":
            return ups.at[at // 2, at % 2], up_keep.at[at], up_x.at[at], up_z.at[at], up_done.at[at]
        return None, attn_keep.at[:, x], attn_x, attn_z, attn_done

    y_first = remote(attn.at[1], attn_y, y_send.at[last], y_recv.at[last], peer)
    y_first.start()
    attn_load = pltpu.make_async_copy(attn.at[0], attn_keep, keep_sem.at[last])
    attn_load.start()
    loads, x_copies, z_copies, outs, y_copies = {}, {}, {}, [], [y_first]
    for item in range(last):
        source, keep, _, _, _ = buffers(item)
        loads[item] = pltpu.make_async_copy(source.at[:, x], keep, keep_sem.at[item])
        loads[item].start()

    def send_x(item):
        source, keep, landing, _, _ = buffers(item)
        if item == last:
            attn_load.wait()
            y_first.wait_recv()
            attn_keep[...] = (attn_keep[...].astype(F32) + attn_y[...].astype(F32)).astype(BF)
            given = attn_keep.at[:, 1 - x]
        else:
            given = source.at[:, 1 - x]
        x_copies[item] = remote(given, landing, x_send.at[item], x_recv.at[item], partner)
        x_copies[item].start()

    def send_z(item):
        _, keep, landing, arrivals, _ = buffers(item)
        if item in loads:
            loads[item].wait()
        x_copies[item].wait_recv()
        keep[...] = (keep[...].astype(F32) + landing[...].astype(F32)).astype(BF)
        for k in range(1, deep):
            copy = remote(
                keep.at[ahead[k]],
                arrivals.at[k - 1],
                z_send.at[item, k],
                z_recv.at[item, k],
                {"dp": 2 * ahead[k] + x},
            )
            copy.start()
            z_copies[item, k] = copy

    def finish(item):
        kind, at = items[item]
        _, keep, _, arrivals, done = buffers(item)
        total = keep[z].astype(F32)
        for k in range(1, deep):
            z_copies[item, k].wait_recv()
            total = total + arrivals[k - 1].astype(F32)
        done[...] = total.astype(BF)
        half = down.shape[4] // 2

        def keep_own(source, target):
            copy = pltpu.make_async_copy(source, target, out_sem.at[item])
            copy.start()
            outs.append(copy)

        def give_peer(source, target):
            copy = remote(source, target, y_send.at[item], y_recv.at[item], peer)
            copy.start()
            y_copies.append(copy)

        if kind == "down":
            keep_own(done.at[:, :half], down_out.at[0, at])
            give_peer(done.at[:, half:], down_out.at[1, at])
        elif kind == "attn":
            keep_own(done, attn_out)
        elif at % 2 == 0:
            keep_own(done, up_out.at[0, at // 2])
        else:
            give_peer(done, up_out.at[1, at // 2])

    for step in range(count + AHEAD + BEHIND):
        if step < count:
            send_x(step)
        if 0 <= step - AHEAD < count:
            send_z(step - AHEAD)
        if 0 <= step - AHEAD - BEHIND < count:
            finish(step - AHEAD - BEHIND)
    for copy in outs:
        copy.wait()
    y_first.wait_send()
    for copy in y_copies[1:]:
        copy.wait()
    for copy in list(x_copies.values()) + list(z_copies.values()):
        copy.wait_send()


def dp_reduce(up_grads, down_grad, attn_grad):
    n = lax.axis_size("dp")
    deep = n // 2
    slots = up_grads.shape[0]
    up_tail, down_tail, attn_tail = up_grads.shape[4:], down_grad.shape[3:], attn_grad.shape[3:]
    sems = pltpu.SemaphoreType.DMA
    count = 3 * slots + 1
    vmem = lambda *shape: pltpu.VMEM(shape, BF)
    half = down_tail[1] // 2
    any_spec = pl.BlockSpec(memory_space=pl.ANY)
    return pl.pallas_call(
        functools.partial(reduce_kernel, n, slots),
        out_shape=[
            jax.ShapeDtypeStruct((2, slots) + up_tail, BF),
            jax.ShapeDtypeStruct((2, slots, down_tail[0], half), BF),
            jax.ShapeDtypeStruct(attn_tail, BF),
        ],
        in_specs=[any_spec] * 3,
        out_specs=[any_spec] * 3,
        scratch_shapes=[
            vmem(2 * slots, deep, *up_tail),
            vmem(slots, deep, *down_tail),
            vmem(deep, 2, *attn_tail),
            vmem(2 * slots, deep, *up_tail),
            vmem(slots, deep, *down_tail),
            vmem(deep, *attn_tail),
            vmem(2 * slots, deep - 1, *up_tail),
            vmem(slots, deep - 1, *down_tail),
            vmem(deep - 1, *attn_tail),
            vmem(2 * slots, *up_tail),
            vmem(slots, *down_tail),
            vmem(*attn_tail),
            vmem(deep, 2, *attn_tail),
            sems((count,)),
            sems((count,)),
            sems((count,)),
            sems((count, deep)),
            sems((count, deep)),
            sems((count,)),
            sems((count,)),
            sems((count,)),
        ],
        compiler_params=pltpu.CompilerParams(
            collective_id=1, has_side_effects=True, vmem_limit_bytes=48 << 20
        ),
    )(up_grads, down_grad, attn_grad)


def order_pair(first_is_own, own, other, axis):
    return jnp.where(
        first_is_own, jnp.concatenate([own, other], axis), jnp.concatenate([other, own], axis)
    )


WINDOW = 2


def gather_kernel(n, plan, *refs):
    count = max(item[0] for item in plan) + 1
    pieces, fulls = refs[:count], refs[count : 2 * count]
    own_sem, z_send, z_recv, x_send, x_recv = refs[2 * count :]
    me = lax.axis_index("dp")
    deep = n // 2
    z, x = me // 2, me % 2
    partner = 2 * z + (1 - x)
    peers = [2 * lax.rem(z + k, deep) + x for k in range(1, deep)]
    sources = [2 * lax.rem(z + deep - k, deep) + x for k in range(deep)]

    greet([{"dp": device} for device in peers + [partner]])

    def region(item, owner):
        at, lead, rows = plan[item]
        full = fulls[at]
        for index in lead:
            full = full.at[index]
        if rows == 0:
            return full.at[owner]
        start = owner * rows
        if rows % 16 == 0:
            start = pl.multiple_of(start, 16)
        return full.at[pl.ds(start, rows)]

    def piece(item):
        at, lead, rows = plan[item]
        ref = pieces[at]
        for index in lead:
            ref = ref.at[index]
        return ref

    total = len(plan)
    local_copies = []
    z_copies = [[] for _ in range(total)]
    x_copies = [[] for _ in range(total)]
    for step in range(total + WINDOW):
        if step < total:
            here = region(step, me)
            for k in range(1, deep):
                copy = remote(
                    piece(step), here, z_send.at[step, k], z_recv.at[step, k], {"dp": peers[k - 1]}
                )
                copy.start()
                z_copies[step].append(copy)
            copy = remote(piece(step), here, x_send.at[step, 0], x_recv.at[step, 0], {"dp": partner})
            copy.start()
            x_copies[step].append(copy)
            copy = pltpu.make_async_copy(piece(step), here, own_sem.at[step])
            copy.start()
            local_copies.append(copy)
        if step >= WINDOW:
            item = step - WINDOW
            for k in range(1, deep):
                z_copies[item][k - 1].wait_recv()
                arrived = region(item, sources[k])
                copy = remote(
                    arrived, arrived, x_send.at[item, k], x_recv.at[item, k], {"dp": partner}
                )
                copy.start()
                x_copies[item].append(copy)
    for item in range(total):
        local_copies[item].wait()
        for copy in z_copies[item]:
            copy.wait_send()
        for copy in x_copies[item]:
            copy.wait()


def dp_gather(pieces, fulls, plan):
    n = lax.axis_size("dp")
    total = len(plan)
    sems = pltpu.SemaphoreType.DMA
    return pl.pallas_call(
        functools.partial(gather_kernel, n, plan),
        out_shape=[
            jax.ShapeDtypeStruct(shape, piece.dtype) for shape, piece in zip(fulls, pieces)
        ],
        in_specs=[pl.BlockSpec(memory_space=pl.ANY)] * len(pieces),
        out_specs=[pl.BlockSpec(memory_space=pl.ANY)] * len(fulls),
        scratch_shapes=[
            sems((total,)),
            sems((total, n // 2)),
            sems((total, n // 2)),
            sems((total, n // 2)),
            sems((total, n // 2)),
        ],
        compiler_params=pltpu.CompilerParams(collective_id=0, has_side_effects=True),
    )(*pieces)


TN = (((0,), (0,)), ((), ()))
TILE = 512


def column(values, index):
    return jnp.sum(jnp.where(lanes_of(values.shape) == index, values, 0.0), axis=1, keepdims=True)


def ffn_kernel(tokens, up_own, up_peer, down_own, down_peer, mix, pre, act, out):
    slot = pl.program_id(0)
    quarter = down_own.shape[1]
    w_up = jnp.concatenate([up_own[0], up_peer[0]], axis=0)
    w_down = jnp.concatenate([down_own[0], down_peer[0]], axis=1)
    for tile in range(tokens.shape[0] // TILE):
        rows = pl.ds(tile * TILE, TILE)
        both = jnp.dot(tokens[rows], w_up, preferred_element_type=F32)
        pre[0, rows] = both.astype(BF)
        gate, up = both[:, :quarter], both[:, quarter:]
        hidden = gate / (1.0 + jnp.exp(-gate)) * up * column(mix[rows], slot)
        act[0, rows] = hidden.astype(BF)
        part = jnp.dot(hidden.astype(BF), w_down, preferred_element_type=F32)

        @pl.when(slot == 0)
        def _():
            out[rows] = part

        @pl.when(slot > 0)
        def _():
            out[rows] += part


def ffn_forward(tokens, up_own, up_peer, down_own, down_peer, mix):
    slots, half, width = up_own.shape
    rows, depth = tokens.shape
    per_slot = lambda *shape: pl.BlockSpec((1,) + shape, lambda e: (e, 0, 0))
    whole = lambda *shape: pl.BlockSpec(shape, lambda e: (0, 0))
    return pl.pallas_call(
        ffn_kernel,
        grid=(slots,),
        out_shape=[
            jax.ShapeDtypeStruct((slots, rows, width), BF),
            jax.ShapeDtypeStruct((slots, rows, width // 2), BF),
            jax.ShapeDtypeStruct((rows, depth), F32),
        ],
        in_specs=[
            whole(rows, depth),
            per_slot(half, width),
            per_slot(half, width),
            per_slot(width // 2, half),
            per_slot(width // 2, half),
            whole(rows, 8),
        ],
        out_specs=[per_slot(rows, width), per_slot(rows, width // 2), whole(rows, depth)],
        compiler_params=pltpu.CompilerParams(vmem_limit_bytes=56 << 20),
        cost_estimate=pl.CostEstimate(
            flops=3 * slots * rows * depth * width,
            bytes_accessed=40 << 20,
            transcendentals=slots * rows * width // 2,
        ),
    )(tokens, up_own, up_peer, down_own, down_peer, mix)


def ffn_back_kernel(
    grads, tokens, pre, act, down_own, down_peer, mix, down_grad, up_grad, pre_grad, gate_sum
):
    slot = pl.program_id(0)
    quarter = down_own.shape[1]
    w_down = jnp.concatenate([down_own[0], down_peer[0]], axis=1)
    depth = tokens.shape[1]
    for tile in range(tokens.shape[0] // TILE):
        rows = pl.ds(tile * TILE, TILE)
        back = lax.dot_general(grads[rows], w_down, NT, preferred_element_type=F32)
        gate = pre[0, rows, :quarter].astype(F32)
        up = pre[0, rows, quarter:].astype(F32)
        sigma = 1.0 / (1.0 + jnp.exp(-gate))
        act_silu = gate * sigma
        sums = jnp.sum(back * act_silu * up, axis=1, keepdims=True)
        mine = lanes_of((TILE, 8)) == slot

        @pl.when(slot == 0)
        def _():
            gate_sum[rows] = jnp.zeros((TILE, 8), F32)

        gate_sum[rows] += jnp.where(mine, sums, 0.0)
        back = back * column(mix[rows], slot)
        pre_grad[0, rows, :quarter] = (back * up * (sigma * (1.0 + gate * (1.0 - sigma)))).astype(BF)
        pre_grad[0, rows, quarter:] = (back * act_silu).astype(BF)
    down_grad[0] = lax.dot_general(act[0], grads[...], TN, preferred_element_type=F32).astype(BF)
    for tile in range(depth // 256):
        columns = slice(tile * 256, (tile + 1) * 256)
        up_grad[0, columns] = lax.dot_general(
            tokens[:, columns], pre_grad[0], TN, preferred_element_type=F32
        ).astype(BF)


def ffn_backward(grads, tokens, pre, act, down_own, down_peer, mix):
    slots, rows, width = pre.shape
    depth = tokens.shape[1]
    per_slot = lambda *shape: pl.BlockSpec((1,) + shape, lambda e: (e, 0, 0))
    whole = lambda *shape: pl.BlockSpec(shape, lambda e: (0, 0), pipeline_mode=pl.Buffered(1))
    return pl.pallas_call(
        ffn_back_kernel,
        grid=(slots,),
        out_shape=[
            jax.ShapeDtypeStruct((slots, width // 2, depth), BF),
            jax.ShapeDtypeStruct((slots, depth, width), BF),
            jax.ShapeDtypeStruct((slots, rows, width), BF),
            jax.ShapeDtypeStruct((rows, 8), F32),
        ],
        in_specs=[
            whole(rows, depth),
            whole(rows, depth),
            per_slot(rows, width),
            per_slot(rows, width // 2),
            per_slot(width // 2, depth // 2),
            per_slot(width // 2, depth // 2),
            whole(rows, 8),
        ],
        out_specs=[
            per_slot(width // 2, depth),
            per_slot(depth, width),
            per_slot(rows, width),
            pl.BlockSpec((rows, 8), lambda e: (0, 0)),
        ],
        compiler_params=pltpu.CompilerParams(vmem_limit_bytes=58 << 20),
        cost_estimate=pl.CostEstimate(
            flops=4 * slots * rows * depth * width,
            bytes_accessed=70 << 20,
            transcendentals=slots * rows * width // 2,
        ),
    )(grads, tokens, pre, act, down_own, down_peer, mix)


def ffn_input_kernel(pre_grad, up_own, up_peer, out):
    slot = pl.program_id(0)
    w_up = jnp.concatenate([up_own[0], up_peer[0]], axis=0)
    for tile in range(out.shape[0] // TILE):
        rows = pl.ds(tile * TILE, TILE)
        part = lax.dot_general(pre_grad[0, rows], w_up, NT, preferred_element_type=F32)

        @pl.when(slot == 0)
        def _():
            out[rows] = part

        @pl.when(slot > 0)
        def _():
            out[rows] += part


def ffn_input(pre_grad, up_own, up_peer, part, parts):
    slots, rows, width = pre_grad.shape
    half = up_own.shape[1]
    depth = 2 * half
    rows = rows // parts
    return pl.pallas_call(
        ffn_input_kernel,
        grid=(slots,),
        out_shape=jax.ShapeDtypeStruct((rows, depth), F32),
        in_specs=[
            pl.BlockSpec((1, rows, width), lambda e: (e, part, 0)),
            pl.BlockSpec((1, half, width), lambda e: (e, 0, 0)),
            pl.BlockSpec((1, half, width), lambda e: (e, 0, 0)),
        ],
        out_specs=pl.BlockSpec((rows, depth), lambda e: (0, 0)),
        compiler_params=pltpu.CompilerParams(vmem_limit_bytes=40 << 20),
        cost_estimate=pl.CostEstimate(
            flops=2 * slots * rows * depth * width, bytes_accessed=20 << 20, transcendentals=0
        ),
    )(pre_grad, up_own, up_peer)


def spread_tokens(own):
    near = swap(own, "col")
    far = swap(flip(own), "row")
    far_near = swap(far, "col")
    return jnp.stack([own, near, far, far_near])


def collect_tokens(parts):
    far = parts[2] + swap(parts[3].astype(BF), "col").astype(F32)
    far = swap(flip(far.astype(BF)), "row").astype(F32)
    own = parts[0] + swap(parts[1].astype(BF), "col").astype(F32)
    return own + far


def from_sequence(values, r, c):
    half = values.shape[1] // 2
    own, peer = values[:, :half], values[:, half:]
    diag = r == c
    send = jnp.where(diag, peer, own)
    kept = jnp.where(diag, own, peer)
    recv = swap(send, "col")
    whole = order_pair(c == 0, kept, recv, 0)
    moved = lax.ppermute(whole, ("row", "col"), [(1, 2), (2, 1)])
    return jnp.where(diag, whole, moved)


def local(
    layer_input,
    teacher,
    valid_mask,
    routes,
    segments,
    gain_attn,
    gain_ffn,
    w_qkv,
    w_out,
    w_router,
    w_shared_up,
    w_shared_down,
    w_expert_up,
    w_expert_down,
):
    r = lax.axis_index("row")
    c = lax.axis_index("col")
    n_dp = lax.axis_size("dp")
    rows = layer_input.shape[0]
    part = rows // 2
    half = layer_input.shape[1]
    heads = w_qkv.shape[2] // HEAD_DIM
    ff = w_shared_up.shape[2]
    quarter = ff // 2
    slots = E + 1

    seg = lax.dynamic_slice_in_dim(segments, r, 1, 0)[0]
    seg_row, seg_col = seg[None, :], seg[:, None]
    tables = rope_tables(rows)
    w_qkv = w_qkv.swapaxes(0, 1)
    vectors = jnp.concatenate(
        [gain_attn[None], gain_ffn[None], w_router.T.astype(F32), jnp.zeros((6 - E, half), F32)]
    )
    (
        queries, keys_rot, values_low, context_low, normed_attn, x_own, hidden,
        w_qkv_peer, w_out_peer, vec_peer, up_own, tokens, up_peer, down_peer, teacher_pair,
    ) = front(
        layer_input, teacher, w_qkv, w_out, vectors, w_shared_up, w_expert_up, w_shared_down, w_expert_down,
        tables, seg,
    )

    vectors = jnp.concatenate([vectors, vec_peer], axis=1)
    gain_a, gain_f, w_r = vectors[0], vectors[1], vectors[2 : 2 + E].astype(BF).T
    teacher_own = jnp.concatenate([teacher_pair[0], teacher_pair[1]], axis=1).astype(F32)
    valid_other = swap(valid_mask, "col")
    valid_seq = jnp.where(r == c, valid_mask, valid_other).astype(F32)
    valid_own = lax.dynamic_slice_in_dim(valid_seq, c * part, part, 0)
    route_blocks = routes.reshape(2, 2, part, 2)
    route_blocks = jnp.where(r == 0, route_blocks, route_blocks[::-1])
    route_blocks = jnp.where(c == 0, route_blocks, route_blocks[:, ::-1]).reshape(4 * part, 2)
    picks = (route_blocks[:, :, None] == jnp.arange(E, dtype=jnp.int32)[None, None, :]).astype(F32)

    down_own = jnp.concatenate([w_shared_down[None], w_expert_down])
    down_own = lax.dynamic_slice_in_dim(down_own, r * quarter, quarter, 1)

    x_own = jnp.concatenate([x_own[0], x_own[1]], axis=1).astype(F32)
    rstd_attn = lax.rsqrt(jnp.mean(x_own * x_own, axis=1) + 1e-06)

    rstd_ffn = lax.rsqrt(jnp.mean(hidden * hidden, axis=1) + 1e-06)
    normed_low = tokens[0]
    tokens = tokens.reshape(4 * part, D)
    logits = jnp.dot(tokens, w_r, preferred_element_type=F32)
    chosen = jnp.sum(picks * logits[:, None, :], axis=2)
    chosen = chosen - jnp.max(chosen, axis=1, keepdims=True)
    gates = jnp.exp(chosen)
    gates = gates / jnp.sum(gates, axis=1, keepdims=True)
    mixing = jnp.sum(picks * gates[:, :, None], axis=1)
    mix = jnp.concatenate(
        [jnp.ones((4 * part, 1), F32), mixing, jnp.zeros((4 * part, 7 - E), F32)], axis=1
    )
    pre, act, branch = ffn_forward(tokens, up_own, up_peer, down_own, down_peer, mix)
    output = hidden + collect_tokens(branch.reshape(4, part, D))

    error = output - teacher_own
    loss_part = jnp.sum(valid_own * jnp.sum(error * error, axis=1))
    grad_out = valid_own[:, None] * error

    grads = spread_tokens(grad_out.astype(BF)).reshape(4 * part, D)
    down_grad, up_grad, pre_grad, gate_sums = ffn_backward(
        grads, tokens, pre, act, down_own, down_peer, mix
    )
    far_part = ffn_input(pre_grad, up_own, up_peer, 1, 2).reshape(2, part, D)
    near_part = ffn_input(pre_grad, up_own, up_peer, 0, 2).reshape(2, part, D)
    normed_ffn_grad = collect_tokens([near_part[0], near_part[1], far_part[0], far_part[1]])
    gate_parts = gate_sums[:, 1 : E + 1].T.reshape(E, 4, part)
    recv = swap(jnp.stack([gate_parts[:, 1], gate_parts[:, 3]]), "col")
    gate_grad = gate_parts[:, 0] + recv[0] + swap(gate_parts[:, 2] + recv[1], "row")
    mix_own = mixing[:part].T
    centre = jnp.sum(mix_own * gate_grad, axis=0, keepdims=True)
    logit_grad = (mix_own * (gate_grad - centre)).T.astype(BF)
    normed_ffn_grad = normed_ffn_grad + jnp.dot(logit_grad, w_r.T, preferred_element_type=F32)
    router_grad = jnp.dot(normed_low.T, logit_grad, preferred_element_type=F32)
    hidden_back, gain_ffn_grad = norm_backward(hidden, rstd_ffn, gain_f, normed_ffn_grad)
    hidden_grad = grad_out + hidden_back

    low_own = hidden_grad.astype(BF)
    low_seq = order_pair(c == 0, low_own, swap(low_own, "col"), 0)
    w_out_grad = jnp.dot(context_low.T, low_seq, preferred_element_type=F32).astype(BF)
    w_out_full = jnp.concatenate([w_out, w_out_peer], axis=1)
    w_qkv_full = jnp.concatenate([w_qkv, w_qkv_peer], axis=1)
    normed_attn = jnp.concatenate([normed_attn[0], normed_attn[1]], axis=1)
    context_grad = jnp.dot(low_seq, w_out_full.T, preferred_element_type=F32)
    context_grad = context_grad.astype(BF)
    qkv_grad = jnp.concatenate(
        [
            attend_backward(
                queries, keys_rot, values_low, context_grad, tables, seg_row, seg_col, pair, 1
            )
            for pair in range(heads // 2)
        ],
        axis=2,
    )
    w_qkv_grad = jnp.einsum(
        "td,kte->dke", normed_attn, qkv_grad, preferred_element_type=F32
    ).astype(BF)
    back_part = jnp.einsum("kte,kde->td", qkv_grad, w_qkv_full, preferred_element_type=F32)
    back_halves = back_part.reshape(2, part, D)
    back_keep = lax.dynamic_index_in_dim(back_halves, c, 0, keepdims=False)
    back_send = lax.dynamic_index_in_dim(back_halves, 1 - c, 0, keepdims=False)
    normed_attn_grad = back_keep + swap(back_send.astype(BF), "col").astype(F32)
    input_back, gain_attn_grad = norm_backward(x_own, rstd_attn, gain_a, normed_attn_grad)
    input_grad = hidden_grad + input_back

    owner_f = quarter // n_dp
    owner_d = half // n_dp
    deep = n_dp // 2
    grad_pair = jnp.concatenate(
        [
            w_qkv_grad.reshape(2, n_dp, owner_d, 3, half),
            w_out_grad.reshape(n_dp, owner_d, 2, half).transpose(2, 0, 1, 3)[:, :, :, None],
        ],
        axis=3,
    ).transpose(0, 1, 3, 2, 4)
    up_pair, down_pair, attn_piece = dp_reduce(
        up_grad.reshape(slots, 2, deep, 2, owner_d, 2 * quarter),
        down_grad.reshape(slots, deep, 2, owner_f, D),
        grad_pair.reshape(2, deep, 2, 4 * owner_d, half),
    )
    attn_piece = attn_piece.reshape(4, owner_d, half)
    down_piece = jnp.where(r == 0, down_pair, down_pair[::-1]).swapaxes(0, 1)
    up_pair = up_pair.reshape(2, slots, owner_d, 2, quarter)
    up_piece = order_pair(r == 0, up_pair[0], up_pair[1], 3)

    small = jnp.concatenate([gain_attn_grad[None], gain_ffn_grad[None], router_grad.T], axis=0)
    small = jnp.where(r == 0, small, flip(small))
    loss_row = jnp.full((1, D), loss_part).at[0, half:].set(jnp.sum(valid_own))
    small = jnp.concatenate([small, loss_row, jnp.zeros((1, D), F32)])
    small = small + swap(small, "row")
    small = small + swap(small, "col")
    plan = [(1, (), owner_d), (3, (0,), owner_f), (3, (1,), owner_f)]
    for e in range(E):
        plan += [(0, (e,), owner_d), (2, (e, 0), owner_f), (2, (e, 1), owner_f)]
    plan += [(4, (), 0), (5, (), 0)]
    up_full, shared_up_full, down_full, shared_down_full, attn_full, small_full = dp_gather(
        (up_piece[1:], up_piece[0], down_piece[1:], down_piece[0], attn_piece, small),
        (
            (E, half, 2, ff),
            (half, 2, ff),
            (E, 2, quarter, half),
            (2, quarter, half),
            (n_dp, 4, owner_d, half),
            (n_dp, E + 4, D),
        ),
        tuple(plan),
    )
    small = jnp.sum(small_full, axis=0)
    count = small[E + 2, half]
    loss = small[E + 2, 0] / (2.0 * count)
    scale = part * 4 * n_dp / count
    small = small[: E + 2] * scale
    attn_full = attn_full.swapaxes(0, 1).reshape(4, half, half).astype(F32) * scale
    small = lax.dynamic_slice_in_dim(small, r * half, half, 1)
    return (
        from_sequence(output, r, c),
        loss,
        from_sequence(input_grad, r, c) * scale,
        small[0],
        small[1],
        attn_full[:3].swapaxes(0, 1),
        attn_full[3],
        small[2:].T,
        shared_up_full.astype(F32) * scale,
        shared_down_full.reshape(ff, half).astype(F32) * scale,
        up_full.astype(F32) * scale,
        down_full.reshape(E, ff, half).astype(F32) * scale,
    )


def solution(mesh):
    return jax.shard_map(
        local,
        mesh=mesh,
        in_specs=(
            P(("dp", "col"), "row"),
            P(("dp", "col"), "row"),
            P(("dp", "col")),
            P("dp", None),
            P("dp", None),
            P("row"),
            P("row"),
            P("row", None, "col"),
            P("col", "row"),
            P("row", None),
            P("row", None, "col"),
            P("col", "row"),
            P(None, "row", None, "col"),
            P(None, "col", "row"),
        ),
        out_specs=(
            P(("dp", "col"), "row"),
            P(),
            P(("dp", "col"), "row"),
            P("row"),
            P("row"),
            P("row", None, "col"),
            P("col", "row"),
            P("row", None),
            P("row", None, "col"),
            P("col", "row"),
            P(None, "row", None, "col"),
            P(None, "col", "row"),
        ),
        check_vma=False,
    )
```

```python
import functools

import jax
import jax.numpy as jnp
from jax import lax
from jax.experimental import pallas as pl
from jax.experimental.pallas import tpu as pltpu
from jax.sharding import PartitionSpec as P

D = 768
HEAD_DIM = 64
E = 4
LEN = 1024
ABLOCK = 256
BF = jnp.bfloat16
F32 = jnp.float32


def norm_backward(values, rstd_rows, gain_vec, incoming):
    scaled = incoming * gain_vec
    inner_sum = jnp.sum(scaled * values, axis=1)
    gain_grad = jnp.sum(incoming * values * rstd_rows[:, None], axis=0)
    result = rstd_rows[:, None] * scaled - values * (rstd_rows**3 * inner_sum / D)[:, None]
    return (result, gain_grad)


def rope_tables(length):
    half_dim = HEAD_DIM // 2
    freqs = 10000.0 ** (-jnp.arange(half_dim, dtype=F32) * 2.0 / HEAD_DIM)
    angles = jnp.arange(length, dtype=F32)[:, None] * freqs[None, :]
    sine = jnp.sin(angles)
    return (jnp.tile(jnp.cos(angles), (1, 4)), jnp.tile(jnp.concatenate([-sine, sine], axis=1), (1, 2)))


def lanes_of(shape):
    return lax.broadcasted_iota(jnp.int32, shape, len(shape) - 1)


def turn(values, first):
    half_dim = HEAD_DIM // 2
    return jnp.where(
        first,
        pltpu.roll(values, PAIR - half_dim, values.ndim - 1),
        pltpu.roll(values, half_dim, values.ndim - 1),
    )


PAIR = 2 * HEAD_DIM
NT = (((1,), (1,)), ((), ()))


def shares_of(key_pair, query_head, seg_col, seg_row):
    scores = lax.dot_general(key_pair, query_head, NT, preferred_element_type=F32)
    scores = jnp.where(seg_col == seg_row, scores, -1e30)
    weight = jnp.exp(scores - jnp.max(scores, axis=0, keepdims=True))
    return weight * (1.0 / jnp.sum(weight, axis=0, keepdims=True))


LAG = 3


def front_kernel(
    n, x_in, teacher, w_qkv, w_out, vectors, shared_up, expert_up, shared_down, expert_down,
    cosine, sine, seg_row, seg_col,
    queries, keys, values, context, normed, x_own, hidden, w_qkv_peer, w_out_peer, vec_peer, up_own,
    tokens, up_peer, down_peer, teacher_pair,
    x_pair, teacher_in, qkv_own, out_own, up_raw, part_raw, up_part, pre, att_send, att_recv, low, low_flip,
    own_sem, x_send, x_recv, w_send, w_recv, t_send, t_recv,
):
    me = lax.axis_index("dp")
    row, col = lax.axis_index("row"), lax.axis_index("col")
    z, x = me // 2, me % 2
    low_z = lax.rem(z, 2)
    x_peer = {"dp": 2 * z + (1 - x)}
    z_peer = {"dp": 2 * (z + 1 - 2 * low_z) + x}
    row_peer, core = {"row": 1 - row}, {"col": 1 - col}
    mine = 2 * low_z + x
    of_x, of_z = 2 * low_z + (1 - x), 2 * (1 - low_z) + x
    rows, half = x_in.shape
    part = rows // 2
    quarter = shared_up.shape[2] // 2
    slots = expert_up.shape[0] + 1
    greet([row_peer, core, x_peer, z_peer])

    def split(index, size):
        return pl.ds(pl.multiple_of(index * size, 16), size)

    def source(item, index):
        if item == 0:
            return w_qkv.at[:, split(index, half // 4)]
        if item == 1:
            return w_out.at[split(index, w_out.shape[0] // 4)]
        slot, kind = (item - 2) // 2, (item - 2) % 2
        if kind == 0:
            return up_part.at[slot]
        ref = shared_down if slot == 0 else expert_down.at[slot - 1]
        first = (1 - row) * quarter + index * (quarter // 4)
        return ref.at[pl.ds(pl.multiple_of(first, 16), quarter // 4)]

    def landing(item, index):
        if item == 0:
            return w_qkv_peer.at[:, split(index, half // 4)]
        if item == 1:
            return w_out_peer.at[split(index, w_out.shape[0] // 4)]
        slot, kind = (item - 2) // 2, (item - 2) % 2
        if kind == 0:
            return up_peer.at[slot, split(index, half // 4)]
        return down_peer.at[slot, split(index, quarter // 4)]

    count = 2 + 2 * slots
    copies = {}

    def start(item, leg, src, device, index):
        copy = remote(
            src, landing(item, index), w_send.at[item, leg], w_recv.at[item, leg], device
        )
        copy.start()
        copies[item, leg] = copy

    def fetch(item):
        start(item, 0, source(item, mine), row_peer, mine)

    def pass_on(item):
        copies[item, 0].wait_recv()
        start(item, 1, landing(item, mine), x_peer, mine)
        start(item, 2, landing(item, mine), z_peer, mine)

    def by_x(item):
        return (item - item // 4) % 2 == 0

    def pass_far(item):
        if by_x(item):
            copies[item, 1].wait_recv()
            start(item, 3, landing(item, of_x), z_peer, of_x)
        else:
            copies[item, 2].wait_recv()
            start(item, 3, landing(item, of_z), x_peer, of_z)

    def arrive(item):
        copies[item, 2 if by_x(item) else 1].wait_recv()
        copies[item, 3].wait_recv()

    progress = [0]

    def pump():
        at = progress[0]
        progress[0] += 1
        if 2 <= at < count:
            pass_on(at)
        if 2 <= at - LAG < count:
            pass_far(at - LAG)

    diagonal = row == col
    over_row = remote(x_in, x_pair.at[1], x_send.at[0], x_recv.at[0], row_peer)
    across_own = remote(x_in, x_pair.at[0], x_send.at[1], x_recv.at[1], core)
    across_peer = remote(x_pair.at[1], x_pair.at[1], x_send.at[2], x_recv.at[2], core)
    own_x = pltpu.make_async_copy(x_in, x_pair.at[0], own_sem.at[0])

    fetch(0)

    @pl.when(diagonal)
    def _():
        own_x.start()
        across_own.start()

    @pl.when(jnp.logical_not(diagonal))
    def _():
        over_row.start()

    def up_slot(slot):
        return shared_up if slot == 0 else expert_up.at[slot - 1]

    keep_lanes = pl.ds(pl.multiple_of(row * quarter, 128), quarter)
    send_lanes = pl.ds(pl.multiple_of((1 - row) * quarter, 128), quarter)
    part_loads, up_loads = [], []
    for slot in range(slots):
        piece = up_slot(slot).at[pl.ds(mine * (half // 4), half // 4), :, send_lanes]
        part_loads.append(pltpu.make_async_copy(piece, part_raw.at[slot], own_sem.at[4 + slot]))
        part_loads[slot].start()

    def split_own(slot):
        up_loads[slot].wait()
        for k in range(2):
            up_own[slot, :, k * quarter : (k + 1) * quarter] = up_raw[slot, :, k]

    give_vectors = remote(vectors, vec_peer, x_send.at[3], x_recv.at[3], row_peer)
    give_vectors.start()
    fetch(1)
    own_qkv = pltpu.make_async_copy(w_qkv, qkv_own, own_sem.at[1])
    own_qkv.start()
    own_out = pltpu.make_async_copy(w_out, out_own, own_sem.at[2])
    own_out.start()

    goal_row = remote(teacher, teacher_in, x_send.at[4], x_recv.at[4], row_peer)
    goal_own = remote(
        teacher.at[split(1 - col, part)], teacher_pair.at[0], x_send.at[5], x_recv.at[5], core
    )
    goal_peer = remote(
        teacher_in.at[split(1 - col, part)], teacher_pair.at[1], x_send.at[6], x_recv.at[6], core
    )
    keep_own = pltpu.make_async_copy(
        teacher.at[split(col, part)], teacher_pair.at[0], own_sem.at[4 + 2 * slots]
    )
    keep_peer = pltpu.make_async_copy(
        teacher_in.at[split(col, part)], teacher_pair.at[1], own_sem.at[5 + 2 * slots]
    )

    for slot in range(slots):
        piece = up_slot(slot).at[:, :, keep_lanes]
        up_loads.append(
            pltpu.make_async_copy(piece, up_raw.at[slot], own_sem.at[4 + slots + slot])
        )
        up_loads[slot].start()
    for slot in range(slots):
        part_loads[slot].wait()
        for k in range(2):
            up_part[slot, :, k * quarter : (k + 1) * quarter] = part_raw[slot, :, k]

    @pl.when(diagonal)
    def _():
        over_row.wait_recv()
        across_peer.start()
        own_x.wait()

    @pl.when(jnp.logical_not(diagonal))
    def _():
        over_row.wait_send()

    for item in range(2, count):
        fetch(item)

    @pl.when(diagonal)
    def _():
        goal_own.start()
        keep_own.start()

    @pl.when(jnp.logical_not(diagonal))
    def _():
        goal_row.start()

    pass_on(0)
    pass_on(1)
    split_own(0)

    @pl.when(jnp.logical_not(diagonal))
    def _():
        across_own.wait_recv()
        across_peer.wait_recv()

    give_vectors.wait_recv()
    progress[0] = 2
    x_first, x_second = x_pair[0].astype(F32), x_pair[1].astype(F32)
    squares = jnp.sum(x_first * x_first, axis=1, keepdims=True)
    squares = squares + jnp.sum(x_second * x_second, axis=1, keepdims=True)
    rstd = lax.rsqrt(squares / (2 * half) + 1e-06)
    normed[0] = (x_first * rstd * vectors[0:1]).astype(BF)
    normed[1] = (x_second * rstd * vec_peer[0:1]).astype(BF)
    pass_far(0)
    pass_far(1)
    for slot in range(1, slots):
        split_own(slot)
    arrive(0)
    own_qkv.wait()
    for j in range(3):
        pre[j] = jnp.dot(normed[0], qkv_own[j], preferred_element_type=F32) + jnp.dot(
            normed[1], w_qkv_peer[j], preferred_element_type=F32
        )
        pump()

    first = lanes_of((rows, PAIR)) % HEAD_DIM < HEAD_DIM // 2
    lower = lanes_of((ABLOCK, PAIR)) < HEAD_DIM
    cos, sin = cosine[...], sine[...]
    for pair in range(half // PAIR):
        lanes = slice(pair * PAIR, (pair + 1) * PAIR)
        query = pre[0, :, lanes]
        queries[:, lanes] = ((query * cos + turn(query, first) * sin) * HEAD_DIM**-0.5).astype(BF)
        key = pre[1, :, lanes]
        keys[:, lanes] = (key * cos + turn(key, first) * sin).astype(BF)
        value = pre[2, :, lanes]
        values[:, lanes] = value.astype(BF)
        value_t = value.T.astype(BF)
        for block in range(rows // ABLOCK):
            begin, stop = block * ABLOCK, (block + 1) * ABLOCK
            query = queries[begin:stop, lanes]
            parts = []
            for head in range(2):
                query_head = jnp.where(lower == (head == 0), query, jnp.zeros_like(query))
                shares = shares_of(
                    keys[:stop, lanes], query_head, seg_col[:stop], seg_row[:, begin:stop]
                ).astype(BF)
                parts.append(jnp.dot(value_t[:, :stop], shares, preferred_element_type=F32))
            both = jnp.concatenate([parts[0][:HEAD_DIM], parts[1][HEAD_DIM:]], axis=0)
            context[begin:stop, lanes] = both.T.astype(BF)
            if block % 2 == 1:
                pump()

    arrive(1)
    own_out.wait()
    there, here = split(1 - col, part), split(col, part)
    for at, weight in enumerate((out_own, w_out_peer)):
        att_send[:, at * half : (at + 1) * half] = jnp.dot(
            context[there], weight[...], preferred_element_type=F32
        ).astype(BF)
    swap_att = remote(att_send, att_recv, t_send.at[0], t_recv.at[0], core)
    swap_att.start()
    pump()
    for at, weight in enumerate((out_own, w_out_peer)):
        lanes = slice(at * half, (at + 1) * half)
        x_own[at] = x_pair[at, here]
        hidden[:, lanes] = x_own[at].astype(F32) + jnp.dot(
            context[here], weight[...], preferred_element_type=F32
        )
    swap_att.wait_recv()
    total = hidden[...] + att_recv[...].astype(F32)
    hidden[...] = total
    rstd = lax.rsqrt(jnp.mean(total * total, axis=1, keepdims=True) + 1e-06)
    gains = jnp.concatenate([vectors[1:2], vec_peer[1:2]], axis=1)
    total = (total * rstd * gains).astype(BF)
    low[...] = total
    low_flip[:, :half] = total[:, half:]
    low_flip[:, half:] = total[:, :half]
    own_tokens = pltpu.make_async_copy(low, tokens.at[0], own_sem.at[3])
    own_tokens.start()
    far = remote(low_flip, tokens.at[2], t_send.at[1], t_recv.at[1], row_peer)
    far.start()
    near = remote(low, tokens.at[1], t_send.at[2], t_recv.at[2], core)
    near.start()
    while progress[0] < count + LAG:
        pump()

    @pl.when(diagonal)
    def _():
        goal_row.wait_recv()
        goal_peer.start()
        keep_peer.start()

    far.wait_recv()
    far_near = remote(tokens.at[2], tokens.at[3], t_send.at[3], t_recv.at[3], core)
    far_near.start()
    for item in range(2, count):
        arrive(item)
    near.wait_recv()
    far_near.wait_recv()
    own_tokens.wait()
    for copy in (give_vectors, swap_att, far, near, far_near, *copies.values()):
        copy.wait_send()

    @pl.when(diagonal)
    def _():
        across_own.wait_send()
        across_peer.wait_send()
        goal_own.wait_send()
        goal_peer.wait_send()
        keep_own.wait()
        keep_peer.wait()

    @pl.when(jnp.logical_not(diagonal))
    def _():
        goal_row.wait_send()
        goal_own.wait_recv()
        goal_peer.wait_recv()


def front(x_in, teacher, w_qkv, w_out, vectors, shared_up, expert_up, shared_down, expert_down, tables, seg):
    n = lax.axis_size("dp")
    rows, half = x_in.shape
    quarter = shared_up.shape[2] // 2
    slots = expert_up.shape[0] + 1
    count = 2 + 2 * slots
    sems = pltpu.SemaphoreType.DMA
    any_spec = pl.BlockSpec(memory_space=pl.ANY)
    vmem_spec = pl.BlockSpec(memory_space=pltpu.VMEM)
    shape = jax.ShapeDtypeStruct
    wide = w_out.shape[0]
    return pl.pallas_call(
        functools.partial(front_kernel, n),
        out_shape=[shape((rows, wide), BF)] * 4
        + [
            shape((2, rows, half), BF),
            shape((2, rows // 2, half), BF),
            shape((rows // 2, 2 * half), F32),
            shape(w_qkv.shape, BF),
            shape(w_out.shape, BF),
            shape(vectors.shape, F32),
            shape((slots, half, 2 * quarter), BF),
            shape((4, rows // 2, 2 * half), BF),
            shape((slots, half, 2 * quarter), BF),
            shape((slots, quarter, half), BF),
            shape((2, rows // 2, half), BF),
        ],
        in_specs=[any_spec] * 4 + [vmem_spec] + [any_spec] * 4 + [vmem_spec] * 4,
        out_specs=[vmem_spec] * 11 + [any_spec] * 4,
        scratch_shapes=[
            pltpu.VMEM((2, rows, half), BF),
            pltpu.VMEM((rows, half), BF),
            pltpu.VMEM(w_qkv.shape, BF),
            pltpu.VMEM(w_out.shape, BF),
            pltpu.VMEM((slots, half, 2, quarter), BF),
            pltpu.VMEM((slots, half // 4, 2, quarter), BF),
            pltpu.VMEM((slots, half // 4, 2 * quarter), BF),
            pltpu.VMEM((3, rows, wide), F32),
            pltpu.VMEM((rows // 2, 2 * half), BF),
            pltpu.VMEM((rows // 2, 2 * half), BF),
            pltpu.VMEM((rows // 2, 2 * half), BF),
            pltpu.VMEM((rows // 2, 2 * half), BF),
            sems((6 + 2 * slots,)),
            sems((7,)),
            sems((7,)),
            sems((count, 4)),
            sems((count, 4)),
            sems((4,)),
            sems((4,)),
        ],
        compiler_params=pltpu.CompilerParams(
            collective_id=2, has_side_effects=True, vmem_limit_bytes=48 << 20
        ),
    )(
        x_in, teacher, w_qkv, w_out, vectors, shared_up, expert_up, shared_down, expert_down,
        tables[0], tables[1], seg[None, :], seg[:, None],
    )


def attend_back_kernel(
    queries, keys, values, context_grad, cosine, sine, seg_row, seg_col, out, key_sum, value_sum
):
    rows = queries.shape[0]
    key_t = keys[...].astype(F32).T.astype(BF)
    lower = lanes_of((ABLOCK, PAIR)) < HEAD_DIM
    first = lanes_of((ABLOCK, PAIR)) % HEAD_DIM < HEAD_DIM // 2
    for block in reversed(range(rows // ABLOCK)):
        start, stop = block * ABLOCK, (block + 1) * ABLOCK
        query, incoming = queries[start:stop], context_grad[start:stop]
        parts, key_part, value_part = [], None, None
        for head in range(2):
            mine = lower == (head == 0)
            query_head = jnp.where(mine, query, jnp.zeros_like(query))
            incoming_head = jnp.where(mine, incoming, jnp.zeros_like(incoming))
            shares = shares_of(keys[:stop], query_head, seg_col[:stop], seg_row[:, start:stop])
            share_grad = lax.dot_general(
                values[:stop], incoming_head, NT, preferred_element_type=F32
            )
            centre = jnp.sum(shares * share_grad, axis=0, keepdims=True)
            score_grad = (shares * (share_grad - centre)).astype(BF)
            parts.append(jnp.dot(key_t[:, :stop], score_grad, preferred_element_type=F32))
            more = jnp.dot(shares.astype(BF), incoming_head, preferred_element_type=F32)
            value_part = more if head == 0 else value_part + more
            more = jnp.dot(score_grad, query_head, preferred_element_type=F32)
            key_part = more if head == 0 else key_part + more
        both = jnp.concatenate([parts[0][:HEAD_DIM], parts[1][HEAD_DIM:]], axis=0)
        grad = both.T * HEAD_DIM**-0.5
        cos, sin = cosine[start:stop], sine[start:stop]
        out[0, start:stop] = (grad * cos + turn(grad * sin, first)).astype(BF)
        if stop == rows:
            key_sum[...] = key_part
            value_sum[...] = value_part
        else:
            key_sum[:stop] += key_part
            value_sum[:stop] += value_part
    for block in range(rows // ABLOCK):
        start, stop = block * ABLOCK, (block + 1) * ABLOCK
        grad = key_sum[start:stop]
        cos, sin = cosine[start:stop], sine[start:stop]
        out[1, start:stop] = (grad * cos + turn(grad * sin, first)).astype(BF)
        out[2, start:stop] = value_sum[start:stop].astype(BF)


def attend_backward(queries, keys, values, context_grad, tables, seg_row, seg_col, first_pair, pairs):
    rows = queries.shape[0]
    block = pl.BlockSpec((rows, PAIR), lambda i: (0, i + first_pair))
    whole = pl.BlockSpec((rows, PAIR), lambda i: (0, 0))
    return pl.pallas_call(
        attend_back_kernel,
        grid=(pairs,),
        out_shape=jax.ShapeDtypeStruct((3, rows, pairs * PAIR), BF),
        in_specs=[block] * 4
        + [
            whole,
            whole,
            pl.BlockSpec((1, rows), lambda i: (0, 0)),
            pl.BlockSpec((rows, 1), lambda i: (0, 0)),
        ],
        out_specs=pl.BlockSpec((3, rows, PAIR), lambda i: (0, 0, i)),
        scratch_shapes=[pltpu.VMEM((rows, PAIR), F32), pltpu.VMEM((rows, PAIR), F32)],
        compiler_params=pltpu.CompilerParams(vmem_limit_bytes=40 << 20),
        cost_estimate=pl.CostEstimate(
            flops=pairs * 14_000_000_000, bytes_accessed=4 << 20, transcendentals=2 << 20
        ),
    )(queries, keys, values, context_grad, tables[0], tables[1], seg_row, seg_col)


def swap(values, axis):
    return lax.ppermute(values, axis, [(0, 1), (1, 0)])


def flip(values):
    half = values.shape[-1] // 2
    return jnp.concatenate([values[..., half:], values[..., :half]], axis=-1)


def remote(src, dst, send, recv, device):
    return pltpu.make_async_remote_copy(
        src_ref=src,
        dst_ref=dst,
        send_sem=send,
        recv_sem=recv,
        device_id=device,
        device_id_type=pl.DeviceIdType.MESH,
    )


def greet(devices):
    barrier = pltpu.get_barrier_semaphore()
    for device in devices:
        pl.semaphore_signal(
            barrier, inc=1, device_id=device, device_id_type=pl.DeviceIdType.MESH
        )
    pl.semaphore_wait(barrier, len(devices))


AHEAD = 3
BEHIND = 3


def reduce_kernel(n, slots, *refs):
    ups, down, attn, up_out, down_out, attn_out = refs[:6]
    (
        up_keep, down_keep, attn_keep, up_x, down_x, attn_x, up_z, down_z, attn_z,
        up_done, down_done, attn_done, attn_y,
        keep_sem, x_send, x_recv, z_send, z_recv, out_sem, y_send, y_recv,
    ) = refs[6:]
    me = lax.axis_index("dp")
    row = lax.axis_index("row")
    deep = n // 2
    z, x = me // 2, me % 2
    partner = {"dp": 2 * z + (1 - x)}
    peer = {"row": 1 - row}
    ahead = [lax.rem(z + k, deep) for k in range(deep)]
    greet([partner, peer] + [{"dp": 2 * ahead[k] + x} for k in range(1, deep)])

    items = [("down", e) for e in range(slots)]
    items += [("up", 2 * e + h) for e in range(slots) for h in (1, 0)]
    items += [("attn", 0)]
    count = len(items)
    last = count - 1

    def buffers(item):
        kind, at = items[item]
        if kind == "down":
            return down.at[at], down_keep.at[at], down_x.at[at], down_z.at[at], down_done.at[at]
        if kind == "up":
            return ups.at[at // 2, at % 2], up_keep.at[at], up_x.at[at], up_z.at[at], up_done.at[at]
        return None, attn_keep.at[:, x], attn_x, attn_z, attn_done

    y_first = remote(attn.at[1], attn_y, y_send.at[last], y_recv.at[last], peer)
    y_first.start()
    attn_load = pltpu.make_async_copy(attn.at[0], attn_keep, keep_sem.at[last])
    attn_load.start()
    loads, x_copies, z_copies, outs, y_copies = {}, {}, {}, [], [y_first]
    for item in range(last):
        source, keep, _, _, _ = buffers(item)
        loads[item] = pltpu.make_async_copy(source.at[:, x], keep, keep_sem.at[item])
        loads[item].start()

    def send_x(item):
        source, keep, landing, _, _ = buffers(item)
        if item == last:
            attn_load.wait()
            y_first.wait_recv()
            attn_keep[...] = (attn_keep[...].astype(F32) + attn_y[...].astype(F32)).astype(BF)
            given = attn_keep.at[:, 1 - x]
        else:
            given = source.at[:, 1 - x]
        x_copies[item] = remote(given, landing, x_send.at[item], x_recv.at[item], partner)
        x_copies[item].start()

    def send_z(item):
        _, keep, landing, arrivals, _ = buffers(item)
        if item in loads:
            loads[item].wait()
        x_copies[item].wait_recv()
        keep[...] = (keep[...].astype(F32) + landing[...].astype(F32)).astype(BF)
        for k in range(1, deep):
            copy = remote(
                keep.at[ahead[k]],
                arrivals.at[k - 1],
                z_send.at[item, k],
                z_recv.at[item, k],
                {"dp": 2 * ahead[k] + x},
            )
            copy.start()
            z_copies[item, k] = copy

    def finish(item):
        kind, at = items[item]
        _, keep, _, arrivals, done = buffers(item)
        total = keep[z].astype(F32)
        for k in range(1, deep):
            z_copies[item, k].wait_recv()
            total = total + arrivals[k - 1].astype(F32)
        done[...] = total.astype(BF)
        half = down.shape[4] // 2

        def keep_own(source, target):
            copy = pltpu.make_async_copy(source, target, out_sem.at[item])
            copy.start()
            outs.append(copy)

        def give_peer(source, target):
            copy = remote(source, target, y_send.at[item], y_recv.at[item], peer)
            copy.start()
            y_copies.append(copy)

        if kind == "down":
            keep_own(done.at[:, :half], down_out.at[0, at])
            give_peer(done.at[:, half:], down_out.at[1, at])
        elif kind == "attn":
            keep_own(done, attn_out)
        elif at % 2 == 0:
            keep_own(done, up_out.at[0, at // 2])
        else:
            give_peer(done, up_out.at[1, at // 2])

    for step in range(count + AHEAD + BEHIND):
        if step < count:
            send_x(step)
        if 0 <= step - AHEAD < count:
            send_z(step - AHEAD)
        if 0 <= step - AHEAD - BEHIND < count:
            finish(step - AHEAD - BEHIND)
    for copy in outs:
        copy.wait()
    y_first.wait_send()
    for copy in y_copies[1:]:
        copy.wait()
    for copy in list(x_copies.values()) + list(z_copies.values()):
        copy.wait_send()


def dp_reduce(up_grads, down_grad, attn_grad):
    n = lax.axis_size("dp")
    deep = n // 2
    slots = up_grads.shape[0]
    up_tail, down_tail, attn_tail = up_grads.shape[4:], down_grad.shape[3:], attn_grad.shape[3:]
    sems = pltpu.SemaphoreType.DMA
    count = 3 * slots + 1
    vmem = lambda *shape: pltpu.VMEM(shape, BF)
    half = down_tail[1] // 2
    any_spec = pl.BlockSpec(memory_space=pl.ANY)
    return pl.pallas_call(
        functools.partial(reduce_kernel, n, slots),
        out_shape=[
            jax.ShapeDtypeStruct((2, slots) + up_tail, BF),
            jax.ShapeDtypeStruct((2, slots, down_tail[0], half), BF),
            jax.ShapeDtypeStruct(attn_tail, BF),
        ],
        in_specs=[any_spec] * 3,
        out_specs=[any_spec] * 3,
        scratch_shapes=[
            vmem(2 * slots, deep, *up_tail),
            vmem(slots, deep, *down_tail),
            vmem(deep, 2, *attn_tail),
            vmem(2 * slots, deep, *up_tail),
            vmem(slots, deep, *down_tail),
            vmem(deep, *attn_tail),
            vmem(2 * slots, deep - 1, *up_tail),
            vmem(slots, deep - 1, *down_tail),
            vmem(deep - 1, *attn_tail),
            vmem(2 * slots, *up_tail),
            vmem(slots, *down_tail),
            vmem(*attn_tail),
            vmem(deep, 2, *attn_tail),
            sems((count,)),
            sems((count,)),
            sems((count,)),
            sems((count, deep)),
            sems((count, deep)),
            sems((count,)),
            sems((count,)),
            sems((count,)),
        ],
        compiler_params=pltpu.CompilerParams(
            collective_id=1, has_side_effects=True, vmem_limit_bytes=48 << 20
        ),
    )(up_grads, down_grad, attn_grad)


def order_pair(first_is_own, own, other, axis):
    return jnp.where(
        first_is_own, jnp.concatenate([own, other], axis), jnp.concatenate([other, own], axis)
    )


WINDOW = 2


def gather_kernel(n, plan, *refs):
    count = max(item[0] for item in plan) + 1
    pieces, fulls = refs[:count], refs[count : 2 * count]
    own_sem, z_send, z_recv, x_send, x_recv = refs[2 * count :]
    me = lax.axis_index("dp")
    deep = n // 2
    z, x = me // 2, me % 2
    partner = 2 * z + (1 - x)
    peers = [2 * lax.rem(z + k, deep) + x for k in range(1, deep)]
    sources = [2 * lax.rem(z + deep - k, deep) + x for k in range(deep)]

    greet([{"dp": device} for device in peers + [partner]])

    def region(item, owner):
        at, lead, rows = plan[item]
        full = fulls[at]
        for index in lead:
            full = full.at[index]
        if rows == 0:
            return full.at[owner]
        start = owner * rows
        if rows % 16 == 0:
            start = pl.multiple_of(start, 16)
        return full.at[pl.ds(start, rows)]

    def piece(item):
        at, lead, rows = plan[item]
        ref = pieces[at]
        for index in lead:
            ref = ref.at[index]
        return ref

    total = len(plan)
    local_copies = []
    z_copies = [[] for _ in range(total)]
    x_copies = [[] for _ in range(total)]
    for step in range(total + WINDOW):
        if step < total:
            here = region(step, me)
            for k in range(1, deep):
                copy = remote(
                    piece(step), here, z_send.at[step, k], z_recv.at[step, k], {"dp": peers[k - 1]}
                )
                copy.start()
                z_copies[step].append(copy)
            copy = remote(piece(step), here, x_send.at[step, 0], x_recv.at[step, 0], {"dp": partner})
            copy.start()
            x_copies[step].append(copy)
            copy = pltpu.make_async_copy(piece(step), here, own_sem.at[step])
            copy.start()
            local_copies.append(copy)
        if step >= WINDOW:
            item = step - WINDOW
            for k in range(1, deep):
                z_copies[item][k - 1].wait_recv()
                arrived = region(item, sources[k])
                copy = remote(
                    arrived, arrived, x_send.at[item, k], x_recv.at[item, k], {"dp": partner}
                )
                copy.start()
                x_copies[item].append(copy)
    for item in range(total):
        local_copies[item].wait()
        for copy in z_copies[item]:
            copy.wait_send()
        for copy in x_copies[item]:
            copy.wait()


def dp_gather(pieces, fulls, plan):
    n = lax.axis_size("dp")
    total = len(plan)
    sems = pltpu.SemaphoreType.DMA
    return pl.pallas_call(
        functools.partial(gather_kernel, n, plan),
        out_shape=[
            jax.ShapeDtypeStruct(shape, piece.dtype) for shape, piece in zip(fulls, pieces)
        ],
        in_specs=[pl.BlockSpec(memory_space=pl.ANY)] * len(pieces),
        out_specs=[pl.BlockSpec(memory_space=pl.ANY)] * len(fulls),
        scratch_shapes=[
            sems((total,)),
            sems((total, n // 2)),
            sems((total, n // 2)),
            sems((total, n // 2)),
            sems((total, n // 2)),
        ],
        compiler_params=pltpu.CompilerParams(collective_id=0, has_side_effects=True),
    )(*pieces)


TN = (((0,), (0,)), ((), ()))
TILE = 512


def column(values, index):
    return jnp.sum(jnp.where(lanes_of(values.shape) == index, values, 0.0), axis=1, keepdims=True)


def clear(first, ref):
    @pl.when(first)
    def _():
        ref[...] = jnp.zeros(ref.shape, ref.dtype)


def ffn_kernel(tokens, up_own, up_peer, down_own, down_peer, mix, *refs):
    pre, act, out = refs[-3:]
    slot = pl.program_id(0)
    quarter = down_own.shape[1]
    clear(slot == 0, out)
    w_up = jnp.concatenate([up_own[0], up_peer[0]], axis=0)
    w_down = jnp.concatenate([down_own[0], down_peer[0]], axis=1)
    for tile in range(tokens.shape[0] // TILE):
        rows = pl.ds(tile * TILE, TILE)
        both = jnp.dot(tokens[rows], w_up, preferred_element_type=F32)
        pre[0, rows] = both.astype(BF)
        gate, up = both[:, :quarter], both[:, quarter:]
        hidden = gate / (1.0 + jnp.exp(-gate)) * up * column(mix[rows], slot)
        act[0, rows] = hidden.astype(BF)
        out[rows] += jnp.dot(hidden.astype(BF), w_down, preferred_element_type=F32)


def ffn_forward(tokens, up_own, up_peer, down_own, down_peer, mix, part, parts, filled=()):
    slots, half, width = up_own.shape
    rows, depth = tokens.shape
    size = rows // parts
    per_slot = lambda *shape: pl.BlockSpec((1,) + shape, lambda e: (e, 0, 0))
    of_part = lambda *shape: pl.BlockSpec((1,) + shape, lambda e: (e, part, 0))
    whole = lambda *shape: pl.BlockSpec(shape, lambda e: (part, 0))
    return pl.pallas_call(
        ffn_kernel,
        grid=(slots,),
        out_shape=[
            jax.ShapeDtypeStruct((slots, rows, width), BF),
            jax.ShapeDtypeStruct((slots, rows, width // 2), BF),
            jax.ShapeDtypeStruct((size, depth), F32),
        ],
        in_specs=[
            whole(size, depth),
            per_slot(half, width),
            per_slot(half, width),
            per_slot(width // 2, half),
            per_slot(width // 2, half),
            whole(size, 8),
        ]
        + [pl.BlockSpec(memory_space=pl.ANY)] * len(filled),
        out_specs=[
            of_part(size, width),
            of_part(size, width // 2),
            pl.BlockSpec((size, depth), lambda e: (0, 0)),
        ],
        input_output_aliases={6: 0, 7: 1} if filled else {},
        compiler_params=pltpu.CompilerParams(vmem_limit_bytes=56 << 20),
        cost_estimate=pl.CostEstimate(
            flops=3 * slots * size * depth * width,
            bytes_accessed=20 << 20,
            transcendentals=slots * size * width // 2,
        ),
    )(tokens, up_own, up_peer, down_own, down_peer, mix, *filled)


def ffn_back_kernel(grads, pre, down_own, down_peer, mix, *refs):
    pre_grad, gate_sum = refs[-2:]
    slot = pl.program_id(0)
    quarter = down_own.shape[1]
    clear(slot == 0, gate_sum)
    w_down = jnp.concatenate([down_own[0], down_peer[0]], axis=1)
    for tile in range(grads.shape[0] // TILE):
        rows = pl.ds(tile * TILE, TILE)
        back = lax.dot_general(grads[rows], w_down, NT, preferred_element_type=F32)
        gate = pre[0, rows, :quarter].astype(F32)
        up = pre[0, rows, quarter:].astype(F32)
        sigma = 1.0 / (1.0 + jnp.exp(-gate))
        act_silu = gate * sigma
        sums = jnp.sum(back * act_silu * up, axis=1, keepdims=True)
        gate_sum[rows] += jnp.where(lanes_of((TILE, 8)) == slot, sums, 0.0)
        back = back * column(mix[rows], slot)
        pre_grad[0, rows, :quarter] = (back * up * (sigma * (1.0 + gate * (1.0 - sigma)))).astype(BF)
        pre_grad[0, rows, quarter:] = (back * act_silu).astype(BF)


def ffn_backward(grads, pre, down_own, down_peer, mix, part, parts, filled=()):
    slots, rows, width = pre.shape
    size, depth = grads.shape
    per_slot = lambda *shape: pl.BlockSpec((1,) + shape, lambda e: (e, 0, 0))
    of_part = lambda *shape: pl.BlockSpec((1,) + shape, lambda e: (e, part, 0))
    return pl.pallas_call(
        ffn_back_kernel,
        grid=(slots,),
        out_shape=[
            jax.ShapeDtypeStruct((slots, rows, width), BF),
            jax.ShapeDtypeStruct((size, 8), F32),
        ],
        in_specs=[
            pl.BlockSpec((size, depth), lambda e: (0, 0)),
            of_part(size, width),
            per_slot(width // 2, depth // 2),
            per_slot(width // 2, depth // 2),
            pl.BlockSpec((size, 8), lambda e: (part, 0)),
        ]
        + [pl.BlockSpec(memory_space=pl.ANY)] * len(filled),
        out_specs=[of_part(size, width), pl.BlockSpec((size, 8), lambda e: (0, 0))],
        input_output_aliases={5: 0} if filled else {},
        compiler_params=pltpu.CompilerParams(vmem_limit_bytes=56 << 20),
        cost_estimate=pl.CostEstimate(
            flops=2 * slots * size * depth * width,
            bytes_accessed=25 << 20,
            transcendentals=slots * size * width // 2,
        ),
    )(grads, pre, down_own, down_peer, mix, *filled)


def ffn_weights_kernel(near, far, tokens, act, pre_grad, down_grad, up_grad):
    size = near.shape[0]
    total = lax.dot_general(act[0, :size], near[...], TN, preferred_element_type=F32)
    total = total + lax.dot_general(act[0, size:], far[...], TN, preferred_element_type=F32)
    down_grad[0] = total.astype(BF)
    for tile in range(tokens.shape[1] // 256):
        columns = slice(tile * 256, (tile + 1) * 256)
        up_grad[0, columns] = lax.dot_general(
            tokens[:, columns], pre_grad[0], TN, preferred_element_type=F32
        ).astype(BF)


def ffn_weights(near, far, tokens, act, pre_grad):
    slots, rows, width = pre_grad.shape
    depth = tokens.shape[1]
    per_slot = lambda *shape: pl.BlockSpec((1,) + shape, lambda e: (e, 0, 0))
    whole = lambda *shape: pl.BlockSpec(shape, lambda e: (0, 0), pipeline_mode=pl.Buffered(1))
    return pl.pallas_call(
        ffn_weights_kernel,
        grid=(slots,),
        out_shape=[
            jax.ShapeDtypeStruct((slots, width // 2, depth), BF),
            jax.ShapeDtypeStruct((slots, depth, width), BF),
        ],
        in_specs=[
            whole(rows // 2, depth),
            whole(rows // 2, depth),
            whole(rows, depth),
            per_slot(rows, width // 2),
            per_slot(rows, width),
        ],
        out_specs=[per_slot(width // 2, depth), per_slot(depth, width)],
        compiler_params=pltpu.CompilerParams(vmem_limit_bytes=56 << 20),
        cost_estimate=pl.CostEstimate(
            flops=3 * slots * rows * depth * width, bytes_accessed=50 << 20, transcendentals=0
        ),
    )(near, far, tokens, act, pre_grad)


def ffn_input_kernel(pre_grad, up_own, up_peer, out):
    clear(pl.program_id(0) == 0, out)
    w_up = jnp.concatenate([up_own[0], up_peer[0]], axis=0)
    for tile in range(out.shape[0] // TILE):
        rows = pl.ds(tile * TILE, TILE)
        out[rows] += lax.dot_general(pre_grad[0, rows], w_up, NT, preferred_element_type=F32)


def ffn_input(pre_grad, up_own, up_peer, part, parts):
    slots, rows, width = pre_grad.shape
    half = up_own.shape[1]
    depth = 2 * half
    rows = rows // parts
    return pl.pallas_call(
        ffn_input_kernel,
        grid=(slots,),
        out_shape=jax.ShapeDtypeStruct((rows, depth), F32),
        in_specs=[
            pl.BlockSpec((1, rows, width), lambda e: (e, part, 0)),
            pl.BlockSpec((1, half, width), lambda e: (e, 0, 0)),
            pl.BlockSpec((1, half, width), lambda e: (e, 0, 0)),
        ],
        out_specs=pl.BlockSpec((rows, depth), lambda e: (0, 0)),
        compiler_params=pltpu.CompilerParams(vmem_limit_bytes=40 << 20),
        cost_estimate=pl.CostEstimate(
            flops=2 * slots * rows * depth * width, bytes_accessed=20 << 20, transcendentals=0
        ),
    )(pre_grad, up_own, up_peer)


def join_core(parts):
    size = parts.shape[0] // 2
    return parts[:size] + swap(parts[size:].astype(BF), "col").astype(F32)


def collect_tokens(far, near_of, operand):
    send = flip(join_core(far).astype(BF))
    send, operand = lax.optimization_barrier((send, operand))
    recv = swap(send, "row")
    near, *rest = near_of(operand)
    near, recv = lax.optimization_barrier((near, recv))
    return (join_core(near) + recv.astype(F32), *rest)


def from_sequence(values, r, c):
    half = values.shape[1] // 2
    own, peer = values[:, :half], values[:, half:]
    diag = r == c
    send = jnp.where(diag, peer, own)
    kept = jnp.where(diag, own, peer)
    recv = swap(send, "col")
    whole = order_pair(c == 0, kept, recv, 0)
    moved = lax.ppermute(whole, ("row", "col"), [(1, 2), (2, 1)])
    return jnp.where(diag, whole, moved)


def local(
    layer_input,
    teacher,
    valid_mask,
    routes,
    segments,
    gain_attn,
    gain_ffn,
    w_qkv,
    w_out,
    w_router,
    w_shared_up,
    w_shared_down,
    w_expert_up,
    w_expert_down,
):
    r = lax.axis_index("row")
    c = lax.axis_index("col")
    n_dp = lax.axis_size("dp")
    rows = layer_input.shape[0]
    part = rows // 2
    half = layer_input.shape[1]
    heads = w_qkv.shape[2] // HEAD_DIM
    ff = w_shared_up.shape[2]
    quarter = ff // 2
    slots = E + 1

    seg = lax.dynamic_slice_in_dim(segments, r, 1, 0)[0]
    seg_row, seg_col = seg[None, :], seg[:, None]
    tables = rope_tables(rows)
    w_qkv = w_qkv.swapaxes(0, 1)
    vectors = jnp.concatenate(
        [gain_attn[None], gain_ffn[None], w_router.T.astype(F32), jnp.zeros((6 - E, half), F32)]
    )
    (
        queries, keys_rot, values_low, context_low, normed_attn, x_own, hidden,
        w_qkv_peer, w_out_peer, vec_peer, up_own, tokens, up_peer, down_peer, teacher_pair,
    ) = front(
        layer_input, teacher, w_qkv, w_out, vectors, w_shared_up, w_expert_up, w_shared_down, w_expert_down,
        tables, seg,
    )

    vectors = jnp.concatenate([vectors, vec_peer], axis=1)
    gain_a, gain_f, w_r = vectors[0], vectors[1], vectors[2 : 2 + E].astype(BF).T
    teacher_own = jnp.concatenate([teacher_pair[0], teacher_pair[1]], axis=1).astype(F32)
    valid_other = swap(valid_mask, "col")
    valid_seq = jnp.where(r == c, valid_mask, valid_other).astype(F32)
    valid_own = lax.dynamic_slice_in_dim(valid_seq, c * part, part, 0)
    route_blocks = routes.reshape(2, 2, part, 2)
    route_blocks = jnp.where(r == 0, route_blocks, route_blocks[::-1])
    route_blocks = jnp.where(c == 0, route_blocks, route_blocks[:, ::-1]).reshape(4 * part, 2)
    picks = (route_blocks[:, :, None] == jnp.arange(E, dtype=jnp.int32)[None, None, :]).astype(F32)

    down_own = jnp.concatenate([w_shared_down[None], w_expert_down])
    down_own = lax.dynamic_slice_in_dim(down_own, r * quarter, quarter, 1)

    x_own = jnp.concatenate([x_own[0], x_own[1]], axis=1).astype(F32)
    rstd_attn = lax.rsqrt(jnp.mean(x_own * x_own, axis=1) + 1e-06)

    rstd_ffn = lax.rsqrt(jnp.mean(hidden * hidden, axis=1) + 1e-06)
    normed_low = tokens[0]
    tokens = tokens.reshape(4 * part, D)
    logits = jnp.dot(tokens, w_r, preferred_element_type=F32)
    chosen = jnp.sum(picks * logits[:, None, :], axis=2)
    chosen = chosen - jnp.max(chosen, axis=1, keepdims=True)
    gates = jnp.exp(chosen)
    gates = gates / jnp.sum(gates, axis=1, keepdims=True)
    mixing = jnp.sum(picks * gates[:, :, None], axis=1)
    mix = jnp.concatenate(
        [jnp.ones((4 * part, 1), F32), mixing, jnp.zeros((4 * part, 7 - E), F32)], axis=1
    )
    weights = (up_own, up_peer, down_own, down_peer)
    pre, act, far = ffn_forward(tokens, *weights, mix, 1, 2)

    def near_forward(operand):
        pre, act, near = ffn_forward(operand[0], *weights, mix, 0, 2, operand[1:])
        return near, pre, act

    branch, pre, act = collect_tokens(far, near_forward, (tokens, pre, act))
    output = hidden + branch

    error = output - teacher_own
    loss_part = jnp.sum(valid_own * jnp.sum(error * error, axis=1))
    grad_out = valid_own[:, None] * error

    low_own = grad_out.astype(BF)
    far = swap(flip(low_own), "row")
    near = jnp.concatenate([low_own, swap(low_own, "col")])
    pre_grad, near_sums = ffn_backward(near, pre, down_own, down_peer, mix, 0, 2)
    pre_grad, far = lax.optimization_barrier((pre_grad, far))
    far = jnp.concatenate([far, swap(far, "col")])
    pre_grad, far_sums = ffn_backward(far, pre, down_own, down_peer, mix, 1, 2, (pre_grad,))
    gate_parts = jnp.concatenate([near_sums, far_sums])[:, 1 : E + 1].T.reshape(E, 4, part)
    recv = swap(jnp.stack([gate_parts[:, 1], gate_parts[:, 3]]), "col")
    gate_grad = gate_parts[:, 0] + recv[0] + swap(gate_parts[:, 2] + recv[1], "row")
    down_grad, up_grad = ffn_weights(near, far, tokens, act, pre_grad)
    pre_grad, gate_grad, up_grad = lax.optimization_barrier((pre_grad, gate_grad, up_grad))
    far = ffn_input(pre_grad, up_own, up_peer, 1, 2)
    (normed_ffn_grad,) = collect_tokens(
        far, lambda operand: (ffn_input(operand, up_own, up_peer, 0, 2),), pre_grad
    )
    mix_own = mixing[:part].T
    centre = jnp.sum(mix_own * gate_grad, axis=0, keepdims=True)
    logit_grad = (mix_own * (gate_grad - centre)).T.astype(BF)
    normed_ffn_grad = normed_ffn_grad + jnp.dot(logit_grad, w_r.T, preferred_element_type=F32)
    router_grad = jnp.dot(normed_low.T, logit_grad, preferred_element_type=F32)
    hidden_back, gain_ffn_grad = norm_backward(hidden, rstd_ffn, gain_f, normed_ffn_grad)
    hidden_grad = grad_out + hidden_back

    low_own = hidden_grad.astype(BF)
    low_seq = order_pair(c == 0, low_own, swap(low_own, "col"), 0)
    w_out_grad = jnp.dot(context_low.T, low_seq, preferred_element_type=F32).astype(BF)
    w_out_full = jnp.concatenate([w_out, w_out_peer], axis=1)
    w_qkv_full = jnp.concatenate([w_qkv, w_qkv_peer], axis=1)
    normed_attn = jnp.concatenate([normed_attn[0], normed_attn[1]], axis=1)
    context_grad = jnp.dot(low_seq, w_out_full.T, preferred_element_type=F32)
    context_grad = context_grad.astype(BF)
    qkv_grad = jnp.concatenate(
        [
            attend_backward(
                queries, keys_rot, values_low, context_grad, tables, seg_row, seg_col, pair, 1
            )
            for pair in range(heads // 2)
        ],
        axis=2,
    )
    w_qkv_grad = jnp.einsum(
        "td,kte->dke", normed_attn, qkv_grad, preferred_element_type=F32
    ).astype(BF)
    back_part = jnp.einsum("kte,kde->td", qkv_grad, w_qkv_full, preferred_element_type=F32)
    back_halves = back_part.reshape(2, part, D)
    back_keep = lax.dynamic_index_in_dim(back_halves, c, 0, keepdims=False)
    back_send = lax.dynamic_index_in_dim(back_halves, 1 - c, 0, keepdims=False)
    normed_attn_grad = back_keep + swap(back_send.astype(BF), "col").astype(F32)
    input_back, gain_attn_grad = norm_backward(x_own, rstd_attn, gain_a, normed_attn_grad)
    input_grad = hidden_grad + input_back

    owner_f = quarter // n_dp
    owner_d = half // n_dp
    deep = n_dp // 2
    grad_pair = jnp.concatenate(
        [
            w_qkv_grad.reshape(2, n_dp, owner_d, 3, half),
            w_out_grad.reshape(n_dp, owner_d, 2, half).transpose(2, 0, 1, 3)[:, :, :, None],
        ],
        axis=3,
    ).transpose(0, 1, 3, 2, 4)
    up_pair, down_pair, attn_piece = dp_reduce(
        up_grad.reshape(slots, 2, deep, 2, owner_d, 2 * quarter),
        down_grad.reshape(slots, deep, 2, owner_f, D),
        grad_pair.reshape(2, deep, 2, 4 * owner_d, half),
    )
    attn_piece = attn_piece.reshape(4, owner_d, half)
    down_piece = jnp.where(r == 0, down_pair, down_pair[::-1]).swapaxes(0, 1)
    up_pair = up_pair.reshape(2, slots, owner_d, 2, quarter)
    up_piece = order_pair(r == 0, up_pair[0], up_pair[1], 3)

    small = jnp.concatenate([gain_attn_grad[None], gain_ffn_grad[None], router_grad.T], axis=0)
    small = jnp.where(r == 0, small, flip(small))
    loss_row = jnp.full((1, D), loss_part).at[0, half:].set(jnp.sum(valid_own))
    small = jnp.concatenate([small, loss_row, jnp.zeros((1, D), F32)])
    small = small + swap(small, "row")
    small = small + swap(small, "col")
    plan = [(1, (), owner_d), (3, (0,), owner_f), (3, (1,), owner_f)]
    for e in range(E):
        plan += [(0, (e,), owner_d), (2, (e, 0), owner_f), (2, (e, 1), owner_f)]
    plan += [(4, (), 0), (5, (), 0)]
    up_full, shared_up_full, down_full, shared_down_full, attn_full, small_full = dp_gather(
        (up_piece[1:], up_piece[0], down_piece[1:], down_piece[0], attn_piece, small),
        (
            (E, half, 2, ff),
            (half, 2, ff),
            (E, 2, quarter, half),
            (2, quarter, half),
            (n_dp, 4, owner_d, half),
            (n_dp, E + 4, D),
        ),
        tuple(plan),
    )
    small = jnp.sum(small_full, axis=0)
    count = small[E + 2, half]
    loss = small[E + 2, 0] / (2.0 * count)
    scale = part * 4 * n_dp / count
    small = small[: E + 2] * scale
    attn_full = attn_full.swapaxes(0, 1).reshape(4, half, half).astype(F32) * scale
    small = lax.dynamic_slice_in_dim(small, r * half, half, 1)
    return (
        from_sequence(output, r, c),
        loss,
        from_sequence(input_grad, r, c) * scale,
        small[0],
        small[1],
        attn_full[:3].swapaxes(0, 1),
        attn_full[3],
        small[2:].T,
        shared_up_full.astype(F32) * scale,
        shared_down_full.reshape(ff, half).astype(F32) * scale,
        up_full.astype(F32) * scale,
        down_full.reshape(E, ff, half).astype(F32) * scale,
    )


def solution(mesh):
    return jax.shard_map(
        local,
        mesh=mesh,
        in_specs=(
            P(("dp", "col"), "row"),
            P(("dp", "col"), "row"),
            P(("dp", "col")),
            P("dp", None),
            P("dp", None),
            P("row"),
            P("row"),
            P("row", None, "col"),
            P("col", "row"),
            P("row", None),
            P("row", None, "col"),
            P("col", "row"),
            P(None, "row", None, "col"),
            P(None, "col", "row"),
        ),
        out_specs=(
            P(("dp", "col"), "row"),
            P(),
            P(("dp", "col"), "row"),
            P("row"),
            P("row"),
            P("row", None, "col"),
            P("col", "row"),
            P("row", None),
            P("row", None, "col"),
            P("col", "row"),
            P(None, "row", None, "col"),
            P(None, "col", "row"),
        ),
        check_vma=False,
    )
```

```python
import functools

import jax
import jax.numpy as jnp
from jax import lax
from jax.experimental import pallas as pl
from jax.experimental.pallas import tpu as pltpu
from jax.sharding import PartitionSpec as P

D = 768
HEAD_DIM = 64
E = 4
LEN = 1024
ABLOCK = 256
BF = jnp.bfloat16
F32 = jnp.float32


def norm_backward(values, rstd_rows, gain_vec, incoming):
    scaled = incoming * gain_vec
    inner_sum = jnp.sum(scaled * values, axis=1)
    gain_grad = jnp.sum(incoming * values * rstd_rows[:, None], axis=0)
    result = rstd_rows[:, None] * scaled - values * (rstd_rows**3 * inner_sum / D)[:, None]
    return (result, gain_grad)


def rope_tables(length):
    half_dim = HEAD_DIM // 2
    freqs = 10000.0 ** (-jnp.arange(half_dim, dtype=F32) * 2.0 / HEAD_DIM)
    angles = jnp.arange(length, dtype=F32)[:, None] * freqs[None, :]
    sine = jnp.sin(angles)
    return (jnp.tile(jnp.cos(angles), (1, 4)), jnp.tile(jnp.concatenate([-sine, sine], axis=1), (1, 2)))


def lanes_of(shape):
    return lax.broadcasted_iota(jnp.int32, shape, len(shape) - 1)


def turn(values, first):
    half_dim = HEAD_DIM // 2
    return jnp.where(
        first,
        pltpu.roll(values, PAIR - half_dim, values.ndim - 1),
        pltpu.roll(values, half_dim, values.ndim - 1),
    )


PAIR = 2 * HEAD_DIM
NT = (((1,), (1,)), ((), ()))


def shares_of(key_pair, query_head, seg_col, seg_row):
    scores = lax.dot_general(key_pair, query_head, NT, preferred_element_type=F32)
    scores = jnp.where(seg_col == seg_row, scores, -1e30)
    weight = jnp.exp(scores - jnp.max(scores, axis=0, keepdims=True))
    return weight * (1.0 / jnp.sum(weight, axis=0, keepdims=True))


LAG = 3


def front_kernel(
    n, x_in, teacher, w_qkv, w_out, vectors, shared_up, expert_up, shared_down, expert_down,
    cosine, sine, seg_row, seg_col,
    queries, keys, values, context, normed, x_own, hidden, w_qkv_peer, w_out_peer, vec_peer, up_own,
    tokens, up_peer, down_peer, teacher_pair,
    x_pair, teacher_in, qkv_own, out_own, up_raw, part_raw, up_part, pre, att_send, att_recv, low, low_flip,
    own_sem, x_send, x_recv, w_send, w_recv, t_send, t_recv,
):
    me = lax.axis_index("dp")
    row, col = lax.axis_index("row"), lax.axis_index("col")
    z, x = me // 2, me % 2
    low_z = lax.rem(z, 2)
    x_peer = {"dp": 2 * z + (1 - x)}
    z_peer = {"dp": 2 * (z + 1 - 2 * low_z) + x}
    row_peer, core = {"row": 1 - row}, {"col": 1 - col}
    mine = 2 * low_z + x
    of_x, of_z = 2 * low_z + (1 - x), 2 * (1 - low_z) + x
    rows, half = x_in.shape
    part = rows // 2
    quarter = shared_up.shape[2] // 2
    slots = expert_up.shape[0] + 1
    greet([row_peer, core, x_peer, z_peer])

    def split(index, size):
        return pl.ds(pl.multiple_of(index * size, 16), size)

    def source(item, index):
        if item == 0:
            return w_qkv.at[:, split(index, half // 4)]
        if item == 1:
            return w_out.at[split(index, w_out.shape[0] // 4)]
        slot, kind = (item - 2) // 2, (item - 2) % 2
        if kind == 0:
            return up_part.at[slot]
        ref = shared_down if slot == 0 else expert_down.at[slot - 1]
        first = (1 - row) * quarter + index * (quarter // 4)
        return ref.at[pl.ds(pl.multiple_of(first, 16), quarter // 4)]

    def landing(item, index):
        if item == 0:
            return w_qkv_peer.at[:, split(index, half // 4)]
        if item == 1:
            return w_out_peer.at[split(index, w_out.shape[0] // 4)]
        slot, kind = (item - 2) // 2, (item - 2) % 2
        if kind == 0:
            return up_peer.at[slot, split(index, half // 4)]
        return down_peer.at[slot, split(index, quarter // 4)]

    count = 2 + 2 * slots
    copies = {}

    def start(item, leg, src, device, index):
        copy = remote(
            src, landing(item, index), w_send.at[item, leg], w_recv.at[item, leg], device
        )
        copy.start()
        copies[item, leg] = copy

    def fetch(item):
        start(item, 0, source(item, mine), row_peer, mine)

    def pass_on(item):
        copies[item, 0].wait_recv()
        start(item, 1, landing(item, mine), x_peer, mine)
        start(item, 2, landing(item, mine), z_peer, mine)

    def by_x(item):
        return (item - item // 4) % 2 == 0

    def pass_far(item):
        if by_x(item):
            copies[item, 1].wait_recv()
            start(item, 3, landing(item, of_x), z_peer, of_x)
        else:
            copies[item, 2].wait_recv()
            start(item, 3, landing(item, of_z), x_peer, of_z)

    def arrive(item):
        copies[item, 2 if by_x(item) else 1].wait_recv()
        copies[item, 3].wait_recv()

    progress = [0]

    def pump():
        at = progress[0]
        progress[0] += 1
        if 2 <= at < count:
            pass_on(at)
        if 2 <= at - LAG < count:
            pass_far(at - LAG)

    diagonal = row == col
    over_row = remote(x_in, x_pair.at[1], x_send.at[0], x_recv.at[0], row_peer)
    across_own = remote(x_in, x_pair.at[0], x_send.at[1], x_recv.at[1], core)
    across_peer = remote(x_pair.at[1], x_pair.at[1], x_send.at[2], x_recv.at[2], core)
    own_x = pltpu.make_async_copy(x_in, x_pair.at[0], own_sem.at[0])

    fetch(0)

    @pl.when(diagonal)
    def _():
        own_x.start()
        across_own.start()

    @pl.when(jnp.logical_not(diagonal))
    def _():
        over_row.start()

    def up_slot(slot):
        return shared_up if slot == 0 else expert_up.at[slot - 1]

    keep_lanes = pl.ds(pl.multiple_of(row * quarter, 128), quarter)
    send_lanes = pl.ds(pl.multiple_of((1 - row) * quarter, 128), quarter)
    part_loads, up_loads = [], []
    for slot in range(slots):
        piece = up_slot(slot).at[pl.ds(mine * (half // 4), half // 4), :, send_lanes]
        part_loads.append(pltpu.make_async_copy(piece, part_raw.at[slot], own_sem.at[4 + slot]))
        part_loads[slot].start()

    def split_own(slot):
        up_loads[slot].wait()
        for k in range(2):
            up_own[slot, :, k * quarter : (k + 1) * quarter] = up_raw[slot, :, k]

    give_vectors = remote(vectors, vec_peer, x_send.at[3], x_recv.at[3], row_peer)
    give_vectors.start()
    fetch(1)
    own_qkv = pltpu.make_async_copy(w_qkv, qkv_own, own_sem.at[1])
    own_qkv.start()
    own_out = pltpu.make_async_copy(w_out, out_own, own_sem.at[2])
    own_out.start()

    goal_row = remote(teacher, teacher_in, x_send.at[4], x_recv.at[4], row_peer)
    goal_own = remote(
        teacher.at[split(1 - col, part)], teacher_pair.at[0], x_send.at[5], x_recv.at[5], core
    )
    goal_peer = remote(
        teacher_in.at[split(1 - col, part)], teacher_pair.at[1], x_send.at[6], x_recv.at[6], core
    )
    keep_own = pltpu.make_async_copy(
        teacher.at[split(col, part)], teacher_pair.at[0], own_sem.at[4 + 2 * slots]
    )
    keep_peer = pltpu.make_async_copy(
        teacher_in.at[split(col, part)], teacher_pair.at[1], own_sem.at[5 + 2 * slots]
    )

    for slot in range(slots):
        piece = up_slot(slot).at[:, :, keep_lanes]
        up_loads.append(
            pltpu.make_async_copy(piece, up_raw.at[slot], own_sem.at[4 + slots + slot])
        )
        up_loads[slot].start()
    for slot in range(slots):
        part_loads[slot].wait()
        for k in range(2):
            up_part[slot, :, k * quarter : (k + 1) * quarter] = part_raw[slot, :, k]

    @pl.when(diagonal)
    def _():
        over_row.wait_recv()
        across_peer.start()
        own_x.wait()

    @pl.when(jnp.logical_not(diagonal))
    def _():
        over_row.wait_send()

    for item in range(2, count):
        fetch(item)

    @pl.when(diagonal)
    def _():
        goal_own.start()
        keep_own.start()

    @pl.when(jnp.logical_not(diagonal))
    def _():
        goal_row.start()

    pass_on(0)
    pass_on(1)
    split_own(0)

    @pl.when(jnp.logical_not(diagonal))
    def _():
        across_own.wait_recv()
        across_peer.wait_recv()

    give_vectors.wait_recv()
    progress[0] = 2
    x_first, x_second = x_pair[0].astype(F32), x_pair[1].astype(F32)
    squares = jnp.sum(x_first * x_first, axis=1, keepdims=True)
    squares = squares + jnp.sum(x_second * x_second, axis=1, keepdims=True)
    rstd = lax.rsqrt(squares / (2 * half) + 1e-06)
    normed[0] = (x_first * rstd * vectors[0:1]).astype(BF)
    normed[1] = (x_second * rstd * vec_peer[0:1]).astype(BF)
    pass_far(0)
    pass_far(1)
    for slot in range(1, slots):
        split_own(slot)
    arrive(0)
    own_qkv.wait()
    for j in range(3):
        pre[j] = jnp.dot(normed[0], qkv_own[j], preferred_element_type=F32) + jnp.dot(
            normed[1], w_qkv_peer[j], preferred_element_type=F32
        )
        pump()

    first = lanes_of((rows, PAIR)) % HEAD_DIM < HEAD_DIM // 2
    lower = lanes_of((ABLOCK, PAIR)) < HEAD_DIM
    cos, sin = cosine[...], sine[...]
    for pair in range(half // PAIR):
        lanes = slice(pair * PAIR, (pair + 1) * PAIR)
        query = pre[0, :, lanes]
        queries[:, lanes] = ((query * cos + turn(query, first) * sin) * HEAD_DIM**-0.5).astype(BF)
        key = pre[1, :, lanes]
        keys[:, lanes] = (key * cos + turn(key, first) * sin).astype(BF)
        value = pre[2, :, lanes]
        values[:, lanes] = value.astype(BF)
        value_t = value.T.astype(BF)
        for block in range(rows // ABLOCK):
            begin, stop = block * ABLOCK, (block + 1) * ABLOCK
            query = queries[begin:stop, lanes]
            parts = []
            for head in range(2):
                query_head = jnp.where(lower == (head == 0), query, jnp.zeros_like(query))
                shares = shares_of(
                    keys[:stop, lanes], query_head, seg_col[:stop], seg_row[:, begin:stop]
                ).astype(BF)
                parts.append(jnp.dot(value_t[:, :stop], shares, preferred_element_type=F32))
            both = jnp.concatenate([parts[0][:HEAD_DIM], parts[1][HEAD_DIM:]], axis=0)
            context[begin:stop, lanes] = both.T.astype(BF)
            if block % 2 == 1:
                pump()

    arrive(1)
    own_out.wait()
    there, here = split(1 - col, part), split(col, part)
    for at, weight in enumerate((out_own, w_out_peer)):
        att_send[:, at * half : (at + 1) * half] = jnp.dot(
            context[there], weight[...], preferred_element_type=F32
        ).astype(BF)
    swap_att = remote(att_send, att_recv, t_send.at[0], t_recv.at[0], core)
    swap_att.start()
    pump()
    for at, weight in enumerate((out_own, w_out_peer)):
        lanes = slice(at * half, (at + 1) * half)
        x_own[at] = x_pair[at, here]
        hidden[:, lanes] = x_own[at].astype(F32) + jnp.dot(
            context[here], weight[...], preferred_element_type=F32
        )
    swap_att.wait_recv()
    total = hidden[...] + att_recv[...].astype(F32)
    hidden[...] = total
    rstd = lax.rsqrt(jnp.mean(total * total, axis=1, keepdims=True) + 1e-06)
    gains = jnp.concatenate([vectors[1:2], vec_peer[1:2]], axis=1)
    total = (total * rstd * gains).astype(BF)
    low[...] = total
    low_flip[:, :half] = total[:, half:]
    low_flip[:, half:] = total[:, :half]
    own_tokens = pltpu.make_async_copy(low, tokens.at[0], own_sem.at[3])
    own_tokens.start()
    far = remote(low_flip, tokens.at[2], t_send.at[1], t_recv.at[1], row_peer)
    far.start()
    near = remote(low, tokens.at[1], t_send.at[2], t_recv.at[2], core)
    near.start()
    while progress[0] < count + LAG:
        pump()

    @pl.when(diagonal)
    def _():
        goal_row.wait_recv()
        goal_peer.start()
        keep_peer.start()

    far.wait_recv()
    far_near = remote(tokens.at[2], tokens.at[3], t_send.at[3], t_recv.at[3], core)
    far_near.start()
    for item in range(2, count):
        arrive(item)
    near.wait_recv()
    far_near.wait_recv()
    own_tokens.wait()
    for copy in (give_vectors, swap_att, far, near, far_near, *copies.values()):
        copy.wait_send()

    @pl.when(diagonal)
    def _():
        across_own.wait_send()
        across_peer.wait_send()
        goal_own.wait_send()
        goal_peer.wait_send()
        keep_own.wait()
        keep_peer.wait()

    @pl.when(jnp.logical_not(diagonal))
    def _():
        goal_row.wait_send()
        goal_own.wait_recv()
        goal_peer.wait_recv()


def front(x_in, teacher, w_qkv, w_out, vectors, shared_up, expert_up, shared_down, expert_down, tables, seg):
    n = lax.axis_size("dp")
    rows, half = x_in.shape
    quarter = shared_up.shape[2] // 2
    slots = expert_up.shape[0] + 1
    count = 2 + 2 * slots
    sems = pltpu.SemaphoreType.DMA
    any_spec = pl.BlockSpec(memory_space=pl.ANY)
    vmem_spec = pl.BlockSpec(memory_space=pltpu.VMEM)
    shape = jax.ShapeDtypeStruct
    wide = w_out.shape[0]
    return pl.pallas_call(
        functools.partial(front_kernel, n),
        out_shape=[shape((rows, wide), BF)] * 4
        + [
            shape((2, rows, half), BF),
            shape((2, rows // 2, half), BF),
            shape((rows // 2, 2 * half), F32),
            shape(w_qkv.shape, BF),
            shape(w_out.shape, BF),
            shape(vectors.shape, F32),
            shape((slots, half, 2 * quarter), BF),
            shape((4, rows // 2, 2 * half), BF),
            shape((slots, half, 2 * quarter), BF),
            shape((slots, quarter, half), BF),
            shape((2, rows // 2, half), BF),
        ],
        in_specs=[any_spec] * 4 + [vmem_spec] + [any_spec] * 4 + [vmem_spec] * 4,
        out_specs=[vmem_spec] * 11 + [any_spec] * 4,
        scratch_shapes=[
            pltpu.VMEM((2, rows, half), BF),
            pltpu.VMEM((rows, half), BF),
            pltpu.VMEM(w_qkv.shape, BF),
            pltpu.VMEM(w_out.shape, BF),
            pltpu.VMEM((slots, half, 2, quarter), BF),
            pltpu.VMEM((slots, half // 4, 2, quarter), BF),
            pltpu.VMEM((slots, half // 4, 2 * quarter), BF),
            pltpu.VMEM((3, rows, wide), F32),
            pltpu.VMEM((rows // 2, 2 * half), BF),
            pltpu.VMEM((rows // 2, 2 * half), BF),
            pltpu.VMEM((rows // 2, 2 * half), BF),
            pltpu.VMEM((rows // 2, 2 * half), BF),
            sems((6 + 2 * slots,)),
            sems((7,)),
            sems((7,)),
            sems((count, 4)),
            sems((count, 4)),
            sems((4,)),
            sems((4,)),
        ],
        compiler_params=pltpu.CompilerParams(
            collective_id=2, has_side_effects=True, vmem_limit_bytes=48 << 20
        ),
    )(
        x_in, teacher, w_qkv, w_out, vectors, shared_up, expert_up, shared_down, expert_down,
        tables[0], tables[1], seg[None, :], seg[:, None],
    )


def attend_back_kernel(
    queries, keys, values, context_grad, cosine, sine, seg_row, seg_col, out, key_sum, value_sum
):
    rows = queries.shape[0]
    key_t = keys[...].astype(F32).T.astype(BF)
    lower = lanes_of((ABLOCK, PAIR)) < HEAD_DIM
    first = lanes_of((ABLOCK, PAIR)) % HEAD_DIM < HEAD_DIM // 2
    for block in reversed(range(rows // ABLOCK)):
        start, stop = block * ABLOCK, (block + 1) * ABLOCK
        query, incoming = queries[start:stop], context_grad[start:stop]
        parts, key_part, value_part = [], None, None
        for head in range(2):
            mine = lower == (head == 0)
            query_head = jnp.where(mine, query, jnp.zeros_like(query))
            incoming_head = jnp.where(mine, incoming, jnp.zeros_like(incoming))
            shares = shares_of(keys[:stop], query_head, seg_col[:stop], seg_row[:, start:stop])
            share_grad = lax.dot_general(
                values[:stop], incoming_head, NT, preferred_element_type=F32
            )
            centre = jnp.sum(shares * share_grad, axis=0, keepdims=True)
            score_grad = (shares * (share_grad - centre)).astype(BF)
            parts.append(jnp.dot(key_t[:, :stop], score_grad, preferred_element_type=F32))
            more = jnp.dot(shares.astype(BF), incoming_head, preferred_element_type=F32)
            value_part = more if head == 0 else value_part + more
            more = jnp.dot(score_grad, query_head, preferred_element_type=F32)
            key_part = more if head == 0 else key_part + more
        both = jnp.concatenate([parts[0][:HEAD_DIM], parts[1][HEAD_DIM:]], axis=0)
        grad = both.T * HEAD_DIM**-0.5
        cos, sin = cosine[start:stop], sine[start:stop]
        out[0, start:stop] = (grad * cos + turn(grad * sin, first)).astype(BF)
        if stop == rows:
            key_sum[...] = key_part
            value_sum[...] = value_part
        else:
            key_sum[:stop] += key_part
            value_sum[:stop] += value_part
    for block in range(rows // ABLOCK):
        start, stop = block * ABLOCK, (block + 1) * ABLOCK
        grad = key_sum[start:stop]
        cos, sin = cosine[start:stop], sine[start:stop]
        out[1, start:stop] = (grad * cos + turn(grad * sin, first)).astype(BF)
        out[2, start:stop] = value_sum[start:stop].astype(BF)


def attend_backward(queries, keys, values, context_grad, tables, seg_row, seg_col, first_pair, pairs):
    rows = queries.shape[0]
    block = pl.BlockSpec((rows, PAIR), lambda i: (0, i + first_pair))
    whole = pl.BlockSpec((rows, PAIR), lambda i: (0, 0))
    return pl.pallas_call(
        attend_back_kernel,
        grid=(pairs,),
        out_shape=jax.ShapeDtypeStruct((3, rows, pairs * PAIR), BF),
        in_specs=[block] * 4
        + [
            whole,
            whole,
            pl.BlockSpec((1, rows), lambda i: (0, 0)),
            pl.BlockSpec((rows, 1), lambda i: (0, 0)),
        ],
        out_specs=pl.BlockSpec((3, rows, PAIR), lambda i: (0, 0, i)),
        scratch_shapes=[pltpu.VMEM((rows, PAIR), F32), pltpu.VMEM((rows, PAIR), F32)],
        compiler_params=pltpu.CompilerParams(vmem_limit_bytes=40 << 20),
        cost_estimate=pl.CostEstimate(
            flops=pairs * 14_000_000_000, bytes_accessed=4 << 20, transcendentals=2 << 20
        ),
    )(queries, keys, values, context_grad, tables[0], tables[1], seg_row, seg_col)


def swap(values, axis):
    return lax.ppermute(values, axis, [(0, 1), (1, 0)])


def flip(values):
    half = values.shape[-1] // 2
    return jnp.concatenate([values[..., half:], values[..., :half]], axis=-1)


def remote(src, dst, send, recv, device):
    return pltpu.make_async_remote_copy(
        src_ref=src,
        dst_ref=dst,
        send_sem=send,
        recv_sem=recv,
        device_id=device,
        device_id_type=pl.DeviceIdType.MESH,
    )


def greet(devices):
    barrier = pltpu.get_barrier_semaphore()
    for device in devices:
        pl.semaphore_signal(
            barrier, inc=1, device_id=device, device_id_type=pl.DeviceIdType.MESH
        )
    pl.semaphore_wait(barrier, len(devices))


BESIDE = 2
AHEAD = 3
BEHIND = 3


def reduce_kernel(n, slots, *refs):
    ups, attn, up_out, attn_out = refs[:4]
    (
        up_keep, attn_keep, up_x, attn_x, up_z, attn_z, up_done, attn_done, attn_y,
        keep_sem, x_send, x_recv, z_send, z_recv, out_sem, y_send, y_recv,
    ) = refs[4:]
    me = lax.axis_index("dp")
    row = lax.axis_index("row")
    deep = n // 2
    z, x = me // 2, me % 2
    partner = {"dp": 2 * z + (1 - x)}
    peer = {"row": 1 - row}
    ahead = [lax.rem(z + k, deep) for k in range(deep)]
    greet([partner, peer] + [{"dp": 2 * ahead[k] + x} for k in range(1, deep)])

    items = [("up", 2 * e + h) for e in range(slots) for h in (1, 0)]
    items += [("attn", 0)]
    count = len(items)
    last = count - 1

    def buffers(item):
        kind, at = items[item]
        if kind == "up":
            return ups.at[BESIDE + at // 2, at % 2], up_keep.at[at], up_x.at[at], up_z.at[at], up_done.at[at]
        return None, attn_keep.at[:, x], attn_x, attn_z, attn_done

    y_first = remote(attn.at[1], attn_y, y_send.at[last], y_recv.at[last], peer)
    y_first.start()
    attn_load = pltpu.make_async_copy(attn.at[0], attn_keep, keep_sem.at[last])
    attn_load.start()
    loads, x_copies, z_copies, outs, y_copies = {}, {}, {}, [], [y_first]
    for item in range(last):
        source, keep, _, _, _ = buffers(item)
        loads[item] = pltpu.make_async_copy(source.at[:, x], keep, keep_sem.at[item])
        loads[item].start()

    def send_x(item):
        source, keep, landing, _, _ = buffers(item)
        if item == last:
            attn_load.wait()
            y_first.wait_recv()
            attn_keep[...] = (attn_keep[...].astype(F32) + attn_y[...].astype(F32)).astype(BF)
            given = attn_keep.at[:, 1 - x]
        else:
            given = source.at[:, 1 - x]
        x_copies[item] = remote(given, landing, x_send.at[item], x_recv.at[item], partner)
        x_copies[item].start()

    def send_z(item):
        _, keep, landing, arrivals, _ = buffers(item)
        if item in loads:
            loads[item].wait()
        x_copies[item].wait_recv()
        keep[...] = (keep[...].astype(F32) + landing[...].astype(F32)).astype(BF)
        for k in range(1, deep):
            copy = remote(
                keep.at[ahead[k]],
                arrivals.at[k - 1],
                z_send.at[item, k],
                z_recv.at[item, k],
                {"dp": 2 * ahead[k] + x},
            )
            copy.start()
            z_copies[item, k] = copy

    def finish(item):
        kind, at = items[item]
        _, keep, _, arrivals, done = buffers(item)
        total = keep[z].astype(F32)
        for k in range(1, deep):
            z_copies[item, k].wait_recv()
            total = total + arrivals[k - 1].astype(F32)
        done[...] = total.astype(BF)

        def keep_own(source, target):
            copy = pltpu.make_async_copy(source, target, out_sem.at[item])
            copy.start()
            outs.append(copy)

        def give_peer(source, target):
            copy = remote(source, target, y_send.at[item], y_recv.at[item], peer)
            copy.start()
            y_copies.append(copy)

        if kind == "attn":
            keep_own(done, attn_out)
        elif at % 2 == 0:
            keep_own(done, up_out.at[0, at // 2])
        else:
            give_peer(done, up_out.at[1, at // 2])

    for step in range(count + AHEAD + BEHIND):
        if step < count:
            send_x(step)
        if 0 <= step - AHEAD < count:
            send_z(step - AHEAD)
        if 0 <= step - AHEAD - BEHIND < count:
            finish(step - AHEAD - BEHIND)
    for copy in outs:
        copy.wait()
    y_first.wait_send()
    for copy in y_copies[1:]:
        copy.wait()
    for copy in list(x_copies.values()) + list(z_copies.values()):
        copy.wait_send()


def dp_reduce(up_grads, attn_grad):
    n = lax.axis_size("dp")
    deep = n // 2
    slots = up_grads.shape[0] - BESIDE
    up_tail, attn_tail = up_grads.shape[4:], attn_grad.shape[3:]
    sems = pltpu.SemaphoreType.DMA
    count = 2 * slots + 1
    vmem = lambda *shape: pltpu.VMEM(shape, BF)
    any_spec = pl.BlockSpec(memory_space=pl.ANY)
    return pl.pallas_call(
        functools.partial(reduce_kernel, n, slots),
        out_shape=[
            jax.ShapeDtypeStruct((2, slots) + up_tail, BF),
            jax.ShapeDtypeStruct(attn_tail, BF),
        ],
        in_specs=[any_spec] * 2,
        out_specs=[any_spec] * 2,
        scratch_shapes=[
            vmem(2 * slots, deep, *up_tail),
            vmem(deep, 2, *attn_tail),
            vmem(2 * slots, deep, *up_tail),
            vmem(deep, *attn_tail),
            vmem(2 * slots, deep - 1, *up_tail),
            vmem(deep - 1, *attn_tail),
            vmem(2 * slots, *up_tail),
            vmem(*attn_tail),
            vmem(deep, 2, *attn_tail),
            sems((count,)),
            sems((count,)),
            sems((count,)),
            sems((count, deep)),
            sems((count, deep)),
            sems((count,)),
            sems((count,)),
            sems((count,)),
        ],
        compiler_params=pltpu.CompilerParams(
            collective_id=1, has_side_effects=True, vmem_limit_bytes=48 << 20
        ),
    )(up_grads, attn_grad)


def pick(values, index, axis):
    return lax.dynamic_index_in_dim(values, index, axis, keepdims=False)


def x_halves(values, axis):
    shape, x = values.shape, lax.axis_index("dp") % 2
    values = values.reshape(shape[:axis] + (shape[axis] // 2, 2) + shape[axis + 1 :])
    return pick(values, x, axis + 1), pick(values, 1 - x, axis + 1)


def along_dp(values, step):
    return lax.ppermute(values, "dp", [(i, i ^ step) for i in range(lax.axis_size("dp"))])


def add_low(*terms):
    return sum(term.astype(F32) for term in terms).astype(BF)


def z_blocks(values, axis):
    z = lax.axis_index("dp") // 2
    return [pick(values, z ^ k, axis) for k in range(values.shape[axis])]


def order_pair(first_is_own, own, other, axis):
    return jnp.where(
        first_is_own, jnp.concatenate([own, other], axis), jnp.concatenate([other, own], axis)
    )


WINDOW = 2


def gather_kernel(n, plan, *refs):
    count = max(item[0] for item in plan) + 1
    pieces, fulls = refs[:count], refs[count : 2 * count]
    own_sem, z_send, z_recv, x_send, x_recv = refs[2 * count :]
    me = lax.axis_index("dp")
    deep = n // 2
    z, x = me // 2, me % 2
    partner = 2 * z + (1 - x)
    peers = [2 * lax.rem(z + k, deep) + x for k in range(1, deep)]
    sources = [2 * lax.rem(z + deep - k, deep) + x for k in range(deep)]

    greet([{"dp": device} for device in peers + [partner]])

    def region(item, owner):
        at, lead, rows = plan[item]
        full = fulls[at]
        for index in lead:
            full = full.at[index]
        if rows == 0:
            return full.at[owner]
        start = owner * rows
        if rows % 16 == 0:
            start = pl.multiple_of(start, 16)
        return full.at[pl.ds(start, rows)]

    def piece(item):
        at, lead, rows = plan[item]
        ref = pieces[at]
        for index in lead:
            ref = ref.at[index]
        return ref

    total = len(plan)
    local_copies = []
    z_copies = [[] for _ in range(total)]
    x_copies = [[] for _ in range(total)]
    for step in range(total + WINDOW):
        if step < total:
            here = region(step, me)
            for k in range(1, deep):
                copy = remote(
                    piece(step), here, z_send.at[step, k], z_recv.at[step, k], {"dp": peers[k - 1]}
                )
                copy.start()
                z_copies[step].append(copy)
            copy = remote(piece(step), here, x_send.at[step, 0], x_recv.at[step, 0], {"dp": partner})
            copy.start()
            x_copies[step].append(copy)
            copy = pltpu.make_async_copy(piece(step), here, own_sem.at[step])
            copy.start()
            local_copies.append(copy)
        if step >= WINDOW:
            item = step - WINDOW
            for k in range(1, deep):
                z_copies[item][k - 1].wait_recv()
                arrived = region(item, sources[k])
                copy = remote(
                    arrived, arrived, x_send.at[item, k], x_recv.at[item, k], {"dp": partner}
                )
                copy.start()
                x_copies[item].append(copy)
    for item in range(total):
        local_copies[item].wait()
        for copy in z_copies[item]:
            copy.wait_send()
        for copy in x_copies[item]:
            copy.wait()


def dp_gather(pieces, fulls, plan):
    n = lax.axis_size("dp")
    total = len(plan)
    sems = pltpu.SemaphoreType.DMA
    return pl.pallas_call(
        functools.partial(gather_kernel, n, plan),
        out_shape=[
            jax.ShapeDtypeStruct(shape, piece.dtype) for shape, piece in zip(fulls, pieces)
        ],
        in_specs=[pl.BlockSpec(memory_space=pl.ANY)] * len(pieces),
        out_specs=[pl.BlockSpec(memory_space=pl.ANY)] * len(fulls),
        scratch_shapes=[
            sems((total,)),
            sems((total, n // 2)),
            sems((total, n // 2)),
            sems((total, n // 2)),
            sems((total, n // 2)),
        ],
        compiler_params=pltpu.CompilerParams(collective_id=0, has_side_effects=True),
    )(*pieces)


TN = (((0,), (0,)), ((), ()))
TILE = 512


def column(values, index):
    return jnp.sum(jnp.where(lanes_of(values.shape) == index, values, 0.0), axis=1, keepdims=True)


def clear(first, ref):
    @pl.when(first)
    def _():
        ref[...] = jnp.zeros(ref.shape, ref.dtype)


def ffn_kernel(tokens, up_own, up_peer, down_own, down_peer, mix, *refs):
    pre, act, out = refs[-3:]
    slot = pl.program_id(0)
    quarter = down_own.shape[1]
    clear(slot == 0, out)
    w_up = jnp.concatenate([up_own[0], up_peer[0]], axis=0)
    w_down = jnp.concatenate([down_own[0], down_peer[0]], axis=1)
    for tile in range(tokens.shape[0] // TILE):
        rows = pl.ds(tile * TILE, TILE)
        both = jnp.dot(tokens[rows], w_up, preferred_element_type=F32)
        pre[0, rows] = both.astype(BF)
        gate, up = both[:, :quarter], both[:, quarter:]
        hidden = gate / (1.0 + jnp.exp(-gate)) * up * column(mix[rows], slot)
        act[0, rows] = hidden.astype(BF)
        out[rows] += jnp.dot(hidden.astype(BF), w_down, preferred_element_type=F32)


def ffn_forward(tokens, up_own, up_peer, down_own, down_peer, mix, part, parts, filled=()):
    slots, half, width = up_own.shape
    rows, depth = tokens.shape
    size = rows // parts
    per_slot = lambda *shape: pl.BlockSpec((1,) + shape, lambda e: (e, 0, 0))
    of_part = lambda *shape: pl.BlockSpec((1,) + shape, lambda e: (e, part, 0))
    whole = lambda *shape: pl.BlockSpec(shape, lambda e: (part, 0))
    return pl.pallas_call(
        ffn_kernel,
        grid=(slots,),
        out_shape=[
            jax.ShapeDtypeStruct((slots, rows, width), BF),
            jax.ShapeDtypeStruct((slots, rows, width // 2), BF),
            jax.ShapeDtypeStruct((size, depth), F32),
        ],
        in_specs=[
            whole(size, depth),
            per_slot(half, width),
            per_slot(half, width),
            per_slot(width // 2, half),
            per_slot(width // 2, half),
            whole(size, 8),
        ]
        + [pl.BlockSpec(memory_space=pl.ANY)] * len(filled),
        out_specs=[
            of_part(size, width),
            of_part(size, width // 2),
            pl.BlockSpec((size, depth), lambda e: (0, 0)),
        ],
        input_output_aliases={6: 0, 7: 1} if filled else {},
        compiler_params=pltpu.CompilerParams(vmem_limit_bytes=56 << 20),
        cost_estimate=pl.CostEstimate(
            flops=3 * slots * size * depth * width,
            bytes_accessed=20 << 20,
            transcendentals=slots * size * width // 2,
        ),
    )(tokens, up_own, up_peer, down_own, down_peer, mix, *filled)


def ffn_back_kernel(grads, pre, down_own, down_peer, mix, *refs):
    pre_grad, gate_sum = refs[-2:]
    slot = pl.program_id(0)
    quarter = down_own.shape[1]
    clear(slot == 0, gate_sum)
    w_down = jnp.concatenate([down_own[0], down_peer[0]], axis=1)
    for tile in range(grads.shape[0] // TILE):
        rows = pl.ds(tile * TILE, TILE)
        back = lax.dot_general(grads[rows], w_down, NT, preferred_element_type=F32)
        gate = pre[0, rows, :quarter].astype(F32)
        up = pre[0, rows, quarter:].astype(F32)
        sigma = 1.0 / (1.0 + jnp.exp(-gate))
        act_silu = gate * sigma
        sums = jnp.sum(back * act_silu * up, axis=1, keepdims=True)
        gate_sum[rows] += jnp.where(lanes_of((TILE, 8)) == slot, sums, 0.0)
        back = back * column(mix[rows], slot)
        pre_grad[0, rows, :quarter] = (back * up * (sigma * (1.0 + gate * (1.0 - sigma)))).astype(BF)
        pre_grad[0, rows, quarter:] = (back * act_silu).astype(BF)


def ffn_backward(grads, pre, down_own, down_peer, mix, part, parts, filled=()):
    slots, rows, width = pre.shape
    size, depth = grads.shape
    per_slot = lambda *shape: pl.BlockSpec((1,) + shape, lambda e: (e, 0, 0))
    of_part = lambda *shape: pl.BlockSpec((1,) + shape, lambda e: (e, part, 0))
    return pl.pallas_call(
        ffn_back_kernel,
        grid=(slots,),
        out_shape=[
            jax.ShapeDtypeStruct((slots, rows, width), BF),
            jax.ShapeDtypeStruct((size, 8), F32),
        ],
        in_specs=[
            pl.BlockSpec((size, depth), lambda e: (0, 0)),
            of_part(size, width),
            per_slot(width // 2, depth // 2),
            per_slot(width // 2, depth // 2),
            pl.BlockSpec((size, 8), lambda e: (part, 0)),
        ]
        + [pl.BlockSpec(memory_space=pl.ANY)] * len(filled),
        out_specs=[of_part(size, width), pl.BlockSpec((size, 8), lambda e: (0, 0))],
        input_output_aliases={5: 0} if filled else {},
        compiler_params=pltpu.CompilerParams(vmem_limit_bytes=56 << 20),
        cost_estimate=pl.CostEstimate(
            flops=2 * slots * size * depth * width,
            bytes_accessed=25 << 20,
            transcendentals=slots * size * width // 2,
        ),
    )(grads, pre, down_own, down_peer, mix, *filled)


def ffn_down_kernel(near, far, act, down_grad):
    size = near.shape[0]
    total = lax.dot_general(act[0, :size], near[...], TN, preferred_element_type=F32)
    total = total + lax.dot_general(act[0, size:], far[...], TN, preferred_element_type=F32)
    down_grad[0] = total.astype(BF)


def ffn_down(near, far, act):
    slots, rows, width = act.shape
    depth = near.shape[1]
    per_slot = lambda *shape: pl.BlockSpec((1,) + shape, lambda e: (e, 0, 0))
    whole = lambda *shape: pl.BlockSpec(shape, lambda e: (0, 0), pipeline_mode=pl.Buffered(1))
    return pl.pallas_call(
        ffn_down_kernel,
        grid=(slots,),
        out_shape=jax.ShapeDtypeStruct((slots, width, depth), BF),
        in_specs=[whole(rows // 2, depth), whole(rows // 2, depth), per_slot(rows, width)],
        out_specs=per_slot(width, depth),
        compiler_params=pltpu.CompilerParams(vmem_limit_bytes=40 << 20),
        cost_estimate=pl.CostEstimate(
            flops=2 * slots * rows * depth * width, bytes_accessed=20 << 20, transcendentals=0
        ),
    )(near, far, act)


def ffn_up_kernel(tokens, pre_grad, up_grad):
    for tile in range(tokens.shape[1] // 256):
        columns = slice(tile * 256, (tile + 1) * 256)
        up_grad[0, columns] = lax.dot_general(
            tokens[:, columns], pre_grad[0], TN, preferred_element_type=F32
        ).astype(BF)


def ffn_up(tokens, pre_grad):
    slots, rows, width = pre_grad.shape
    depth = tokens.shape[1]
    per_slot = lambda *shape: pl.BlockSpec((1,) + shape, lambda e: (e, 0, 0))
    return pl.pallas_call(
        ffn_up_kernel,
        grid=(slots,),
        out_shape=jax.ShapeDtypeStruct((slots, depth, width), BF),
        in_specs=[
            pl.BlockSpec((rows, depth), lambda e: (0, 0), pipeline_mode=pl.Buffered(1)),
            per_slot(rows, width),
        ],
        out_specs=per_slot(depth, width),
        compiler_params=pltpu.CompilerParams(vmem_limit_bytes=40 << 20),
        cost_estimate=pl.CostEstimate(
            flops=2 * slots * rows * depth * width, bytes_accessed=35 << 20, transcendentals=0
        ),
    )(tokens, pre_grad)


def ffn_input_kernel(pre_grad, up_own, up_peer, out):
    clear(pl.program_id(0) == 0, out)
    w_up = jnp.concatenate([up_own[0], up_peer[0]], axis=0)
    for tile in range(out.shape[0] // TILE):
        rows = pl.ds(tile * TILE, TILE)
        out[rows] += lax.dot_general(pre_grad[0, rows], w_up, NT, preferred_element_type=F32)


def ffn_input(pre_grad, up_own, up_peer, part, parts):
    slots, rows, width = pre_grad.shape
    half = up_own.shape[1]
    depth = 2 * half
    rows = rows // parts
    return pl.pallas_call(
        ffn_input_kernel,
        grid=(slots,),
        out_shape=jax.ShapeDtypeStruct((rows, depth), F32),
        in_specs=[
            pl.BlockSpec((1, rows, width), lambda e: (e, part, 0)),
            pl.BlockSpec((1, half, width), lambda e: (e, 0, 0)),
            pl.BlockSpec((1, half, width), lambda e: (e, 0, 0)),
        ],
        out_specs=pl.BlockSpec((rows, depth), lambda e: (0, 0)),
        compiler_params=pltpu.CompilerParams(vmem_limit_bytes=40 << 20),
        cost_estimate=pl.CostEstimate(
            flops=2 * slots * rows * depth * width, bytes_accessed=20 << 20, transcendentals=0
        ),
    )(pre_grad, up_own, up_peer)


def join_core(parts):
    size = parts.shape[0] // 2
    return parts[:size] + swap(parts[size:].astype(BF), "col").astype(F32)


def collect_tokens(far, near_of, operand):
    send = flip(join_core(far).astype(BF))
    send, operand = lax.optimization_barrier((send, operand))
    recv = swap(send, "row")
    near, *rest = near_of(operand)
    near, recv = lax.optimization_barrier((near, recv))
    return (join_core(near) + recv.astype(F32), *rest)


def from_sequence(values, r, c):
    half = values.shape[1] // 2
    own, peer = values[:, :half], values[:, half:]
    diag = r == c
    send = jnp.where(diag, peer, own)
    kept = jnp.where(diag, own, peer)
    recv = swap(send, "col")
    whole = order_pair(c == 0, kept, recv, 0)
    moved = lax.ppermute(whole, ("row", "col"), [(1, 2), (2, 1)])
    return jnp.where(diag, whole, moved)


def local(
    layer_input,
    teacher,
    valid_mask,
    routes,
    segments,
    gain_attn,
    gain_ffn,
    w_qkv,
    w_out,
    w_router,
    w_shared_up,
    w_shared_down,
    w_expert_up,
    w_expert_down,
):
    r = lax.axis_index("row")
    c = lax.axis_index("col")
    n_dp = lax.axis_size("dp")
    rows = layer_input.shape[0]
    part = rows // 2
    half = layer_input.shape[1]
    heads = w_qkv.shape[2] // HEAD_DIM
    ff = w_shared_up.shape[2]
    quarter = ff // 2
    slots = E + 1

    seg = lax.dynamic_slice_in_dim(segments, r, 1, 0)[0]
    seg_row, seg_col = seg[None, :], seg[:, None]
    tables = rope_tables(rows)
    w_qkv = w_qkv.swapaxes(0, 1)
    vectors = jnp.concatenate(
        [gain_attn[None], gain_ffn[None], w_router.T.astype(F32), jnp.zeros((6 - E, half), F32)]
    )
    (
        queries, keys_rot, values_low, context_low, normed_attn, x_own, hidden,
        w_qkv_peer, w_out_peer, vec_peer, up_own, tokens, up_peer, down_peer, teacher_pair,
    ) = front(
        layer_input, teacher, w_qkv, w_out, vectors, w_shared_up, w_expert_up, w_shared_down, w_expert_down,
        tables, seg,
    )

    vectors = jnp.concatenate([vectors, vec_peer], axis=1)
    gain_a, gain_f, w_r = vectors[0], vectors[1], vectors[2 : 2 + E].astype(BF).T
    teacher_own = jnp.concatenate([teacher_pair[0], teacher_pair[1]], axis=1).astype(F32)
    valid_other = swap(valid_mask, "col")
    valid_seq = jnp.where(r == c, valid_mask, valid_other).astype(F32)
    valid_own = lax.dynamic_slice_in_dim(valid_seq, c * part, part, 0)
    route_blocks = routes.reshape(2, 2, part, 2)
    route_blocks = jnp.where(r == 0, route_blocks, route_blocks[::-1])
    route_blocks = jnp.where(c == 0, route_blocks, route_blocks[:, ::-1]).reshape(4 * part, 2)
    picks = (route_blocks[:, :, None] == jnp.arange(E, dtype=jnp.int32)[None, None, :]).astype(F32)

    down_own = jnp.concatenate([w_shared_down[None], w_expert_down])
    down_own = lax.dynamic_slice_in_dim(down_own, r * quarter, quarter, 1)

    x_own = jnp.concatenate([x_own[0], x_own[1]], axis=1).astype(F32)
    rstd_attn = lax.rsqrt(jnp.mean(x_own * x_own, axis=1) + 1e-06)

    rstd_ffn = lax.rsqrt(jnp.mean(hidden * hidden, axis=1) + 1e-06)
    normed_low = tokens[0]
    tokens = tokens.reshape(4 * part, D)
    logits = jnp.dot(tokens, w_r, preferred_element_type=F32)
    chosen = jnp.sum(picks * logits[:, None, :], axis=2)
    chosen = chosen - jnp.max(chosen, axis=1, keepdims=True)
    gates = jnp.exp(chosen)
    gates = gates / jnp.sum(gates, axis=1, keepdims=True)
    mixing = jnp.sum(picks * gates[:, :, None], axis=1)
    mix = jnp.concatenate(
        [jnp.ones((4 * part, 1), F32), mixing, jnp.zeros((4 * part, 7 - E), F32)], axis=1
    )
    weights = (up_own, up_peer, down_own, down_peer)
    pre, act, far = ffn_forward(tokens, *weights, mix, 1, 2)

    def near_forward(operand):
        pre, act, near = ffn_forward(operand[0], *weights, mix, 0, 2, operand[1:])
        return near, pre, act

    branch, pre, act = collect_tokens(far, near_forward, (tokens, pre, act))
    output = hidden + branch

    error = output - teacher_own
    loss_part = jnp.sum(valid_own * jnp.sum(error * error, axis=1))
    grad_out = valid_own[:, None] * error

    low_own = grad_out.astype(BF)
    far = swap(flip(low_own), "row")
    near = jnp.concatenate([low_own, swap(low_own, "col")])
    pre_grad, near_sums = ffn_backward(near, pre, down_own, down_peer, mix, 0, 2)
    pre_grad, far = lax.optimization_barrier((pre_grad, far))
    far = jnp.concatenate([far, swap(far, "col")])
    owner_f = quarter // n_dp
    owner_d = half // n_dp
    deep = n_dp // 2
    down_grad = ffn_down(near, far, act)
    down_keep, down_send = x_halves(down_grad.reshape(slots, n_dp, owner_f, D), 1)
    pre_grad, far, down_send = lax.optimization_barrier((pre_grad, far, down_send))
    first_recv = along_dp(down_send[:3], 1)
    second_recv = along_dp(down_send[3:], 1)
    pre_grad, far_sums = ffn_backward(far, pre, down_own, down_peer, mix, 1, 2, (pre_grad,))
    gate_parts = jnp.concatenate([near_sums, far_sums])[:, 1 : E + 1].T.reshape(E, 4, part)
    recv = swap(jnp.stack([gate_parts[:, 1], gate_parts[:, 3]]), "col")
    gate_grad = gate_parts[:, 0] + recv[0] + swap(gate_parts[:, 2] + recv[1], "row")
    up_grad = ffn_up(tokens, pre_grad)
    up_grad = up_grad.reshape(slots, 2, n_dp, owner_d, 2 * quarter)
    up_keep, up_send = x_halves(up_grad[:BESIDE], 2)
    pre_grad, gate_grad, up_send, first_recv = lax.optimization_barrier(
        (pre_grad, gate_grad, up_send, first_recv)
    )
    far = ffn_input(pre_grad, up_own, up_peer, 1, 2)
    (normed_ffn_grad,) = collect_tokens(
        far, lambda operand: (ffn_input(operand, up_own, up_peer, 0, 2),), pre_grad
    )
    normed_ffn_grad, second_recv = lax.optimization_barrier((normed_ffn_grad, second_recv))
    down_recv = jnp.concatenate([first_recv, second_recv])
    down_own_sum, *down_sends = z_blocks(add_low(down_keep, down_recv), 1)
    normed_ffn_grad, down_sends, up_send = lax.optimization_barrier(
        (normed_ffn_grad, down_sends, up_send)
    )
    up_recv = along_dp(up_send, 1)
    down_recvs = [along_dp(block, 2 * k + 2) for k, block in enumerate(down_sends)]
    mix_own = mixing[:part].T
    centre = jnp.sum(mix_own * gate_grad, axis=0, keepdims=True)
    logit_grad = (mix_own * (gate_grad - centre)).T.astype(BF)
    normed_ffn_grad = normed_ffn_grad + jnp.dot(logit_grad, w_r.T, preferred_element_type=F32)
    router_grad = jnp.dot(normed_low.T, logit_grad, preferred_element_type=F32)
    hidden_back, gain_ffn_grad = norm_backward(hidden, rstd_ffn, gain_f, normed_ffn_grad)
    hidden_grad = grad_out + hidden_back

    low_own = hidden_grad.astype(BF)
    low_seq = order_pair(c == 0, low_own, swap(low_own, "col"), 0)
    w_out_grad = jnp.dot(context_low.T, low_seq, preferred_element_type=F32).astype(BF)
    w_out_full = jnp.concatenate([w_out, w_out_peer], axis=1)
    w_qkv_full = jnp.concatenate([w_qkv, w_qkv_peer], axis=1)
    normed_attn = jnp.concatenate([normed_attn[0], normed_attn[1]], axis=1)
    context_grad = jnp.dot(low_seq, w_out_full.T, preferred_element_type=F32)
    context_grad = context_grad.astype(BF)
    qkv_grad = jnp.concatenate(
        [
            attend_backward(
                queries, keys_rot, values_low, context_grad, tables, seg_row, seg_col, pair, 1
            )
            for pair in range(heads // 2)
        ],
        axis=2,
    )
    qkv_grad, down_recvs, up_recv = lax.optimization_barrier((qkv_grad, down_recvs, up_recv))
    up_own_sum, *up_sends = z_blocks(add_low(up_keep, up_recv), 2)
    qkv_grad, up_sends = lax.optimization_barrier((qkv_grad, up_sends))
    up_recvs = [along_dp(block, 2 * k + 2) for k, block in enumerate(up_sends)]
    down_sum = add_low(down_own_sum, *down_recvs)
    down_peer_sum = swap(down_sum[:, :, half:], "row")
    w_qkv_grad = jnp.einsum(
        "td,kte->dke", normed_attn, qkv_grad, preferred_element_type=F32
    ).astype(BF)
    back_part = jnp.einsum("kte,kde->td", qkv_grad, w_qkv_full, preferred_element_type=F32)
    back_halves = back_part.reshape(2, part, D)
    back_keep = lax.dynamic_index_in_dim(back_halves, c, 0, keepdims=False)
    back_send = lax.dynamic_index_in_dim(back_halves, 1 - c, 0, keepdims=False)
    normed_attn_grad = back_keep + swap(back_send.astype(BF), "col").astype(F32)
    input_back, gain_attn_grad = norm_backward(x_own, rstd_attn, gain_a, normed_attn_grad)
    input_grad = hidden_grad + input_back

    grad_pair = jnp.concatenate(
        [
            w_qkv_grad.reshape(2, n_dp, owner_d, 3, half),
            w_out_grad.reshape(n_dp, owner_d, 2, half).transpose(2, 0, 1, 3)[:, :, :, None],
        ],
        axis=3,
    ).transpose(0, 1, 3, 2, 4)
    up_pair, attn_piece = dp_reduce(
        up_grad.reshape(slots, 2, deep, 2, owner_d, 2 * quarter),
        grad_pair.reshape(2, deep, 2, 4 * owner_d, half),
    )
    up_pair, attn_piece, up_recvs = lax.optimization_barrier((up_pair, attn_piece, up_recvs))
    up_sum = add_low(up_own_sum, *up_recvs)
    up_peer_sum = swap(up_sum[:, 1], "row")
    attn_piece = attn_piece.reshape(4, owner_d, half)
    down_piece = order_pair(r == 0, down_sum[:, None, :, :half], down_peer_sum[:, None], 1)
    up_pair = jnp.concatenate([jnp.stack([up_sum[:, 0], up_peer_sum]), up_pair], axis=1)
    up_pair = up_pair.reshape(2, slots, owner_d, 2, quarter)
    up_piece = order_pair(r == 0, up_pair[0], up_pair[1], 3)

    small = jnp.concatenate([gain_attn_grad[None], gain_ffn_grad[None], router_grad.T], axis=0)
    small = jnp.where(r == 0, small, flip(small))
    loss_row = jnp.full((1, D), loss_part).at[0, half:].set(jnp.sum(valid_own))
    small = jnp.concatenate([small, loss_row, jnp.zeros((1, D), F32)])
    small = small + swap(small, "row")
    small = small + swap(small, "col")
    plan = [(1, (), owner_d), (3, (0,), owner_f), (3, (1,), owner_f)]
    for e in range(E):
        plan += [(0, (e,), owner_d), (2, (e, 0), owner_f), (2, (e, 1), owner_f)]
    plan += [(4, (), 0), (5, (), 0)]
    up_full, shared_up_full, down_full, shared_down_full, attn_full, small_full = dp_gather(
        (up_piece[1:], up_piece[0], down_piece[1:], down_piece[0], attn_piece, small),
        (
            (E, half, 2, ff),
            (half, 2, ff),
            (E, 2, quarter, half),
            (2, quarter, half),
            (n_dp, 4, owner_d, half),
            (n_dp, E + 4, D),
        ),
        tuple(plan),
    )
    small = jnp.sum(small_full, axis=0)
    count = small[E + 2, half]
    loss = small[E + 2, 0] / (2.0 * count)
    scale = part * 4 * n_dp / count
    small = small[: E + 2] * scale
    attn_full = attn_full.swapaxes(0, 1).reshape(4, half, half).astype(F32) * scale
    small = lax.dynamic_slice_in_dim(small, r * half, half, 1)
    return (
        from_sequence(output, r, c),
        loss,
        from_sequence(input_grad, r, c) * scale,
        small[0],
        small[1],
        attn_full[:3].swapaxes(0, 1),
        attn_full[3],
        small[2:].T,
        shared_up_full.astype(F32) * scale,
        shared_down_full.reshape(ff, half).astype(F32) * scale,
        up_full.astype(F32) * scale,
        down_full.reshape(E, ff, half).astype(F32) * scale,
    )


def solution(mesh):
    return jax.shard_map(
        local,
        mesh=mesh,
        in_specs=(
            P(("dp", "col"), "row"),
            P(("dp", "col"), "row"),
            P(("dp", "col")),
            P("dp", None),
            P("dp", None),
            P("row"),
            P("row"),
            P("row", None, "col"),
            P("col", "row"),
            P("row", None),
            P("row", None, "col"),
            P("col", "row"),
            P(None, "row", None, "col"),
            P(None, "col", "row"),
        ),
        out_specs=(
            P(("dp", "col"), "row"),
            P(),
            P(("dp", "col"), "row"),
            P("row"),
            P("row"),
            P("row", None, "col"),
            P("col", "row"),
            P("row", None),
            P("row", None, "col"),
            P("col", "row"),
            P(None, "row", None, "col"),
            P(None, "col", "row"),
        ),
        check_vma=False,
    )
```

```python
import functools

import jax
import jax.numpy as jnp
from jax import lax
from jax.experimental import pallas as pl
from jax.experimental.pallas import tpu as pltpu
from jax.sharding import PartitionSpec as P

D = 768
HEAD_DIM = 64
E = 4
LEN = 1024
ABLOCK = 256
BF = jnp.bfloat16
F32 = jnp.float32


def norm_backward(values, rstd_rows, gain_vec, incoming):
    scaled = incoming * gain_vec
    inner_sum = jnp.sum(scaled * values, axis=1)
    gain_grad = jnp.sum(incoming * values * rstd_rows[:, None], axis=0)
    result = rstd_rows[:, None] * scaled - values * (rstd_rows**3 * inner_sum / D)[:, None]
    return (result, gain_grad)


def rope_tables(length):
    half_dim = HEAD_DIM // 2
    freqs = 10000.0 ** (-jnp.arange(half_dim, dtype=F32) * 2.0 / HEAD_DIM)
    angles = jnp.arange(length, dtype=F32)[:, None] * freqs[None, :]
    sine = jnp.sin(angles)
    return (jnp.tile(jnp.cos(angles), (1, 4)), jnp.tile(jnp.concatenate([-sine, sine], axis=1), (1, 2)))


def lanes_of(shape):
    return lax.broadcasted_iota(jnp.int32, shape, len(shape) - 1)


def turn(values, first):
    half_dim = HEAD_DIM // 2
    return jnp.where(
        first,
        pltpu.roll(values, PAIR - half_dim, values.ndim - 1),
        pltpu.roll(values, half_dim, values.ndim - 1),
    )


PAIR = 2 * HEAD_DIM
NT = (((1,), (1,)), ((), ()))


def shares_of(key_pair, query_head, seg_col, seg_row):
    scores = lax.dot_general(key_pair, query_head, NT, preferred_element_type=F32)
    scores = jnp.where(seg_col == seg_row, scores, -1e30)
    weight = jnp.exp(scores - jnp.max(scores, axis=0, keepdims=True))
    return weight * (1.0 / jnp.sum(weight, axis=0, keepdims=True))


LAG = 3


def front_kernel(
    n, x_in, teacher, w_qkv, w_out, vectors, shared_up, expert_up, shared_down, expert_down,
    cosine, sine, seg_row, seg_col,
    queries, keys, values, context, normed, x_own, hidden, w_qkv_peer, w_out_peer, vec_peer, up_own,
    tokens, up_peer, down_peer, teacher_pair,
    x_pair, teacher_in, qkv_own, out_own, up_raw, part_raw, up_part, pre, att_send, att_recv, low, low_flip,
    own_sem, x_send, x_recv, w_send, w_recv, t_send, t_recv,
):
    me = lax.axis_index("dp")
    row, col = lax.axis_index("row"), lax.axis_index("col")
    z, x = me // 2, me % 2
    low_z = lax.rem(z, 2)
    x_peer = {"dp": 2 * z + (1 - x)}
    z_peer = {"dp": 2 * (z + 1 - 2 * low_z) + x}
    row_peer, core = {"row": 1 - row}, {"col": 1 - col}
    mine = 2 * low_z + x
    of_x, of_z = 2 * low_z + (1 - x), 2 * (1 - low_z) + x
    rows, half = x_in.shape
    part = rows // 2
    quarter = shared_up.shape[2] // 2
    slots = expert_up.shape[0] + 1
    greet([row_peer, core, x_peer, z_peer])

    def split(index, size):
        return pl.ds(pl.multiple_of(index * size, 16), size)

    def source(item, index):
        if item == 0:
            return w_qkv.at[:, split(index, half // 4)]
        if item == 1:
            return w_out.at[split(index, w_out.shape[0] // 4)]
        slot, kind = (item - 2) // 2, (item - 2) % 2
        if kind == 0:
            return up_part.at[slot]
        ref = shared_down if slot == 0 else expert_down.at[slot - 1]
        first = (1 - row) * quarter + index * (quarter // 4)
        return ref.at[pl.ds(pl.multiple_of(first, 16), quarter // 4)]

    def landing(item, index):
        if item == 0:
            return w_qkv_peer.at[:, split(index, half // 4)]
        if item == 1:
            return w_out_peer.at[split(index, w_out.shape[0] // 4)]
        slot, kind = (item - 2) // 2, (item - 2) % 2
        if kind == 0:
            return up_peer.at[slot, split(index, half // 4)]
        return down_peer.at[slot, split(index, quarter // 4)]

    count = 2 + 2 * slots
    copies = {}

    def start(item, leg, src, device, index):
        copy = remote(
            src, landing(item, index), w_send.at[item, leg], w_recv.at[item, leg], device
        )
        copy.start()
        copies[item, leg] = copy

    def fetch(item):
        start(item, 0, source(item, mine), row_peer, mine)

    def pass_on(item):
        copies[item, 0].wait_recv()
        start(item, 1, landing(item, mine), x_peer, mine)
        start(item, 2, landing(item, mine), z_peer, mine)

    def by_x(item):
        return (item - item // 4) % 2 == 0

    def pass_far(item):
        if by_x(item):
            copies[item, 1].wait_recv()
            start(item, 3, landing(item, of_x), z_peer, of_x)
        else:
            copies[item, 2].wait_recv()
            start(item, 3, landing(item, of_z), x_peer, of_z)

    def arrive(item):
        copies[item, 2 if by_x(item) else 1].wait_recv()
        copies[item, 3].wait_recv()

    progress = [0]

    def pump():
        at = progress[0]
        progress[0] += 1
        if 2 <= at < count:
            pass_on(at)
        if 2 <= at - LAG < count:
            pass_far(at - LAG)

    diagonal = row == col
    over_row = remote(x_in, x_pair.at[1], x_send.at[0], x_recv.at[0], row_peer)
    across_own = remote(x_in, x_pair.at[0], x_send.at[1], x_recv.at[1], core)
    across_peer = remote(x_pair.at[1], x_pair.at[1], x_send.at[2], x_recv.at[2], core)
    own_x = pltpu.make_async_copy(x_in, x_pair.at[0], own_sem.at[0])

    fetch(0)

    @pl.when(diagonal)
    def _():
        own_x.start()
        across_own.start()

    @pl.when(jnp.logical_not(diagonal))
    def _():
        over_row.start()

    def up_slot(slot):
        return shared_up if slot == 0 else expert_up.at[slot - 1]

    keep_lanes = pl.ds(pl.multiple_of(row * quarter, 128), quarter)
    send_lanes = pl.ds(pl.multiple_of((1 - row) * quarter, 128), quarter)
    part_loads, up_loads = [], []
    for slot in range(slots):
        piece = up_slot(slot).at[pl.ds(mine * (half // 4), half // 4), :, send_lanes]
        part_loads.append(pltpu.make_async_copy(piece, part_raw.at[slot], own_sem.at[4 + slot]))
        part_loads[slot].start()

    def split_own(slot):
        up_loads[slot].wait()
        for k in range(2):
            up_own[slot, :, k * quarter : (k + 1) * quarter] = up_raw[slot, :, k]

    give_vectors = remote(vectors, vec_peer, x_send.at[3], x_recv.at[3], row_peer)
    give_vectors.start()
    fetch(1)
    own_qkv = pltpu.make_async_copy(w_qkv, qkv_own, own_sem.at[1])
    own_qkv.start()
    own_out = pltpu.make_async_copy(w_out, out_own, own_sem.at[2])
    own_out.start()

    goal_row = remote(teacher, teacher_in, x_send.at[4], x_recv.at[4], row_peer)
    goal_own = remote(
        teacher.at[split(1 - col, part)], teacher_pair.at[0], x_send.at[5], x_recv.at[5], core
    )
    goal_peer = remote(
        teacher_in.at[split(1 - col, part)], teacher_pair.at[1], x_send.at[6], x_recv.at[6], core
    )
    keep_own = pltpu.make_async_copy(
        teacher.at[split(col, part)], teacher_pair.at[0], own_sem.at[4 + 2 * slots]
    )
    keep_peer = pltpu.make_async_copy(
        teacher_in.at[split(col, part)], teacher_pair.at[1], own_sem.at[5 + 2 * slots]
    )

    for slot in range(slots):
        piece = up_slot(slot).at[:, :, keep_lanes]
        up_loads.append(
            pltpu.make_async_copy(piece, up_raw.at[slot], own_sem.at[4 + slots + slot])
        )
        up_loads[slot].start()
    for slot in range(slots):
        part_loads[slot].wait()
        for k in range(2):
            up_part[slot, :, k * quarter : (k + 1) * quarter] = part_raw[slot, :, k]

    @pl.when(diagonal)
    def _():
        over_row.wait_recv()
        across_peer.start()
        own_x.wait()

    @pl.when(jnp.logical_not(diagonal))
    def _():
        over_row.wait_send()

    for item in range(2, count):
        fetch(item)

    @pl.when(diagonal)
    def _():
        goal_own.start()
        keep_own.start()

    @pl.when(jnp.logical_not(diagonal))
    def _():
        goal_row.start()

    pass_on(0)
    pass_on(1)
    split_own(0)

    @pl.when(jnp.logical_not(diagonal))
    def _():
        across_own.wait_recv()
        across_peer.wait_recv()

    give_vectors.wait_recv()
    progress[0] = 2
    x_first, x_second = x_pair[0].astype(F32), x_pair[1].astype(F32)
    squares = jnp.sum(x_first * x_first, axis=1, keepdims=True)
    squares = squares + jnp.sum(x_second * x_second, axis=1, keepdims=True)
    rstd = lax.rsqrt(squares / (2 * half) + 1e-06)
    normed[0] = (x_first * rstd * vectors[0:1]).astype(BF)
    normed[1] = (x_second * rstd * vec_peer[0:1]).astype(BF)
    pass_far(0)
    pass_far(1)
    for slot in range(1, slots):
        split_own(slot)
    arrive(0)
    own_qkv.wait()
    for j in range(3):
        pre[j] = jnp.dot(normed[0], qkv_own[j], preferred_element_type=F32) + jnp.dot(
            normed[1], w_qkv_peer[j], preferred_element_type=F32
        )
        pump()

    first = lanes_of((rows, PAIR)) % HEAD_DIM < HEAD_DIM // 2
    lower = lanes_of((ABLOCK, PAIR)) < HEAD_DIM
    cos, sin = cosine[...], sine[...]
    for pair in range(half // PAIR):
        lanes = slice(pair * PAIR, (pair + 1) * PAIR)
        query = pre[0, :, lanes]
        queries[:, lanes] = ((query * cos + turn(query, first) * sin) * HEAD_DIM**-0.5).astype(BF)
        key = pre[1, :, lanes]
        keys[:, lanes] = (key * cos + turn(key, first) * sin).astype(BF)
        value = pre[2, :, lanes]
        values[:, lanes] = value.astype(BF)
        value_t = value.T.astype(BF)
        for block in range(rows // ABLOCK):
            begin, stop = block * ABLOCK, (block + 1) * ABLOCK
            query = queries[begin:stop, lanes]
            parts = []
            for head in range(2):
                query_head = jnp.where(lower == (head == 0), query, jnp.zeros_like(query))
                shares = shares_of(
                    keys[:stop, lanes], query_head, seg_col[:stop], seg_row[:, begin:stop]
                ).astype(BF)
                parts.append(jnp.dot(value_t[:, :stop], shares, preferred_element_type=F32))
            both = jnp.concatenate([parts[0][:HEAD_DIM], parts[1][HEAD_DIM:]], axis=0)
            context[begin:stop, lanes] = both.T.astype(BF)
            if block % 2 == 1:
                pump()

    arrive(1)
    own_out.wait()
    there, here = split(1 - col, part), split(col, part)
    for at, weight in enumerate((out_own, w_out_peer)):
        att_send[:, at * half : (at + 1) * half] = jnp.dot(
            context[there], weight[...], preferred_element_type=F32
        ).astype(BF)
    swap_att = remote(att_send, att_recv, t_send.at[0], t_recv.at[0], core)
    swap_att.start()
    pump()
    for at, weight in enumerate((out_own, w_out_peer)):
        lanes = slice(at * half, (at + 1) * half)
        x_own[at] = x_pair[at, here]
        hidden[:, lanes] = x_own[at].astype(F32) + jnp.dot(
            context[here], weight[...], preferred_element_type=F32
        )
    swap_att.wait_recv()
    total = hidden[...] + att_recv[...].astype(F32)
    hidden[...] = total
    rstd = lax.rsqrt(jnp.mean(total * total, axis=1, keepdims=True) + 1e-06)
    gains = jnp.concatenate([vectors[1:2], vec_peer[1:2]], axis=1)
    total = (total * rstd * gains).astype(BF)
    low[...] = total
    low_flip[:, :half] = total[:, half:]
    low_flip[:, half:] = total[:, :half]
    own_tokens = pltpu.make_async_copy(low, tokens.at[0], own_sem.at[3])
    own_tokens.start()
    far = remote(low_flip, tokens.at[2], t_send.at[1], t_recv.at[1], row_peer)
    far.start()
    near = remote(low, tokens.at[1], t_send.at[2], t_recv.at[2], core)
    near.start()
    while progress[0] < count + LAG:
        pump()

    @pl.when(diagonal)
    def _():
        goal_row.wait_recv()
        goal_peer.start()
        keep_peer.start()

    far.wait_recv()
    far_near = remote(tokens.at[2], tokens.at[3], t_send.at[3], t_recv.at[3], core)
    far_near.start()
    for item in range(2, count):
        arrive(item)
    near.wait_recv()
    far_near.wait_recv()
    own_tokens.wait()
    for copy in (give_vectors, swap_att, far, near, far_near, *copies.values()):
        copy.wait_send()

    @pl.when(diagonal)
    def _():
        across_own.wait_send()
        across_peer.wait_send()
        goal_own.wait_send()
        goal_peer.wait_send()
        keep_own.wait()
        keep_peer.wait()

    @pl.when(jnp.logical_not(diagonal))
    def _():
        goal_row.wait_send()
        goal_own.wait_recv()
        goal_peer.wait_recv()


def front(x_in, teacher, w_qkv, w_out, vectors, shared_up, expert_up, shared_down, expert_down, tables, seg):
    n = lax.axis_size("dp")
    rows, half = x_in.shape
    quarter = shared_up.shape[2] // 2
    slots = expert_up.shape[0] + 1
    count = 2 + 2 * slots
    sems = pltpu.SemaphoreType.DMA
    any_spec = pl.BlockSpec(memory_space=pl.ANY)
    vmem_spec = pl.BlockSpec(memory_space=pltpu.VMEM)
    shape = jax.ShapeDtypeStruct
    wide = w_out.shape[0]
    return pl.pallas_call(
        functools.partial(front_kernel, n),
        out_shape=[shape((rows, wide), BF)] * 4
        + [
            shape((2, rows, half), BF),
            shape((2, rows // 2, half), BF),
            shape((rows // 2, 2 * half), F32),
            shape(w_qkv.shape, BF),
            shape(w_out.shape, BF),
            shape(vectors.shape, F32),
            shape((slots, half, 2 * quarter), BF),
            shape((4, rows // 2, 2 * half), BF),
            shape((slots, half, 2 * quarter), BF),
            shape((slots, quarter, half), BF),
            shape((2, rows // 2, half), BF),
        ],
        in_specs=[any_spec] * 4 + [vmem_spec] + [any_spec] * 4 + [vmem_spec] * 4,
        out_specs=[vmem_spec] * 11 + [any_spec] * 4,
        scratch_shapes=[
            pltpu.VMEM((2, rows, half), BF),
            pltpu.VMEM((rows, half), BF),
            pltpu.VMEM(w_qkv.shape, BF),
            pltpu.VMEM(w_out.shape, BF),
            pltpu.VMEM((slots, half, 2, quarter), BF),
            pltpu.VMEM((slots, half // 4, 2, quarter), BF),
            pltpu.VMEM((slots, half // 4, 2 * quarter), BF),
            pltpu.VMEM((3, rows, wide), F32),
            pltpu.VMEM((rows // 2, 2 * half), BF),
            pltpu.VMEM((rows // 2, 2 * half), BF),
            pltpu.VMEM((rows // 2, 2 * half), BF),
            pltpu.VMEM((rows // 2, 2 * half), BF),
            sems((6 + 2 * slots,)),
            sems((7,)),
            sems((7,)),
            sems((count, 4)),
            sems((count, 4)),
            sems((4,)),
            sems((4,)),
        ],
        compiler_params=pltpu.CompilerParams(
            collective_id=2, has_side_effects=True, vmem_limit_bytes=48 << 20
        ),
    )(
        x_in, teacher, w_qkv, w_out, vectors, shared_up, expert_up, shared_down, expert_down,
        tables[0], tables[1], seg[None, :], seg[:, None],
    )


def attend_back_kernel(
    queries, keys, values, context_grad, cosine, sine, seg_row, seg_col, out, key_sum, value_sum
):
    rows = queries.shape[0]
    key_t = keys[...].astype(F32).T.astype(BF)
    lower = lanes_of((ABLOCK, PAIR)) < HEAD_DIM
    first = lanes_of((ABLOCK, PAIR)) % HEAD_DIM < HEAD_DIM // 2
    for block in reversed(range(rows // ABLOCK)):
        start, stop = block * ABLOCK, (block + 1) * ABLOCK
        query, incoming = queries[start:stop], context_grad[start:stop]
        parts, key_part, value_part = [], None, None
        for head in range(2):
            mine = lower == (head == 0)
            query_head = jnp.where(mine, query, jnp.zeros_like(query))
            incoming_head = jnp.where(mine, incoming, jnp.zeros_like(incoming))
            shares = shares_of(keys[:stop], query_head, seg_col[:stop], seg_row[:, start:stop])
            share_grad = lax.dot_general(
                values[:stop], incoming_head, NT, preferred_element_type=F32
            )
            centre = jnp.sum(shares * share_grad, axis=0, keepdims=True)
            score_grad = (shares * (share_grad - centre)).astype(BF)
            parts.append(jnp.dot(key_t[:, :stop], score_grad, preferred_element_type=F32))
            more = jnp.dot(shares.astype(BF), incoming_head, preferred_element_type=F32)
            value_part = more if head == 0 else value_part + more
            more = jnp.dot(score_grad, query_head, preferred_element_type=F32)
            key_part = more if head == 0 else key_part + more
        both = jnp.concatenate([parts[0][:HEAD_DIM], parts[1][HEAD_DIM:]], axis=0)
        grad = both.T * HEAD_DIM**-0.5
        cos, sin = cosine[start:stop], sine[start:stop]
        out[0, start:stop] = (grad * cos + turn(grad * sin, first)).astype(BF)
        if stop == rows:
            key_sum[...] = key_part
            value_sum[...] = value_part
        else:
            key_sum[:stop] += key_part
            value_sum[:stop] += value_part
    for block in range(rows // ABLOCK):
        start, stop = block * ABLOCK, (block + 1) * ABLOCK
        grad = key_sum[start:stop]
        cos, sin = cosine[start:stop], sine[start:stop]
        out[1, start:stop] = (grad * cos + turn(grad * sin, first)).astype(BF)
        out[2, start:stop] = value_sum[start:stop].astype(BF)


def attend_backward(queries, keys, values, context_grad, tables, seg_row, seg_col, first_pair, pairs):
    rows = queries.shape[0]
    block = pl.BlockSpec((rows, PAIR), lambda i: (0, i + first_pair))
    whole = pl.BlockSpec((rows, PAIR), lambda i: (0, 0))
    return pl.pallas_call(
        attend_back_kernel,
        grid=(pairs,),
        out_shape=jax.ShapeDtypeStruct((3, rows, pairs * PAIR), BF),
        in_specs=[block] * 4
        + [
            whole,
            whole,
            pl.BlockSpec((1, rows), lambda i: (0, 0)),
            pl.BlockSpec((rows, 1), lambda i: (0, 0)),
        ],
        out_specs=pl.BlockSpec((3, rows, PAIR), lambda i: (0, 0, i)),
        scratch_shapes=[pltpu.VMEM((rows, PAIR), F32), pltpu.VMEM((rows, PAIR), F32)],
        compiler_params=pltpu.CompilerParams(vmem_limit_bytes=40 << 20),
        cost_estimate=pl.CostEstimate(
            flops=pairs * 14_000_000_000, bytes_accessed=4 << 20, transcendentals=2 << 20
        ),
    )(queries, keys, values, context_grad, tables[0], tables[1], seg_row, seg_col)


def swap(values, axis):
    return lax.ppermute(values, axis, [(0, 1), (1, 0)])


def flip(values):
    half = values.shape[-1] // 2
    return jnp.concatenate([values[..., half:], values[..., :half]], axis=-1)


def remote(src, dst, send, recv, device):
    return pltpu.make_async_remote_copy(
        src_ref=src,
        dst_ref=dst,
        send_sem=send,
        recv_sem=recv,
        device_id=device,
        device_id_type=pl.DeviceIdType.MESH,
    )


def greet(devices):
    barrier = pltpu.get_barrier_semaphore()
    for device in devices:
        pl.semaphore_signal(
            barrier, inc=1, device_id=device, device_id_type=pl.DeviceIdType.MESH
        )
    pl.semaphore_wait(barrier, len(devices))


BESIDE = 2
AHEAD = 3
BEHIND = 3


def reduce_kernel(n, slots, *refs):
    ups, attn, up_out, attn_out = refs[:4]
    (
        up_keep, attn_keep, up_x, attn_x, up_z, attn_z, up_done, attn_done, attn_y,
        keep_sem, x_send, x_recv, z_send, z_recv, out_sem, y_send, y_recv,
    ) = refs[4:]
    me = lax.axis_index("dp")
    row = lax.axis_index("row")
    deep = n // 2
    z, x = me // 2, me % 2
    partner = {"dp": 2 * z + (1 - x)}
    peer = {"row": 1 - row}
    ahead = [lax.rem(z + k, deep) for k in range(deep)]
    greet([partner, peer] + [{"dp": 2 * ahead[k] + x} for k in range(1, deep)])

    items = [("up", 2 * e + h) for e in range(slots) for h in (1, 0)]
    items += [("attn", 0)]
    count = len(items)
    last = count - 1

    def buffers(item):
        kind, at = items[item]
        if kind == "up":
            return ups.at[BESIDE + at // 2, at % 2], up_keep.at[at], up_x.at[at], up_z.at[at], up_done.at[at]
        return None, attn_keep.at[:, x], attn_x, attn_z, attn_done

    y_first = remote(attn.at[1], attn_y, y_send.at[last], y_recv.at[last], peer)
    y_first.start()
    attn_load = pltpu.make_async_copy(attn.at[0], attn_keep, keep_sem.at[last])
    attn_load.start()
    loads, x_copies, z_copies, outs, y_copies = {}, {}, {}, [], [y_first]
    for item in range(last):
        source, keep, _, _, _ = buffers(item)
        loads[item] = pltpu.make_async_copy(source.at[:, x], keep, keep_sem.at[item])
        loads[item].start()

    def send_x(item):
        source, keep, landing, _, _ = buffers(item)
        if item == last:
            attn_load.wait()
            y_first.wait_recv()
            attn_keep[...] = (attn_keep[...].astype(F32) + attn_y[...].astype(F32)).astype(BF)
            given = attn_keep.at[:, 1 - x]
        else:
            given = source.at[:, 1 - x]
        x_copies[item] = remote(given, landing, x_send.at[item], x_recv.at[item], partner)
        x_copies[item].start()

    def send_z(item):
        _, keep, landing, arrivals, _ = buffers(item)
        if item in loads:
            loads[item].wait()
        x_copies[item].wait_recv()
        keep[...] = (keep[...].astype(F32) + landing[...].astype(F32)).astype(BF)
        for k in range(1, deep):
            copy = remote(
                keep.at[ahead[k]],
                arrivals.at[k - 1],
                z_send.at[item, k],
                z_recv.at[item, k],
                {"dp": 2 * ahead[k] + x},
            )
            copy.start()
            z_copies[item, k] = copy

    def finish(item):
        kind, at = items[item]
        _, keep, _, arrivals, done = buffers(item)
        total = keep[z].astype(F32)
        for k in range(1, deep):
            z_copies[item, k].wait_recv()
            total = total + arrivals[k - 1].astype(F32)
        done[...] = total.astype(BF)

        def keep_own(source, target):
            copy = pltpu.make_async_copy(source, target, out_sem.at[item])
            copy.start()
            outs.append(copy)

        def give_peer(source, target):
            copy = remote(source, target, y_send.at[item], y_recv.at[item], peer)
            copy.start()
            y_copies.append(copy)

        if kind == "attn":
            keep_own(done, attn_out)
        elif at % 2 == 0:
            keep_own(done, up_out.at[0, at // 2])
        else:
            give_peer(done, up_out.at[1, at // 2])

    for step in range(count + AHEAD + BEHIND):
        if step < count:
            send_x(step)
        if 0 <= step - AHEAD < count:
            send_z(step - AHEAD)
        if 0 <= step - AHEAD - BEHIND < count:
            finish(step - AHEAD - BEHIND)
    for copy in outs:
        copy.wait()
    y_first.wait_send()
    for copy in y_copies[1:]:
        copy.wait()
    for copy in list(x_copies.values()) + list(z_copies.values()):
        copy.wait_send()


def dp_reduce(up_grads, attn_grad):
    n = lax.axis_size("dp")
    deep = n // 2
    slots = up_grads.shape[0] - BESIDE
    up_tail, attn_tail = up_grads.shape[4:], attn_grad.shape[3:]
    sems = pltpu.SemaphoreType.DMA
    count = 2 * slots + 1
    vmem = lambda *shape: pltpu.VMEM(shape, BF)
    any_spec = pl.BlockSpec(memory_space=pl.ANY)
    return pl.pallas_call(
        functools.partial(reduce_kernel, n, slots),
        out_shape=[
            jax.ShapeDtypeStruct((2, slots) + up_tail, BF),
            jax.ShapeDtypeStruct(attn_tail, BF),
        ],
        in_specs=[any_spec] * 2,
        out_specs=[any_spec] * 2,
        scratch_shapes=[
            vmem(2 * slots, deep, *up_tail),
            vmem(deep, 2, *attn_tail),
            vmem(2 * slots, deep, *up_tail),
            vmem(deep, *attn_tail),
            vmem(2 * slots, deep - 1, *up_tail),
            vmem(deep - 1, *attn_tail),
            vmem(2 * slots, *up_tail),
            vmem(*attn_tail),
            vmem(deep, 2, *attn_tail),
            sems((count,)),
            sems((count,)),
            sems((count,)),
            sems((count, deep)),
            sems((count, deep)),
            sems((count,)),
            sems((count,)),
            sems((count,)),
        ],
        compiler_params=pltpu.CompilerParams(
            collective_id=1, has_side_effects=True, vmem_limit_bytes=48 << 20
        ),
    )(up_grads, attn_grad)


def pick(values, index, axis):
    return lax.dynamic_index_in_dim(values, index, axis, keepdims=False)


def x_halves(values, axis):
    shape, x = values.shape, lax.axis_index("dp") % 2
    values = values.reshape(shape[:axis] + (shape[axis] // 2, 2) + shape[axis + 1 :])
    return pick(values, x, axis + 1), pick(values, 1 - x, axis + 1)


def along_dp(values, step):
    return lax.ppermute(values, "dp", [(i, i ^ step) for i in range(lax.axis_size("dp"))])


def add_low(*terms):
    return sum(term.astype(F32) for term in terms).astype(BF)


def z_blocks(values, axis):
    z = lax.axis_index("dp") // 2
    return [pick(values, z ^ k, axis) for k in range(values.shape[axis])]


def order_pair(first_is_own, own, other, axis):
    return jnp.where(
        first_is_own, jnp.concatenate([own, other], axis), jnp.concatenate([other, own], axis)
    )


WINDOW = 2


def gather_kernel(n, plan, *refs):
    count = max(item[0] for item in plan) + 1
    pieces, fulls = refs[:count], refs[count : 2 * count]
    own_sem, z_send, z_recv, x_send, x_recv = refs[2 * count :]
    me = lax.axis_index("dp")
    deep = n // 2
    z, x = me // 2, me % 2
    partner = 2 * z + (1 - x)
    peers = [2 * lax.rem(z + k, deep) + x for k in range(1, deep)]
    sources = [2 * lax.rem(z + deep - k, deep) + x for k in range(deep)]

    greet([{"dp": device} for device in peers + [partner]])

    def region(item, owner):
        at, lead, rows = plan[item]
        full = fulls[at]
        for index in lead:
            full = full.at[index]
        if rows == 0:
            return full.at[owner]
        start = owner * rows
        if rows % 16 == 0:
            start = pl.multiple_of(start, 16)
        return full.at[pl.ds(start, rows)]

    def piece(item):
        at, lead, rows = plan[item]
        ref = pieces[at]
        for index in lead:
            ref = ref.at[index]
        return ref

    total = len(plan)
    local_copies = []
    z_copies = [[] for _ in range(total)]
    x_copies = [[] for _ in range(total)]
    for step in range(total + WINDOW):
        if step < total:
            here = region(step, me)
            for k in range(1, deep):
                copy = remote(
                    piece(step), here, z_send.at[step, k], z_recv.at[step, k], {"dp": peers[k - 1]}
                )
                copy.start()
                z_copies[step].append(copy)
            copy = remote(piece(step), here, x_send.at[step, 0], x_recv.at[step, 0], {"dp": partner})
            copy.start()
            x_copies[step].append(copy)
            copy = pltpu.make_async_copy(piece(step), here, own_sem.at[step])
            copy.start()
            local_copies.append(copy)
        if step >= WINDOW:
            item = step - WINDOW
            for k in range(1, deep):
                z_copies[item][k - 1].wait_recv()
                arrived = region(item, sources[k])
                copy = remote(
                    arrived, arrived, x_send.at[item, k], x_recv.at[item, k], {"dp": partner}
                )
                copy.start()
                x_copies[item].append(copy)
    for item in range(total):
        local_copies[item].wait()
        for copy in z_copies[item]:
            copy.wait_send()
        for copy in x_copies[item]:
            copy.wait()


def dp_gather(pieces, fulls, plan):
    n = lax.axis_size("dp")
    total = len(plan)
    sems = pltpu.SemaphoreType.DMA
    return pl.pallas_call(
        functools.partial(gather_kernel, n, plan),
        out_shape=[
            jax.ShapeDtypeStruct(shape, piece.dtype) for shape, piece in zip(fulls, pieces)
        ],
        in_specs=[pl.BlockSpec(memory_space=pl.ANY)] * len(pieces),
        out_specs=[pl.BlockSpec(memory_space=pl.ANY)] * len(fulls),
        scratch_shapes=[
            sems((total,)),
            sems((total, n // 2)),
            sems((total, n // 2)),
            sems((total, n // 2)),
            sems((total, n // 2)),
        ],
        compiler_params=pltpu.CompilerParams(collective_id=0, has_side_effects=True),
    )(*pieces)


TN = (((0,), (0,)), ((), ()))
TILE = 512


def column(values, index):
    return jnp.sum(jnp.where(lanes_of(values.shape) == index, values, 0.0), axis=1, keepdims=True)


def clear(first, ref):
    @pl.when(first)
    def _():
        ref[...] = jnp.zeros(ref.shape, ref.dtype)


def ffn_kernel(tokens, up_own, up_peer, down_own, down_peer, mix, *refs):
    pre, act, out = refs[-3:]
    slot = pl.program_id(0)
    quarter = down_own.shape[1]
    clear(slot == 0, out)
    w_up = jnp.concatenate([up_own[0], up_peer[0]], axis=0)
    w_down = jnp.concatenate([down_own[0], down_peer[0]], axis=1)
    for tile in range(tokens.shape[0] // TILE):
        rows = pl.ds(tile * TILE, TILE)
        both = jnp.dot(tokens[rows], w_up, preferred_element_type=F32)
        pre[0, rows] = both.astype(BF)
        gate, up = both[:, :quarter], both[:, quarter:]
        hidden = gate / (1.0 + jnp.exp(-gate)) * up * column(mix[rows], slot)
        act[0, rows] = hidden.astype(BF)
        out[rows] += jnp.dot(hidden.astype(BF), w_down, preferred_element_type=F32)


def ffn_forward(tokens, up_own, up_peer, down_own, down_peer, mix, part, parts, filled=()):
    slots, half, width = up_own.shape
    rows, depth = tokens.shape
    size = rows // parts
    per_slot = lambda *shape: pl.BlockSpec((1,) + shape, lambda e: (e, 0, 0))
    of_part = lambda *shape: pl.BlockSpec((1,) + shape, lambda e: (e, part, 0))
    whole = lambda *shape: pl.BlockSpec(shape, lambda e: (part, 0))
    return pl.pallas_call(
        ffn_kernel,
        grid=(slots,),
        out_shape=[
            jax.ShapeDtypeStruct((slots, rows, width), BF),
            jax.ShapeDtypeStruct((slots, rows, width // 2), BF),
            jax.ShapeDtypeStruct((size, depth), F32),
        ],
        in_specs=[
            whole(size, depth),
            per_slot(half, width),
            per_slot(half, width),
            per_slot(width // 2, half),
            per_slot(width // 2, half),
            whole(size, 8),
        ]
        + [pl.BlockSpec(memory_space=pl.ANY)] * len(filled),
        out_specs=[
            of_part(size, width),
            of_part(size, width // 2),
            pl.BlockSpec((size, depth), lambda e: (0, 0)),
        ],
        input_output_aliases={6: 0, 7: 1} if filled else {},
        compiler_params=pltpu.CompilerParams(vmem_limit_bytes=56 << 20),
        cost_estimate=pl.CostEstimate(
            flops=3 * slots * size * depth * width,
            bytes_accessed=20 << 20,
            transcendentals=slots * size * width // 2,
        ),
    )(tokens, up_own, up_peer, down_own, down_peer, mix, *filled)


def ffn_back_kernel(grads, pre, down_own, down_peer, mix, *refs):
    pre_grad, gate_sum = refs[-2:]
    slot = pl.program_id(0)
    quarter = down_own.shape[1]
    clear(slot == 0, gate_sum)
    w_down = jnp.concatenate([down_own[0], down_peer[0]], axis=1)
    for tile in range(grads.shape[0] // TILE):
        rows = pl.ds(tile * TILE, TILE)
        back = lax.dot_general(grads[rows], w_down, NT, preferred_element_type=F32)
        gate = pre[0, rows, :quarter].astype(F32)
        up = pre[0, rows, quarter:].astype(F32)
        sigma = 1.0 / (1.0 + jnp.exp(-gate))
        act_silu = gate * sigma
        sums = jnp.sum(back * act_silu * up, axis=1, keepdims=True)
        gate_sum[rows] += jnp.where(lanes_of((TILE, 8)) == slot, sums, 0.0)
        back = back * column(mix[rows], slot)
        pre_grad[0, rows, :quarter] = (back * up * (sigma * (1.0 + gate * (1.0 - sigma)))).astype(BF)
        pre_grad[0, rows, quarter:] = (back * act_silu).astype(BF)


def ffn_backward(grads, pre, down_own, down_peer, mix, part, parts, filled=()):
    slots, rows, width = pre.shape
    size, depth = grads.shape
    per_slot = lambda *shape: pl.BlockSpec((1,) + shape, lambda e: (e, 0, 0))
    of_part = lambda *shape: pl.BlockSpec((1,) + shape, lambda e: (e, part, 0))
    return pl.pallas_call(
        ffn_back_kernel,
        grid=(slots,),
        out_shape=[
            jax.ShapeDtypeStruct((slots, rows, width), BF),
            jax.ShapeDtypeStruct((size, 8), F32),
        ],
        in_specs=[
            pl.BlockSpec((size, depth), lambda e: (0, 0)),
            of_part(size, width),
            per_slot(width // 2, depth // 2),
            per_slot(width // 2, depth // 2),
            pl.BlockSpec((size, 8), lambda e: (part, 0)),
        ]
        + [pl.BlockSpec(memory_space=pl.ANY)] * len(filled),
        out_specs=[of_part(size, width), pl.BlockSpec((size, 8), lambda e: (0, 0))],
        input_output_aliases={5: 0} if filled else {},
        compiler_params=pltpu.CompilerParams(vmem_limit_bytes=56 << 20),
        cost_estimate=pl.CostEstimate(
            flops=2 * slots * size * depth * width,
            bytes_accessed=25 << 20,
            transcendentals=slots * size * width // 2,
        ),
    )(grads, pre, down_own, down_peer, mix, *filled)


def ffn_down_kernel(near, far, act, down_grad):
    size = near.shape[0]
    total = lax.dot_general(act[0, :size], near[...], TN, preferred_element_type=F32)
    total = total + lax.dot_general(act[0, size:], far[...], TN, preferred_element_type=F32)
    down_grad[0] = total.astype(BF)


def ffn_down(near, far, act):
    slots, rows, width = act.shape
    depth = near.shape[1]
    per_slot = lambda *shape: pl.BlockSpec((1,) + shape, lambda e: (e, 0, 0))
    whole = lambda *shape: pl.BlockSpec(shape, lambda e: (0, 0), pipeline_mode=pl.Buffered(1))
    return pl.pallas_call(
        ffn_down_kernel,
        grid=(slots,),
        out_shape=jax.ShapeDtypeStruct((slots, width, depth), BF),
        in_specs=[whole(rows // 2, depth), whole(rows // 2, depth), per_slot(rows, width)],
        out_specs=per_slot(width, depth),
        compiler_params=pltpu.CompilerParams(vmem_limit_bytes=40 << 20),
        cost_estimate=pl.CostEstimate(
            flops=2 * slots * rows * depth * width, bytes_accessed=20 << 20, transcendentals=0
        ),
    )(near, far, act)


def ffn_up_kernel(tokens, pre_grad, up_grad):
    for tile in range(tokens.shape[1] // 256):
        columns = slice(tile * 256, (tile + 1) * 256)
        up_grad[0, columns] = lax.dot_general(
            tokens[:, columns], pre_grad[0], TN, preferred_element_type=F32
        ).astype(BF)


def ffn_up(tokens, pre_grad):
    slots, rows, width = pre_grad.shape
    depth = tokens.shape[1]
    per_slot = lambda *shape: pl.BlockSpec((1,) + shape, lambda e: (e, 0, 0))
    return pl.pallas_call(
        ffn_up_kernel,
        grid=(slots,),
        out_shape=jax.ShapeDtypeStruct((slots, depth, width), BF),
        in_specs=[
            pl.BlockSpec((rows, depth), lambda e: (0, 0), pipeline_mode=pl.Buffered(1)),
            per_slot(rows, width),
        ],
        out_specs=per_slot(depth, width),
        compiler_params=pltpu.CompilerParams(vmem_limit_bytes=40 << 20),
        cost_estimate=pl.CostEstimate(
            flops=2 * slots * rows * depth * width, bytes_accessed=35 << 20, transcendentals=0
        ),
    )(tokens, pre_grad)


def ffn_input_kernel(pre_grad, up_own, up_peer, out):
    clear(pl.program_id(0) == 0, out)
    w_up = jnp.concatenate([up_own[0], up_peer[0]], axis=0)
    for tile in range(out.shape[0] // TILE):
        rows = pl.ds(tile * TILE, TILE)
        out[rows] += lax.dot_general(pre_grad[0, rows], w_up, NT, preferred_element_type=F32)


def ffn_input(pre_grad, up_own, up_peer, part, parts):
    slots, rows, width = pre_grad.shape
    half = up_own.shape[1]
    depth = 2 * half
    rows = rows // parts
    return pl.pallas_call(
        ffn_input_kernel,
        grid=(slots,),
        out_shape=jax.ShapeDtypeStruct((rows, depth), F32),
        in_specs=[
            pl.BlockSpec((1, rows, width), lambda e: (e, part, 0)),
            pl.BlockSpec((1, half, width), lambda e: (e, 0, 0)),
            pl.BlockSpec((1, half, width), lambda e: (e, 0, 0)),
        ],
        out_specs=pl.BlockSpec((rows, depth), lambda e: (0, 0)),
        compiler_params=pltpu.CompilerParams(vmem_limit_bytes=40 << 20),
        cost_estimate=pl.CostEstimate(
            flops=2 * slots * rows * depth * width, bytes_accessed=20 << 20, transcendentals=0
        ),
    )(pre_grad, up_own, up_peer)


def join_core(parts):
    size = parts.shape[0] // 2
    return parts[:size] + swap(parts[size:].astype(BF), "col").astype(F32)


def collect_tokens(far, near_of, operand):
    send = flip(join_core(far).astype(BF))
    send, operand = lax.optimization_barrier((send, operand))
    recv = swap(send, "row")
    near, *rest = near_of(operand)
    near, recv = lax.optimization_barrier((near, recv))
    return (join_core(near) + recv.astype(F32), *rest)


def from_sequence(values, r, c):
    half = values.shape[1] // 2
    own, peer = values[:, :half], values[:, half:]
    diag = r == c
    send = jnp.where(diag, peer, own)
    kept = jnp.where(diag, own, peer)
    recv = swap(send, "col")
    whole = order_pair(c == 0, kept, recv, 0)
    moved = lax.ppermute(whole, ("row", "col"), [(1, 2), (2, 1)])
    return jnp.where(diag, whole, moved)


def local(
    layer_input,
    teacher,
    valid_mask,
    routes,
    segments,
    gain_attn,
    gain_ffn,
    w_qkv,
    w_out,
    w_router,
    w_shared_up,
    w_shared_down,
    w_expert_up,
    w_expert_down,
):
    r = lax.axis_index("row")
    c = lax.axis_index("col")
    n_dp = lax.axis_size("dp")
    rows = layer_input.shape[0]
    part = rows // 2
    half = layer_input.shape[1]
    heads = w_qkv.shape[2] // HEAD_DIM
    ff = w_shared_up.shape[2]
    quarter = ff // 2
    slots = E + 1

    seg = lax.dynamic_slice_in_dim(segments, r, 1, 0)[0]
    seg_row, seg_col = seg[None, :], seg[:, None]
    tables = rope_tables(rows)
    w_qkv = w_qkv.swapaxes(0, 1)
    vectors = jnp.concatenate(
        [gain_attn[None], gain_ffn[None], w_router.T.astype(F32), jnp.zeros((6 - E, half), F32)]
    )
    (
        queries, keys_rot, values_low, context_low, normed_attn, x_own, hidden,
        w_qkv_peer, w_out_peer, vec_peer, up_own, tokens, up_peer, down_peer, teacher_pair,
    ) = front(
        layer_input, teacher, w_qkv, w_out, vectors, w_shared_up, w_expert_up, w_shared_down, w_expert_down,
        tables, seg,
    )

    vectors = jnp.concatenate([vectors, vec_peer], axis=1)
    gain_a, gain_f, w_r = vectors[0], vectors[1], vectors[2 : 2 + E].astype(BF).T
    teacher_own = jnp.concatenate([teacher_pair[0], teacher_pair[1]], axis=1).astype(F32)
    valid_other = swap(valid_mask, "col")
    valid_seq = jnp.where(r == c, valid_mask, valid_other).astype(F32)
    valid_own = lax.dynamic_slice_in_dim(valid_seq, c * part, part, 0)
    route_blocks = routes.reshape(2, 2, part, 2)
    route_blocks = jnp.where(r == 0, route_blocks, route_blocks[::-1])
    route_blocks = jnp.where(c == 0, route_blocks, route_blocks[:, ::-1]).reshape(4 * part, 2)
    picks = (route_blocks[:, :, None] == jnp.arange(E, dtype=jnp.int32)[None, None, :]).astype(F32)

    down_own = jnp.concatenate([w_shared_down[None], w_expert_down])
    down_own = lax.dynamic_slice_in_dim(down_own, r * quarter, quarter, 1)

    x_own = jnp.concatenate([x_own[0], x_own[1]], axis=1).astype(F32)
    rstd_attn = lax.rsqrt(jnp.mean(x_own * x_own, axis=1) + 1e-06)

    rstd_ffn = lax.rsqrt(jnp.mean(hidden * hidden, axis=1) + 1e-06)
    normed_low = tokens[0]
    tokens = tokens.reshape(4 * part, D)
    logits = jnp.dot(tokens, w_r, preferred_element_type=F32)
    chosen = jnp.sum(picks * logits[:, None, :], axis=2)
    chosen = chosen - jnp.max(chosen, axis=1, keepdims=True)
    gates = jnp.exp(chosen)
    gates = gates / jnp.sum(gates, axis=1, keepdims=True)
    mixing = jnp.sum(picks * gates[:, :, None], axis=1)
    mix = jnp.concatenate(
        [jnp.ones((4 * part, 1), F32), mixing, jnp.zeros((4 * part, 7 - E), F32)], axis=1
    )
    weights = (up_own, up_peer, down_own, down_peer)
    pre, act, far = ffn_forward(tokens, *weights, mix, 1, 2)

    def near_forward(operand):
        pre, act, near = ffn_forward(operand[0], *weights, mix, 0, 2, operand[1:])
        return near, pre, act

    branch, pre, act = collect_tokens(far, near_forward, (tokens, pre, act))
    output = hidden + branch

    error = output - teacher_own
    loss_part = jnp.sum(valid_own * jnp.sum(error * error, axis=1))
    grad_out = valid_own[:, None] * error

    low_own = grad_out.astype(BF)
    far = swap(flip(low_own), "row")
    near = jnp.concatenate([low_own, swap(low_own, "col")])
    pre_grad, near_sums = ffn_backward(near, pre, down_own, down_peer, mix, 0, 2)
    pre_grad, far = lax.optimization_barrier((pre_grad, far))
    far = jnp.concatenate([far, swap(far, "col")])
    owner_f = quarter // n_dp
    owner_d = half // n_dp
    deep = n_dp // 2
    down_grad = ffn_down(near, far, act)
    down_keep, down_send = x_halves(down_grad.reshape(slots, n_dp, owner_f, D), 1)
    pre_grad, far, down_send = lax.optimization_barrier((pre_grad, far, down_send))
    first_recv = along_dp(down_send[:3], 1)
    second_recv = along_dp(down_send[3:], 1)
    pre_grad, far_sums = ffn_backward(far, pre, down_own, down_peer, mix, 1, 2, (pre_grad,))
    gate_parts = jnp.concatenate([near_sums, far_sums])[:, 1 : E + 1].T.reshape(E, 4, part)
    recv = swap(jnp.stack([gate_parts[:, 1], gate_parts[:, 3]]), "col")
    gate_grad = gate_parts[:, 0] + recv[0] + swap(gate_parts[:, 2] + recv[1], "row")
    up_grad = ffn_up(tokens, pre_grad)
    up_grad = up_grad.reshape(slots, 2, n_dp, owner_d, 2 * quarter)
    up_keep, up_send = x_halves(up_grad[:BESIDE], 2)
    pre_grad, gate_grad, up_send, first_recv = lax.optimization_barrier(
        (pre_grad, gate_grad, up_send, first_recv)
    )
    far = ffn_input(pre_grad, up_own, up_peer, 1, 2)
    (normed_ffn_grad,) = collect_tokens(
        far, lambda operand: (ffn_input(operand, up_own, up_peer, 0, 2),), pre_grad
    )
    mix_own = mixing[:part].T
    centre = jnp.sum(mix_own * gate_grad, axis=0, keepdims=True)
    logit_grad = (mix_own * (gate_grad - centre)).T.astype(BF)
    normed_ffn_grad = normed_ffn_grad + jnp.dot(logit_grad, w_r.T, preferred_element_type=F32)
    router_grad = jnp.dot(normed_low.T, logit_grad, preferred_element_type=F32)
    hidden_back, gain_ffn_grad = norm_backward(hidden, rstd_ffn, gain_f, normed_ffn_grad)
    hidden_grad = grad_out + hidden_back

    low_own = hidden_grad.astype(BF)
    low_seq = order_pair(c == 0, low_own, swap(low_own, "col"), 0)
    w_out_grad = jnp.dot(context_low.T, low_seq, preferred_element_type=F32).astype(BF)
    w_out_full = jnp.concatenate([w_out, w_out_peer], axis=1)
    w_qkv_full = jnp.concatenate([w_qkv, w_qkv_peer], axis=1)
    normed_attn = jnp.concatenate([normed_attn[0], normed_attn[1]], axis=1)
    context_grad = jnp.dot(low_seq, w_out_full.T, preferred_element_type=F32)
    context_grad = context_grad.astype(BF)
    context_grad, second_recv = lax.optimization_barrier((context_grad, second_recv))
    down_recv = jnp.concatenate([first_recv, second_recv])
    down_own_sum, *down_sends = z_blocks(add_low(down_keep, down_recv), 1)
    context_grad, down_sends, up_send = lax.optimization_barrier(
        (context_grad, down_sends, up_send)
    )
    up_recv = along_dp(up_send, 1)
    down_recvs = [along_dp(block, 2 * k + 2) for k, block in enumerate(down_sends)]
    qkv_grad = jnp.concatenate(
        [
            attend_backward(
                queries, keys_rot, values_low, context_grad, tables, seg_row, seg_col, pair, 1
            )
            for pair in range(heads // 2)
        ],
        axis=2,
    )
    qkv_grad, up_recv = lax.optimization_barrier((qkv_grad, up_recv))
    up_own_sum, *up_sends = z_blocks(add_low(up_keep, up_recv), 2)
    qkv_grad, up_sends = lax.optimization_barrier((qkv_grad, up_sends))
    up_recvs = [along_dp(block, 2 * k + 2) for k, block in enumerate(up_sends)]
    w_qkv_grad = jnp.einsum(
        "td,kte->dke", normed_attn, qkv_grad, preferred_element_type=F32
    ).astype(BF)
    back_part = jnp.einsum("kte,kde->td", qkv_grad, w_qkv_full, preferred_element_type=F32)
    back_halves = back_part.reshape(2, part, D)
    back_keep = lax.dynamic_index_in_dim(back_halves, c, 0, keepdims=False)
    back_send = lax.dynamic_index_in_dim(back_halves, 1 - c, 0, keepdims=False)
    normed_attn_grad = back_keep + swap(back_send.astype(BF), "col").astype(F32)
    input_back, gain_attn_grad = norm_backward(x_own, rstd_attn, gain_a, normed_attn_grad)
    input_grad = hidden_grad + input_back

    w_qkv_grad, down_recvs = lax.optimization_barrier((w_qkv_grad, down_recvs))
    down_sum = add_low(down_own_sum, *down_recvs)
    down_peer_sum = swap(down_sum[:, :, half:], "row")
    grad_pair = jnp.concatenate(
        [
            w_qkv_grad.reshape(2, n_dp, owner_d, 3, half),
            w_out_grad.reshape(n_dp, owner_d, 2, half).transpose(2, 0, 1, 3)[:, :, :, None],
        ],
        axis=3,
    ).transpose(0, 1, 3, 2, 4)
    up_pair, attn_piece = dp_reduce(
        up_grad.reshape(slots, 2, deep, 2, owner_d, 2 * quarter),
        grad_pair.reshape(2, deep, 2, 4 * owner_d, half),
    )
    up_pair, attn_piece, up_recvs = lax.optimization_barrier((up_pair, attn_piece, up_recvs))
    up_sum = add_low(up_own_sum, *up_recvs)
    up_peer_sum = swap(up_sum[:, 1], "row")
    attn_piece = attn_piece.reshape(4, owner_d, half)
    down_piece = order_pair(r == 0, down_sum[:, None, :, :half], down_peer_sum[:, None], 1)
    up_pair = jnp.concatenate([jnp.stack([up_sum[:, 0], up_peer_sum]), up_pair], axis=1)
    up_pair = up_pair.reshape(2, slots, owner_d, 2, quarter)
    up_piece = order_pair(r == 0, up_pair[0], up_pair[1], 3)

    small = jnp.concatenate([gain_attn_grad[None], gain_ffn_grad[None], router_grad.T], axis=0)
    small = jnp.where(r == 0, small, flip(small))
    loss_row = jnp.full((1, D), loss_part).at[0, half:].set(jnp.sum(valid_own))
    small = jnp.concatenate([small, loss_row, jnp.zeros((1, D), F32)])
    small = small + swap(small, "row")
    small = small + swap(small, "col")
    plan = [(1, (), owner_d), (3, (0,), owner_f), (3, (1,), owner_f)]
    for e in range(E):
        plan += [(0, (e,), owner_d), (2, (e, 0), owner_f), (2, (e, 1), owner_f)]
    plan += [(4, (), 0), (5, (), 0)]
    up_full, shared_up_full, down_full, shared_down_full, attn_full, small_full = dp_gather(
        (up_piece[1:], up_piece[0], down_piece[1:], down_piece[0], attn_piece, small),
        (
            (E, half, 2, ff),
            (half, 2, ff),
            (E, 2, quarter, half),
            (2, quarter, half),
            (n_dp, 4, owner_d, half),
            (n_dp, E + 4, D),
        ),
        tuple(plan),
    )
    small = jnp.sum(small_full, axis=0)
    count = small[E + 2, half]
    loss = small[E + 2, 0] / (2.0 * count)
    scale = part * 4 * n_dp / count
    small = small[: E + 2] * scale
    attn_full = attn_full.swapaxes(0, 1).reshape(4, half, half).astype(F32) * scale
    small = lax.dynamic_slice_in_dim(small, r * half, half, 1)
    return (
        from_sequence(output, r, c),
        loss,
        from_sequence(input_grad, r, c) * scale,
        small[0],
        small[1],
        attn_full[:3].swapaxes(0, 1),
        attn_full[3],
        small[2:].T,
        shared_up_full.astype(F32) * scale,
        shared_down_full.reshape(ff, half).astype(F32) * scale,
        up_full.astype(F32) * scale,
        down_full.reshape(E, ff, half).astype(F32) * scale,
    )


def solution(mesh):
    return jax.shard_map(
        local,
        mesh=mesh,
        in_specs=(
            P(("dp", "col"), "row"),
            P(("dp", "col"), "row"),
            P(("dp", "col")),
            P("dp", None),
            P("dp", None),
            P("row"),
            P("row"),
            P("row", None, "col"),
            P("col", "row"),
            P("row", None),
            P("row", None, "col"),
            P("col", "row"),
            P(None, "row", None, "col"),
            P(None, "col", "row"),
        ),
        out_specs=(
            P(("dp", "col"), "row"),
            P(),
            P(("dp", "col"), "row"),
            P("row"),
            P("row"),
            P("row", None, "col"),
            P("col", "row"),
            P("row", None),
            P("row", None, "col"),
            P("col", "row"),
            P(None, "row", None, "col"),
            P(None, "col", "row"),
        ),
        check_vma=False,
    )
```
